32 devices in a mesh: seq: 8 (over y, x, core), ctx: 4 (over z).
Axes of the slice: x: 2, y: 2, z: 4, core: 2. Of those that a mesh axis runs over, the one named last changes fastest.
Arguments:
- tokens: bfloat16 [16, 1024, 768], P('seq', 'ctx'), may hold values from -6 to 6
- segments: int32 [16, 1024], P('seq'), may hold values from 0 to 6, as said below
- positions: int32 [16, 1024], P('seq', 'ctx'), may hold values from 0 to 1023, as said below
- w_query: bfloat16 [768, 768], P(('seq', 'ctx')), may hold values from -0.21875 to 0.21875
- w_key: bfloat16 [768, 768], P(('seq', 'ctx')), may hold values from -0.21875 to 0.21875
- w_value: bfloat16 [768, 768], P(('seq', 'ctx')), may hold values from -0.21875 to 0.21875
- w_out: bfloat16 [768, 768], P(('seq', 'ctx')), may hold values from -1.75 to 1.75
- w_gate: bfloat16 [768, 3072], P(('seq', 'ctx')), may hold values from -0.21875 to 0.21875
- w_up: bfloat16 [768, 3072], P(('seq', 'ctx')), may hold values from -0.21875 to 0.21875
- w_down: bfloat16 [3072, 768], P(('seq', 'ctx')), may hold values from -0.109375 to 0.109375
- gain_attn: bfloat16 [768], P(('seq', 'ctx')), may hold values from 0.5 to 1.5
- gain_mlp: bfloat16 [768], P(('seq', 'ctx')), may hold values from 0.5 to 1.5
- cotangent: bfloat16 [16, 1024, 768], P('seq', 'ctx'), may hold values from -6 to 6
Outputs:
- output: bfloat16 [16, 1024, 768], P('seq', 'ctx')
- input_grad: float32 [16, 1024, 768], P('seq', 'ctx')
- grad_query: float32 [768, 768], P(('seq', 'ctx'))
- grad_key: float32 [768, 768], P(('seq', 'ctx'))
- grad_value: float32 [768, 768], P(('seq', 'ctx'))
- grad_out: float32 [768, 768], P(('seq', 'ctx'))
- grad_gate: float32 [768, 3072], P(('seq', 'ctx'))
- grad_up: float32 [768, 3072], P(('seq', 'ctx'))
- grad_down: float32 [3072, 768], P(('seq', 'ctx'))
- grad_gain_attn: float32 [768], P(('seq', 'ctx'))
- grad_gain_mlp: float32 [768], P(('seq', 'ctx'))
The draws below stay inside these ranges and needn't reach their ends.
Inputs may be any that keep to these rules, and one draw needn't show every extreme that they name: `segments`: in each packed sequence the segment numbers start at 0, never fall and rise by one at six places: three among the first 256 tokens and three among the last 256. `positions`: A token's position is its document's first position plus its place in the document; the first document of every packed sequence starts at 0, and every document ends at or below 1023, the last one exactly there.
All inputs are finite; a program needn't handle non-finite values.
Results may differ from the reference program's by a relative error of at most 0.013.
Values may be sent and summed in bfloat16 or wider, within the bound.
No kernel may reach another device: no remote copies, remote signals or barrier semaphores. Data moves between devices by JAX's collectives and lax.ppermute only.
A program may use at most 192 MiB of HBM per device.

```python
import jax
import jax.numpy as jnp
from jax import lax

D = 768
FF = 3072
HEADS = 12
KV_HEADS = 12
HEAD_DIM = 64
LEN = 1024
SEQS = 16
SPAN = 256
KV_WIDTH = 768


def packing(key):
    row_keys = jax.random.split(key, SEQS)

    def one_row(row_key):
        head_key, tail_key, offset_key = jax.random.split(row_key, 3)
        head_cuts = jax.random.permutation(head_key, SPAN - 1)[:3] + 1
        tail_cuts = jax.random.permutation(tail_key, SPAN - 1)[:3] + (LEN - SPAN + 1)
        cut_points = jnp.concatenate([head_cuts, tail_cuts]).astype(jnp.int32)
        token_ids = jnp.arange(LEN, dtype=jnp.int32)
        is_start = jnp.any(token_ids[:, None] == cut_points[None, :], axis=1)
        segment_ids = jnp.cumsum(is_start.astype(jnp.int32)).astype(jnp.int32)
        doc_first = lax.cummax(jnp.where(is_start, token_ids, 0), axis=0)
        doc_ids = jnp.arange(7, dtype=jnp.int32)
        doc_length = jnp.sum((segment_ids[None, :] == doc_ids[:, None]).astype(jnp.int32), axis=1).astype(jnp.int32)
        room = (LEN - doc_length + 1).astype(jnp.int32)
        offsets = jax.random.randint(offset_key, (7,), 0, room, dtype=jnp.int32)
        offsets = jnp.where(doc_ids == 0, 0, offsets)
        offsets = jnp.where(doc_ids == 6, LEN - doc_length, offsets).astype(jnp.int32)
        position_ids = (offsets[segment_ids] + token_ids - doc_first).astype(jnp.int32)
        return (segment_ids, position_ids)
    return jax.vmap(one_row)(row_keys)


def draw_segments(key, part):
    shared = packing(key)
    return shared[0]


def draw_positions(key, part):
    shared = packing(key)
    return shared[1]


def steps_of(own_key, dims, cuts, least, high):
    loudness = 1.0
    for position, blocks in cuts:
        steps = jax.random.uniform(jax.random.fold_in(jax.random.fold_in(own_key, 6), position), (blocks,), jnp.float32, least / len(cuts), high / len(cuts))
        loudness = loudness * jnp.repeat(jnp.exp(steps), dims[position] // blocks).reshape((-1,) + (1,) * (len(dims) - 1 - position))
    return loudness


def bell_draw(stream_key, dims, spread, limit, cuts=(), kind=jnp.bfloat16):
    factor_of = steps_of(stream_key, dims, cuts, -0.22, 0.18) if cuts else 1.0
    values = jax.random.normal(stream_key, dims, jnp.float32) * spread * factor_of
    return jnp.minimum(jnp.maximum(values, -limit), limit).astype(kind)


def setup_inputs(seed: int = 0) -> dict:
    streams_of = jax.random.split(jax.random.key(seed), 14)
    return {
        "tokens": bell_draw(streams_of[0], (SEQS, LEN, D), 1.0, 6.0, ((0, 8), (1, 4))),
        "segments": draw_segments(jax.random.fold_in(streams_of[13], 71), 0),
        "positions": draw_positions(jax.random.fold_in(streams_of[13], 71), 0),
        "w_query": bell_draw(streams_of[3], (D, D), D ** -0.5, 0.21875, ((0, 32),)),
        "w_key": bell_draw(streams_of[4], (D, KV_WIDTH), D ** -0.5, 0.21875, ((0, 32),)),
        "w_value": bell_draw(streams_of[5], (D, KV_WIDTH), D ** -0.5, 0.21875, ((0, 32),)),
        "w_out": bell_draw(streams_of[6], (D, D), (D // 64) ** -0.5, 1.75, ((0, 32),)),
        "w_gate": bell_draw(streams_of[7], (D, FF), D ** -0.5, 0.21875, ((0, 32),)),
        "w_up": bell_draw(streams_of[8], (D, FF), D ** -0.5, 0.21875, ((0, 32),)),
        "w_down": bell_draw(streams_of[9], (FF, D), FF ** -0.5, 0.109375, ((0, 32),)),
        "gain_attn": jnp.clip(1.0 + 0.1 * jax.random.normal(streams_of[10], (D,), jnp.float32), 0.5, 1.5).astype(jnp.bfloat16),
        "gain_mlp": jnp.clip(1.0 + 0.1 * jax.random.normal(streams_of[11], (D,), jnp.float32), 0.5, 1.5).astype(jnp.bfloat16),
        "cotangent": bell_draw(streams_of[12], (SEQS, LEN, D), 1.0, 6.0, ((0, 8), (1, 4))),
    }


@jax.custom_vjp
def low(v):
    return lax.optimization_barrier(v.astype(jnp.bfloat16)).astype(jnp.float32)

@jax.custom_vjp
def low_back(v):
    return v

def low_keep(v):
    return (low(v), None)

def low_pass(kept, grad):
    return (grad,)

def back_keep(v):
    return (v, None)

def back_low(kept, grad):
    return (low(grad),)
low.defvjp(low_keep, low_pass)
low_back.defvjp(back_keep, back_low)
epsilon = 1e-05

def hdot(left, right):
    return jnp.dot(left, right, precision=lax.Precision.HIGHEST, preferred_element_type=jnp.float32)

def rms_scale(values_in, gain_in):
    return values_in * lax.rsqrt(lax.optimization_barrier(jnp.mean(values_in * values_in, axis=-1, keepdims=True)) + epsilon) * gain_in

def angle_tables(position_ids, head_size):
    half_dim = head_size // 2
    frequency = 10000.0 ** (-(jnp.arange(half_dim, dtype=jnp.float32) * 2.0 / head_size))
    angles = position_ids.astype(jnp.float32)[:, None] * frequency[None, :]
    angles = jnp.concatenate([angles, angles], axis=-1)
    return (jnp.cos(angles), jnp.sin(angles))

def rotate(values_in, cosine, sine_table):
    half_dim = values_in.shape[-1] // 2
    turned = jnp.concatenate([-values_in[..., half_dim:], values_in[..., :half_dim]], axis=-1)
    return values_in * cosine[:, None, :] + turned * sine_table[:, None, :]

def layer_row(x_row, seg_row, pos_row, w_query, w_key, w_value, w_out, w_gate, w_up, w_down, gain_attn, gain_mlp):
    seq_len = x_row.shape[0]
    head_group = HEADS // KV_HEADS
    score_scale = HEAD_DIM ** (-0.5)
    cosine, sine_table = angle_tables(pos_row, HEAD_DIM)
    normed = low(rms_scale(x_row, gain_attn))
    query_rot = low(rotate(low_back(hdot(normed, w_query)).reshape(seq_len, HEADS, HEAD_DIM), cosine, sine_table))
    key_rot = low(rotate(low_back(hdot(normed, w_key)).reshape(seq_len, KV_HEADS, HEAD_DIM), cosine, sine_table))
    value_low = low(low_back(hdot(normed, w_value))).reshape(seq_len, KV_HEADS, HEAD_DIM)
    queries = query_rot.reshape(seq_len, KV_HEADS, head_group, HEAD_DIM)
    raw_scores = jnp.einsum('qkgd,skd->kgqs', queries, key_rot, precision=lax.Precision.HIGHEST)
    token_ids = jnp.arange(seq_len, dtype=jnp.int32)
    allowed = (token_ids[None, :] <= token_ids[:, None]) & (seg_row[:, None] == seg_row[None, :])
    logits = jnp.where(allowed[None, None], low_back(raw_scores) * score_scale, -1e+30)
    row_max = lax.optimization_barrier(jnp.max(logits, axis=-1, keepdims=True))
    shifted_exp = jnp.exp(logits - row_max)
    probs = low(shifted_exp / lax.optimization_barrier(jnp.sum(shifted_exp, axis=-1, keepdims=True)))
    mixed_heads = jnp.einsum('kgqs,skd->qkgd', probs, value_low, precision=lax.Precision.HIGHEST)
    attended = low(low_back(mixed_heads.reshape(seq_len, HEADS * HEAD_DIM)))
    hidden_state = x_row + low_back(hdot(attended, w_out))
    normed_two = low(rms_scale(hidden_state, gain_mlp))
    gate_proj = low_back(hdot(normed_two, w_gate))
    up_proj = low_back(hdot(normed_two, w_up))
    activated = low(jax.nn.silu(gate_proj) * up_proj)
    return hidden_state + low_back(hdot(activated, w_down))

def reference(tokens, segments, positions, w_query, w_key, w_value, w_out, w_gate, w_up, w_down, gain_attn, gain_mlp, cotangent):
    row_layer = jax.checkpoint(layer_row)

    def whole_layer(inputs, f_query, f_key, f_value, f_out, f_gate, f_up, f_down, f_gain_one, f_gain_two):

        def scan_step(state_in, pieces):
            x_row, seg_row, pos_row = pieces
            return (state_in, row_layer(x_row, seg_row, pos_row, f_query, f_key, f_value, f_out, f_gate, f_up, f_down, f_gain_one, f_gain_two))
        unused, outputs = lax.scan(scan_step, None, (inputs, segments, positions))
        return outputs
    outputs, pullback = jax.vjp(whole_layer, tokens.astype(jnp.float32), w_query.astype(jnp.float32), w_key.astype(jnp.float32), w_value.astype(jnp.float32), w_out.astype(jnp.float32), w_gate.astype(jnp.float32), w_up.astype(jnp.float32), w_down.astype(jnp.float32), gain_attn.astype(jnp.float32), gain_mlp.astype(jnp.float32))
    grads = pullback(cotangent.astype(jnp.float32))
    return (outputs.astype(jnp.bfloat16), grads[0], grads[1], grads[2], grads[3], grads[4], grads[5], grads[6], grads[7], grads[8], grads[9])
```

```python
import functools

import jax
import jax.numpy as jnp
from jax import lax
from jax.experimental import pallas as pl
from jax.experimental.pallas import tpu as pltpu
from jax.sharding import PartitionSpec as P

HEADS = 12
KV_HEADS = 12
HEAD_DIM = 64
VMEM = 56 << 20


epsilon = 1e-05


def shortened(value):
    return jax.tree.map(lambda a: a.astype(jnp.bfloat16) if a.dtype == jnp.float32 else a, value)


def rms_scale(values_in, gain_in):
    return (
        values_in
        * lax.rsqrt(jnp.mean(values_in * values_in, axis=-1, keepdims=True) + epsilon)
        * gain_in
    )


def angle_tables(position_ids, head_size):
    half_dim = head_size // 2
    frequency = 10000.0 ** (-(jnp.arange(half_dim, dtype=jnp.float32) * 2.0 / head_size))
    angles = position_ids.astype(jnp.float32)[:, None] * frequency[None, :]
    angles = jnp.concatenate([angles, angles], axis=-1)
    return (jnp.cos(angles), jnp.sin(angles))


def rotate(values_in, cosine, sine_table):
    half_dim = values_in.shape[-1] // 2
    turned = jnp.concatenate([-values_in[..., half_dim:], values_in[..., :half_dim]], axis=-1)
    return values_in * cosine[:, None, :] + turned * sine_table[:, None, :]


def unrotate(grad_in, cosine, sine_table):
    half_dim = grad_in.shape[-1] // 2
    scaled = grad_in * sine_table[:, None, :]
    turned = jnp.concatenate([scaled[..., half_dim:], -scaled[..., :half_dim]], axis=-1)
    return grad_in * cosine[:, None, :] + turned


def gather_flat(weight_set):
    return jax.tree.map(
        lambda part, own: part.astype(own.dtype),
        lax.all_gather(shortened(weight_set), ("seq", "ctx"), axis=0, tiled=True),
        weight_set,
    )


def fetch_weights(weight_set):
    return (gather_flat(weight_set), weight_set)


def fetch_again(kept_set):
    return gather_flat(kept_set)


def reduce_grads(grad_set):
    return lax.psum_scatter(grad_set, ("seq", "ctx"), scatter_dimension=0, tiled=True)


def on_device(
    tokens,
    segments,
    positions,
    w_query,
    w_key,
    w_value,
    w_out,
    w_gate,
    w_up,
    w_down,
    gain_attn,
    gain_mlp,
    cotangent,
):
    seq_count, local_len, model_width = tokens.shape
    seq_len = segments.shape[1]
    row_count = seq_count * local_len
    head_group = HEADS // KV_HEADS
    kv_width = KV_HEADS * HEAD_DIM
    score_scale = HEAD_DIM ** (-0.5)
    first_token = lax.axis_index("ctx") * local_len
    own_tokens = first_token + jnp.arange(local_len, dtype=jnp.int32)
    all_tokens = jnp.arange(seq_len, dtype=jnp.int32)
    causal = all_tokens[None, :] <= own_tokens[:, None]
    inputs = tokens.reshape(row_count, model_width).astype(jnp.float32)
    cosine, sine_table = angle_tables(positions.reshape(row_count), HEAD_DIM)
    attn_full, attn_kept = fetch_weights((w_query, w_key, w_value, w_out, gain_attn))
    full_query, full_key, full_value, full_out, full_gain_one = attn_full
    normed = rms_scale(inputs, full_gain_one.astype(jnp.float32)).astype(jnp.bfloat16)
    query_proj = jnp.dot(normed, full_query, preferred_element_type=jnp.float32)
    key_proj = jnp.dot(normed, full_key, preferred_element_type=jnp.float32)
    value_proj = jnp.dot(normed, full_value, preferred_element_type=jnp.float32)
    query_rot = rotate(query_proj.reshape(row_count, HEADS, HEAD_DIM), cosine, sine_table).astype(
        jnp.bfloat16
    )
    key_rot = rotate(key_proj.reshape(row_count, KV_HEADS, HEAD_DIM), cosine, sine_table).astype(
        jnp.bfloat16
    )
    value_low = value_proj.astype(jnp.bfloat16)
    keys_all, values_all = (
        lax.all_gather(key_rot.reshape(seq_count, local_len, kv_width), "ctx", axis=1, tiled=True),
        lax.all_gather(
            value_low.reshape(seq_count, local_len, kv_width), "ctx", axis=1, tiled=True
        ),
    )
    queries = query_rot.reshape(seq_count, local_len, KV_HEADS, head_group, HEAD_DIM)

    def scores_of(q_seq, k_seq, seg_seq):
        own_seg = lax.dynamic_slice_in_dim(seg_seq, first_token, local_len)
        allowed = causal & (own_seg[:, None] == seg_seq[None, :])
        k_heads = k_seq.reshape(seq_len, KV_HEADS, HEAD_DIM)
        raw_scores = jnp.einsum(
            "qkgd,skd->kgqs", q_seq, k_heads, preferred_element_type=jnp.float32
        )
        return jnp.where(allowed[None, None], raw_scores * score_scale, -1e30)

    def attend(pieces):
        q_seq, k_seq, v_seq, seg_seq = pieces
        logits = scores_of(q_seq, k_seq, seg_seq)
        row_max = jnp.max(logits, axis=-1, keepdims=True)
        shifted_exp = jnp.exp(logits - row_max)
        row_sum = jnp.sum(shifted_exp, axis=-1, keepdims=True)
        probs_low = (shifted_exp / row_sum).astype(jnp.bfloat16)
        mixed_heads = jnp.einsum(
            "kgqs,skd->qkgd",
            probs_low,
            v_seq.reshape(seq_len, KV_HEADS, HEAD_DIM),
            preferred_element_type=jnp.float32,
        )
        return (
            mixed_heads.astype(jnp.bfloat16).reshape(local_len, model_width),
            (row_max + jnp.log(row_sum))[..., 0],
        )

    attended, log_totals = lax.map(attend, (queries, keys_all, values_all, segments))
    attended = attended.reshape(row_count, model_width)
    hidden_state = inputs + jnp.dot(attended, full_out, preferred_element_type=jnp.float32)
    mlp_full, mlp_kept = fetch_weights((w_gate, w_up, w_down, gain_mlp))
    full_gate, full_up, full_down, full_gain_two = mlp_full
    normed_two = rms_scale(hidden_state, full_gain_two.astype(jnp.float32)).astype(jnp.bfloat16)
    gate_proj = jnp.dot(normed_two, full_gate, preferred_element_type=jnp.float32)
    up_proj = jnp.dot(normed_two, full_up, preferred_element_type=jnp.float32)
    activated = (jax.nn.silu(gate_proj) * up_proj).astype(jnp.bfloat16)
    final_state = hidden_state + jnp.dot(activated, full_down, preferred_element_type=jnp.float32)
    output = final_state.astype(jnp.bfloat16).reshape(seq_count, local_len, model_width)
    out_grad = cotangent.reshape(row_count, model_width)
    again_gate, again_up, again_down, again_gain_two = fetch_again(mlp_kept)
    grad_down = jnp.einsum("tf,td->fd", activated, out_grad, preferred_element_type=jnp.float32)
    d_activated = jnp.einsum("td,fd->tf", out_grad, again_down, preferred_element_type=jnp.float32)

    def swiglu(gate_in, up_in):
        return jax.nn.silu(gate_in) * up_in

    unused_mlp, swiglu_back = jax.vjp(swiglu, gate_proj, up_proj)
    d_gate, d_up = swiglu_back(d_activated)
    d_gate = d_gate.astype(jnp.bfloat16)
    d_up = d_up.astype(jnp.bfloat16)
    grad_gate = jnp.einsum("td,tf->df", normed_two, d_gate, preferred_element_type=jnp.float32)
    grad_up = jnp.einsum("td,tf->df", normed_two, d_up, preferred_element_type=jnp.float32)
    d_normed_two = jnp.einsum(
        "tf,df->td", d_gate, again_gate, preferred_element_type=jnp.float32
    ) + jnp.einsum("tf,df->td", d_up, again_up, preferred_element_type=jnp.float32)
    unused_norm, norm_two_back = jax.vjp(
        rms_scale, hidden_state, again_gain_two.astype(jnp.float32)
    )
    d_hidden, grad_gain_mlp = norm_two_back(d_normed_two)
    mlp_sums = reduce_grads((grad_gate, grad_up, grad_down, grad_gain_mlp))
    d_hidden = d_hidden + out_grad.astype(jnp.float32)
    d_branch = d_hidden.astype(jnp.bfloat16)
    again_query, again_key, again_value, again_out, again_gain_one = fetch_again(attn_kept)
    grad_out = jnp.einsum("td,te->de", attended, d_branch, preferred_element_type=jnp.float32)
    d_attended = jnp.einsum(
        "te,de->td", d_branch, again_out, preferred_element_type=jnp.float32
    ).astype(jnp.bfloat16)
    d_heads = d_attended.reshape(seq_count, local_len, KV_HEADS, head_group, HEAD_DIM)

    def attend_back(pieces):
        q_seq, k_seq, v_seq, seg_seq, lse_seq, do_seq = pieces
        logits = scores_of(q_seq, k_seq, seg_seq)
        probs = jnp.exp(logits - lse_seq[..., None])
        probs_low = probs.astype(jnp.bfloat16)
        v_heads = v_seq.reshape(seq_len, KV_HEADS, HEAD_DIM)
        d_probs = jnp.einsum("qkgd,skd->kgqs", do_seq, v_heads, preferred_element_type=jnp.float32)
        d_value = jnp.einsum(
            "kgqs,qkgd->skd", probs_low, do_seq, preferred_element_type=jnp.float32
        )
        row_dot = jnp.sum(probs * d_probs, axis=-1, keepdims=True)
        d_scores = (probs * (d_probs - row_dot) * score_scale).astype(jnp.bfloat16)
        d_query = jnp.einsum(
            "kgqs,skd->qkgd",
            d_scores,
            k_seq.reshape(seq_len, KV_HEADS, HEAD_DIM),
            preferred_element_type=jnp.float32,
        )
        d_key = jnp.einsum("kgqs,qkgd->skd", d_scores, q_seq, preferred_element_type=jnp.float32)
        return (
            d_query.reshape(local_len, HEADS, HEAD_DIM),
            d_key.reshape(seq_len, kv_width),
            d_value.reshape(seq_len, kv_width),
        )

    d_query_all, d_key_part, d_value_part = lax.map(
        attend_back, (queries, keys_all, values_all, segments, log_totals, d_heads)
    )
    d_key_own, d_value_own = (
        lax.psum_scatter(d_key_part, "ctx", scatter_dimension=1, tiled=True),
        lax.psum_scatter(d_value_part, "ctx", scatter_dimension=1, tiled=True),
    )
    d_query_low = (
        unrotate(d_query_all.reshape(row_count, HEADS, HEAD_DIM), cosine, sine_table)
        .astype(jnp.bfloat16)
        .reshape(row_count, model_width)
    )
    d_key_low = (
        unrotate(d_key_own.reshape(row_count, KV_HEADS, HEAD_DIM), cosine, sine_table)
        .astype(jnp.bfloat16)
        .reshape(row_count, kv_width)
    )
    d_value_low = d_value_own.reshape(row_count, kv_width).astype(jnp.bfloat16)
    grad_query = jnp.einsum("td,te->de", normed, d_query_low, preferred_element_type=jnp.float32)
    grad_key = jnp.einsum("td,te->de", normed, d_key_low, preferred_element_type=jnp.float32)
    grad_value = jnp.einsum("td,te->de", normed, d_value_low, preferred_element_type=jnp.float32)
    d_normed = jnp.einsum("te,de->td", d_query_low, again_query, preferred_element_type=jnp.float32)
    d_normed = d_normed + jnp.einsum(
        "te,de->td", d_key_low, again_key, preferred_element_type=jnp.float32
    )
    d_normed = d_normed + jnp.einsum(
        "te,de->td", d_value_low, again_value, preferred_element_type=jnp.float32
    )
    unused_first, norm_one_back = jax.vjp(rms_scale, inputs, again_gain_one.astype(jnp.float32))
    d_inputs, grad_gain_attn = norm_one_back(d_normed)
    attn_sums = reduce_grads((grad_query, grad_key, grad_value, grad_out, grad_gain_attn))
    input_grad = (d_hidden + d_inputs).reshape(seq_count, local_len, model_width)
    return (
        output,
        input_grad,
        attn_sums[0],
        attn_sums[1],
        attn_sums[2],
        attn_sums[3],
        mlp_sums[0],
        mlp_sums[1],
        mlp_sums[2],
        attn_sums[4],
        mlp_sums[3],
    )


EPS = epsilon
NEG = -1e30


def dot32(left, right, dims=((1,), (0,))):
    return lax.dot_general(left, right, (dims, ((), ())), preferred_element_type=jnp.float32)


NT = ((1,), (1,))
TN = ((0,), (0,))


def lane_mask(rows):
    return lax.broadcasted_iota(jnp.int32, (rows, 128), 1) < HEAD_DIM


def swap_halves(u):
    half = HEAD_DIM // 2
    lanes = lax.broadcasted_iota(jnp.int32, u.shape, 1) % HEAD_DIM
    return jnp.where(lanes < half, pltpu.roll(u, 128 - half, 1), pltpu.roll(u, half, 1))


def allowed_pairs(seg_col, seg_row, first, rows, keys):
    q_ids = lax.broadcasted_iota(jnp.int32, (rows, keys), 0) + first
    k_ids = lax.broadcasted_iota(jnp.int32, (rows, keys), 1)
    return (k_ids <= q_ids) & (seg_col == seg_row)


def attend_kernel(block, q_ref, k_ref, v_ref, seg_col_ref, seg_row_ref, o_ref, lse_ref):
    length = q_ref.shape[0]
    first_head = lane_mask(block)
    for step in range(length // block):
        rows = slice(step * block, (step + 1) * block)
        keys = (step + 1) * block
        allowed = allowed_pairs(
            seg_col_ref[rows, :], seg_row_ref[:, :keys], step * block, block, keys
        )
        q_pair = q_ref[rows, :]
        k_pair = k_ref[:keys, :]
        v_pair = v_ref[:keys, :]
        outs, totals = [], []
        for head in range(2):
            mine = first_head if head == 0 else jnp.logical_not(first_head)
            q_head = jnp.where(mine, q_pair, jnp.zeros_like(q_pair))
            z = jnp.where(allowed, dot32(q_head, k_pair, NT), NEG)
            top = jnp.max(z, axis=-1, keepdims=True)
            e = jnp.exp(z - top)
            total = jnp.sum(e, axis=-1, keepdims=True)
            p = (e * (1.0 / total)).astype(jnp.bfloat16)
            outs.append(dot32(p, v_pair))
            totals.append(top + jnp.log(total))
        o_ref[rows, :] = jnp.where(first_head, outs[0], outs[1]).astype(o_ref.dtype)
        lse_ref[rows, :] = jnp.where(first_head, totals[0], totals[1])


def attend_back_kernel(
    block, q_ref, k_ref, v_ref, do_ref, lse_ref, cos_ref, sin_ref, seg_col_ref, seg_row_ref,
    dq_ref, dk_ref, dv_ref, dk_sum, dv_sum,
):
    length = q_ref.shape[0]
    first_head = lane_mask(block)
    for step in range(length // block):
        rows = slice(step * block, (step + 1) * block)
        keys = (step + 1) * block
        allowed = allowed_pairs(
            seg_col_ref[rows, :], seg_row_ref[:, :keys], step * block, block, keys
        )
        q_pair = q_ref[rows, :]
        k_pair = k_ref[:keys, :]
        v_pair = v_ref[:keys, :]
        do_pair = do_ref[rows, :]
        dq_heads = []
        dk_step = dv_step = None
        for head in range(2):
            mine = first_head if head == 0 else jnp.logical_not(first_head)
            q_head = jnp.where(mine, q_pair, jnp.zeros_like(q_pair))
            do_head = jnp.where(mine, do_pair, jnp.zeros_like(do_pair))
            lse = lse_ref[rows, head * HEAD_DIM : head * HEAD_DIM + 1]
            z = jnp.where(allowed, dot32(q_head, k_pair, NT), NEG)
            p = jnp.exp(z - lse)
            dp = dot32(do_head, v_pair, NT)
            dv_head = dot32(p.astype(jnp.bfloat16), do_head, TN)
            row_dot = jnp.sum(p * dp, axis=-1, keepdims=True)
            ds = (p * (dp - row_dot)).astype(jnp.bfloat16)
            dq_heads.append(dot32(ds, k_pair))
            dk_head = dot32(ds, q_head, TN)
            dk_step = dk_head if dk_step is None else dk_step + dk_head
            dv_step = dv_head if dv_step is None else dv_step + dv_head
        dq = jnp.where(first_head, dq_heads[0], dq_heads[1]) * (HEAD_DIM**-0.5)
        dq = dq * cos_ref[rows, :] - swap_halves(dq) * sin_ref[rows, :]
        dq_ref[rows, :] = dq.astype(dq_ref.dtype)
        last = slice(step * block, keys)
        if step > 0:
            dk_sum[: step * block, :] += dk_step[: step * block]
            dv_sum[: step * block, :] += dv_step[: step * block]
        dk_sum[last, :] = dk_step[step * block :]
        dv_sum[last, :] = dv_step[step * block :]
    dk = dk_sum[...]
    dk = dk * cos_ref[...] - swap_halves(dk) * sin_ref[...]
    dk_ref[...] = dk.astype(dk_ref.dtype)
    dv_ref[...] = dv_sum[...].astype(dv_ref.dtype)


def qkv_kernel(x_ref, gain_ref, w_ref, cos_ref, sin_ref, a_ref, q_ref, k_ref, v_ref):
    x = x_ref[...].astype(jnp.float32)
    r = lax.rsqrt(jnp.mean(x * x, axis=-1, keepdims=True) + EPS)
    a = (x * r * gain_ref[...]).astype(jnp.bfloat16)
    a_ref[...] = a
    u = dot32(a, w_ref[...])
    width = q_ref.shape[1]
    cos, sin = cos_ref[...], sin_ref[...]
    for at in range(0, width, 128):
        q = u[:, at : at + 128]
        q = (q * cos + swap_halves(q) * sin) * (HEAD_DIM**-0.5)
        q_ref[:, at : at + 128] = q.astype(jnp.bfloat16)
        k = u[:, width + at : width + at + 128]
        k = k * cos + swap_halves(k) * sin
        k_ref[:, at : at + 128] = k.astype(jnp.bfloat16)
    v_ref[...] = u[:, 2 * width :].astype(jnp.bfloat16)


def whole(shape):
    return pl.BlockSpec(shape, lambda i: (0,) * len(shape))


def row_block(rows, width):
    return pl.BlockSpec((rows, width), lambda i: (i, 0))


def lane_block(length):
    return pl.BlockSpec((length, 128), lambda i: (0, i))


def project(x, gain, w, cos, sin):
    length, model = x.shape
    width = w.shape[1] // 3
    rows = 256
    low = lambda n: jax.ShapeDtypeStruct((length, n), jnp.bfloat16)
    return pl.pallas_call(
        qkv_kernel,
        grid=(length // rows,),
        in_specs=[
            row_block(rows, model), whole((1, model)), whole(w.shape),
            row_block(rows, 128), row_block(rows, 128),
        ],
        out_specs=[row_block(rows, model)] + [row_block(rows, width)] * 3,
        out_shape=[low(model), low(width), low(width), low(width)],
        compiler_params=pltpu.CompilerParams(vmem_limit_bytes=VMEM),
        cost_estimate=pl.CostEstimate(
            flops=2 * length * model * 3 * width, bytes_accessed=8 << 20, transcendentals=0
        ),
        name="project",
    )(x, gain, w, cos, sin)


def attend(q, k, v, seg_col, seg_row):
    length, width = q.shape
    return pl.pallas_call(
        functools.partial(attend_kernel, 256),
        grid=(width // 128,),
        in_specs=[lane_block(length)] * 3 + [whole((length, 1)), whole((1, length))],
        out_specs=[lane_block(length)] * 2,
        out_shape=[
            jax.ShapeDtypeStruct((length, width), jnp.bfloat16),
            jax.ShapeDtypeStruct((length, width), jnp.float32),
        ],
        compiler_params=pltpu.CompilerParams(vmem_limit_bytes=VMEM),
        cost_estimate=pl.CostEstimate(
            flops=8 * length * length * width, bytes_accessed=6 << 20,
            transcendentals=length * length * width // 64,
        ),
        name="attend",
    )(q, k, v, seg_col, seg_row)


def attend_back(q, k, v, do, lse, cos, sin, seg_col, seg_row):
    length, width = q.shape
    return pl.pallas_call(
        functools.partial(attend_back_kernel, 256),
        grid=(width // 128,),
        in_specs=[lane_block(length)] * 5
        + [whole((length, 128))] * 2
        + [whole((length, 1)), whole((1, length))],
        out_specs=[lane_block(length)] * 3,
        out_shape=[jax.ShapeDtypeStruct((length, width), jnp.bfloat16)] * 3,
        scratch_shapes=[pltpu.VMEM((length, 128), jnp.float32)] * 2,
        compiler_params=pltpu.CompilerParams(vmem_limit_bytes=VMEM),
        cost_estimate=pl.CostEstimate(
            flops=20 * length * length * width, bytes_accessed=10 << 20,
            transcendentals=length * length * width // 64,
        ),
        name="attend_back",
    )(q, k, v, do, lse, cos, sin, seg_col, seg_row)


class Lines:
    def __init__(self, seq_size, ctx_size):
        self.seq_size, self.ctx_size = seq_size, ctx_size
        s = lax.axis_index("seq")
        self.z = lax.axis_index("ctx")
        self.core, self.x, self.y = s % 2, (s // 2) % 2, s // 4

    def flip(self, v, bit):
        return lax.ppermute(v, "seq", [(s, s ^ bit) for s in range(self.seq_size)])

    def shift(self, v, by):
        n = self.ctx_size
        return lax.ppermute(v, "ctx", [(z, (z + by) % n) for z in range(n)])

    def ordered(self, own, other, bit, axis):
        first = jnp.where(bit == 0, own, other)
        second = jnp.where(bit == 0, other, own)
        return jnp.stack([first, second], axis=axis)

    def rolled(self, pieces, start):
        doubled = jnp.stack(list(pieces) + list(pieces)[:-1])
        return lax.dynamic_slice_in_dim(doubled, start, len(pieces), axis=0)

    def pick(self, v, at, axis):
        return lax.dynamic_index_in_dim(v, at, axis, keepdims=False)

    def gather(self, piece, x_first, z_axis):
        n = self.ctx_size
        came = [piece] + [self.shift(piece, k) for k in range(1, n)]
        by_offset = [came[(n - j) % n] for j in range(n)]
        line = self.rolled(by_offset, (n - self.z) % n)
        line = jnp.moveaxis(line, 0, z_axis)
        if x_first:
            line = self.ordered(line, self.flip(line, 2), self.x, 0)
            return self.ordered(line, self.flip(line, 4), self.y, 0)
        line = self.ordered(line, self.flip(line, 4), self.y, 0)
        return self.ordered(line, self.flip(line, 2), self.x, 1)

    def scatter(self, grad, x_first, z_axis):
        def halve(v, axis, bit, step, last=False):
            away = self.pick(v, 1 - bit, axis)
            kept = self.pick(v, bit, axis)
            total = kept.astype(jnp.float32) + self.flip(away, step).astype(jnp.float32)
            return total.astype(jnp.bfloat16)

        if x_first:
            grad = halve(grad, 1, self.x, 2)
            grad = halve(grad, 0, self.y, 4)
        else:
            grad = halve(grad, 0, self.y, 4)
            grad = halve(grad, 0, self.x, 2)
        n = self.ctx_size
        total = self.pick(grad, self.z, z_axis).astype(jnp.float32)
        for k in range(1, n):
            came = self.shift(self.pick(grad, (self.z + k) % n, z_axis), k)
            total = total + came.astype(jnp.float32)
        return total

    def _rounds(self):
        n_line, n_seqs = self.ctx_size, self.ctx_size // 2
        rounds = []
        for r in range(n_line):
            pairs = []
            for s in range(self.seq_size):
                for z in range(n_line):
                    k = (z - r) % n_line
                    chip = n_seqs * (s % 2) + k // 2
                    pairs.append((s * n_line + z, (s - s % 2 + k % 2) * n_line + chip))
            rounds.append(pairs)
        return rounds

    def _first(self):
        return 2 * (self.z % (self.ctx_size // 2)) + self.core

    def to_chip(self, v):
        n = self.ctx_size
        pieces = v.reshape((n, v.shape[1] // 2) + v.shape[2:])
        came = [
            lax.ppermute(self.pick(pieces, (self.z - r) % n, 0), ("seq", "ctx"), pairs)
            for r, pairs in enumerate(self._rounds())
        ]
        return self.rolled(came, (n - self._first()) % n)

    def from_chip(self, half):
        n = self.ctx_size
        came = [
            lax.ppermute(
                self.pick(half, (r + self._first()) % n, 0),
                ("seq", "ctx"),
                [(work, hold) for hold, work in pairs],
            )
            for r, pairs in enumerate(self._rounds())
        ]
        pieces = self.rolled([came[(n - j) % n] for j in range(n)], (n - self.z) % n)
        return pieces.reshape((n // 2, 2 * half.shape[1]) + half.shape[2:])

    def both_halves(self, half):
        return self.ordered(half, self.flip(half, 1), self.core, 1)

    def sum_cores(self, v):
        return self.pick(v, self.core, 1) + self.flip(self.pick(v, 1 - self.core, 1), 1)

    def sum_all(self, v):
        v = v + self.flip(v, 1)
        v = v + self.flip(v, 2)
        v = v + self.flip(v, 4)
        return v + sum(self.shift(v, k) for k in range(1, self.ctx_size))


def sequence_per_chip(seq_size, ctx_size):
    def on_device(
        tokens, segments, positions,
        w_query, w_key, w_value, w_out, w_gate, w_up, w_down,
        gain_attn, gain_mlp, cotangent,
    ):
        lines = Lines(seq_size, ctx_size)
        core = lines.core
        seq_len = segments.shape[1]
        model = tokens.shape[2]
        span = seq_len // (2 * ctx_size)
        own_rows = w_query.shape[0]
        half_width = w_query.shape[1] // 2
        ff_rows = w_down.shape[0]
        n_blocks = seq_size // 2
        ff_half = w_gate.shape[1] // 2

        x_half = lines.to_chip(tokens)
        x = lines.both_halves(x_half).reshape(seq_len, model)
        pos = lines.both_halves(lines.to_chip(positions)).reshape(seq_len)
        other_segments = lines.flip(segments, 1)
        seg = lines.pick(
            jnp.concatenate(
                [
                    jnp.where(core == 0, segments, other_segments),
                    jnp.where(core == 0, other_segments, segments),
                ]
            ),
            lines.z, 0,
        )
        seg_col, seg_row = seg[:, None], seg[None, :]
        cos, sin = angle_tables(pos, HEAD_DIM)
        sign = jnp.where(jnp.arange(HEAD_DIM) < HEAD_DIM // 2, -1.0, 1.0)
        cos = jnp.concatenate([cos, cos], axis=1)
        sin = jnp.concatenate([sin * sign, sin * sign], axis=1)

        def by_half(w):
            return w.reshape(own_rows, 2, w.shape[1] // 2)

        def by_owner(w):
            return w.reshape(own_rows, n_blocks, 2, w.shape[1] // (2 * n_blocks)).swapaxes(1, 2).reshape(own_rows, 2, w.shape[1] // 2)

        def both_rows(w):
            return lines.ordered(lines.pick(w, core, 1), lines.flip(lines.pick(w, 1 - core, 1), 1), core, 0)

        def gather_rows(w, x_first):
            full = lines.gather(w, x_first, 1)
            return full.reshape(-1, w.shape[-1])

        qk_piece = both_rows(jnp.concatenate([by_half(w_query), by_half(w_key)], axis=2))
        vo_piece = both_rows(jnp.concatenate([by_half(w_value), by_half(w_out)], axis=2))
        gate_piece = both_rows(by_owner(w_gate))
        up_piece = both_rows(by_owner(w_up))

        gains = jnp.stack([gain_attn, gain_mlp])
        gains = lines.gather(lines.ordered(gains, lines.flip(gains, 1), core, 0), True, 1)
        gains = jnp.moveaxis(gains, 4, 0).reshape(2, 1, model).astype(jnp.float32)
        gain_one, gain_two = gains[0], gains[1]

        qk_full = gather_rows(qk_piece, True)
        vo_full = gather_rows(vo_piece, False)
        w_qkv = jnp.concatenate([qk_full, vo_full[:, :half_width]], axis=1)
        out_half = vo_full[:, half_width:]
        out_full = lines.ordered(out_half, lines.flip(out_half, 1), core, 1).reshape(-1, model)

        normed, q, k, v = project(x, gain_one, w_qkv, cos, sin)
        ob_half, lse = attend(q, k, v, seg_col, seg_row)
        ob = lines.ordered(ob_half, lines.flip(ob_half, 1), core, 1).reshape(seq_len, model)

        gate_full = gather_rows(gate_piece, True)
        up_full = gather_rows(up_piece, False)
        split = ff_rows // 2
        down_full = jnp.concatenate(
            [
                lines.gather(w_down[:split], True, 0),
                lines.gather(w_down[split:], False, 0),
            ],
            axis=3,
        ).reshape(-1, model)
        dy_half = lines.to_chip(cotangent)
        dy = lines.both_halves(dy_half).reshape(seq_len, model)

        def own_half(t):
            return lines.pick(t.reshape(ctx_size, 2, span, t.shape[-1]), core, 1)

        h1 = x.astype(jnp.float32) + dot32(ob, out_full)
        normed_two = rms_scale(h1, gain_two).astype(jnp.bfloat16)
        gate = dot32(normed_two, gate_full)
        up = dot32(normed_two, up_full)
        s = jax.nn.sigmoid(gate)
        hid = (gate * s * up).astype(jnp.bfloat16)
        down = dot32(hid, down_full)
        h1_half = own_half(h1)
        out_sum = lines.sum_cores(down.reshape(ctx_size, 2, span, model))
        output = lines.from_chip((h1_half + out_sum).astype(jnp.bfloat16))

        d_hid = dot32(dy, down_full, NT)
        d_up = (d_hid * gate * s).astype(jnp.bfloat16)
        d_gate = (d_hid * up * s * (1.0 + gate * (1.0 - s))).astype(jnp.bfloat16)
        dc = dot32(d_gate, gate_full, NT) + dot32(d_up, up_full, NT)

        grad_down = dot32(hid, dy, TN).astype(jnp.bfloat16)
        grad_gate = dot32(normed_two, d_gate, TN).astype(jnp.bfloat16)
        grad_up = dot32(normed_two, d_up, TN).astype(jnp.bfloat16)

        def norm_back(u, gain, dn):
            r = lax.rsqrt(jnp.mean(u * u, axis=-1, keepdims=True) + EPS)
            gain_grad = jnp.sum(dn * u * r, axis=(0, 1))
            gd = gain * dn
            du = r * gd - u * (r * r * r) * jnp.mean(gd * u, axis=-1, keepdims=True)
            return du, gain_grad

        dc_half = lines.sum_cores(dc.reshape(ctx_size, 2, span, model))
        du2, gain_two_grad = norm_back(h1_half, gain_two, dc_half)
        dh1_half = dy_half.astype(jnp.float32) + du2
        db = lines.both_halves(dh1_half.astype(jnp.bfloat16)).reshape(seq_len, model)

        def scatter_rows(g, x_first):
            g = g.reshape(n_blocks // 2, 2, 2, ctx_size, own_rows, g.shape[-1])
            return lines.scatter(g, x_first, 1)

        def to_owner(g):
            other = lines.flip(lines.pick(g, 1 - core, 0), 1)
            return lines.ordered(lines.pick(g, core, 0), other, core, 1)

        down_view = grad_down.reshape(n_blocks // 2, 2, ctx_size, ff_rows, model)
        g_down = jnp.concatenate(
            [
                lines.scatter(down_view[:, :, :, :split], True, 0),
                lines.scatter(down_view[:, :, :, split:], False, 0),
            ]
        )

        def from_owner_columns(g):
            cols = g.shape[-1]
            return g.reshape(own_rows, 2, n_blocks, cols // n_blocks).swapaxes(1, 2).reshape(own_rows, 2 * cols)

        g_gate = from_owner_columns(to_owner(scatter_rows(grad_gate, True)))
        g_up = from_owner_columns(to_owner(scatter_rows(grad_up, False)))

        out_rows = lax.dynamic_slice_in_dim(out_full, core * half_width, half_width, axis=0)
        d_attended = dot32(db, out_rows, NT).astype(jnp.bfloat16)
        dq, dk, dv = attend_back(q, k, v, d_attended, lse, cos, sin, seg_col, seg_row)
        d_qkv = jnp.concatenate([dq, dk, dv], axis=1)
        grad_qkv = dot32(normed, d_qkv, TN).astype(jnp.bfloat16)
        db_cols = lines.pick(db.reshape(seq_len, 2, half_width), core, 1)
        grad_out = dot32(ob, db_cols, TN).astype(jnp.bfloat16)
        da = dot32(d_qkv, w_qkv, NT)
        da_half = lines.sum_cores(da.reshape(ctx_size, 2, span, model))
        du1, gain_one_grad = norm_back(x_half.astype(jnp.float32), gain_one, da_half)
        input_grad = lines.from_chip((dh1_half + du1).astype(jnp.bfloat16)).astype(jnp.float32)

        gqk = to_owner(scatter_rows(grad_qkv[:, : 2 * half_width], True))
        gvo = to_owner(
            scatter_rows(jnp.concatenate([grad_qkv[:, 2 * half_width :], grad_out], axis=1), False)
        )

        def two_halves(g):
            return g.reshape(own_rows, 2 * half_width)

        gain_grads = lines.sum_all(jnp.stack([gain_one_grad, gain_two_grad]))
        device = lax.axis_index("seq") * ctx_size + lines.z
        gain_grads = lax.dynamic_slice_in_dim(gain_grads, device * own_rows, own_rows, axis=1)
        return (
            output,
            input_grad,
            two_halves(gqk[:, :, :half_width]),
            two_halves(gqk[:, :, half_width:]),
            two_halves(gvo[:, :, :half_width]),
            two_halves(gvo[:, :, half_width:]),
            g_gate,
            g_up,
            g_down,
            gain_grads[0],
            gain_grads[1],
        )

    return on_device


def solution(mesh):
    in_specs = (
        P("seq", "ctx", None),
        P("seq", None),
        P("seq", "ctx"),
        P(("seq", "ctx"), None),
        P(("seq", "ctx"), None),
        P(("seq", "ctx"), None),
        P(("seq", "ctx"), None),
        P(("seq", "ctx"), None),
        P(("seq", "ctx"), None),
        P(("seq", "ctx"), None),
        P(("seq", "ctx")),
        P(("seq", "ctx")),
        P("seq", "ctx", None),
    )
    out_specs = (
        P("seq", "ctx", None),
        P("seq", "ctx", None),
        P(("seq", "ctx"), None),
        P(("seq", "ctx"), None),
        P(("seq", "ctx"), None),
        P(("seq", "ctx"), None),
        P(("seq", "ctx"), None),
        P(("seq", "ctx"), None),
        P(("seq", "ctx"), None),
        P(("seq", "ctx")),
        P(("seq", "ctx")),
    )
    seq_size, ctx_size = mesh.shape["seq"], mesh.shape["ctx"]
    one_each = sequence_per_chip(seq_size, ctx_size)

    def program(tokens, *others):
        if seq_size == 8 and ctx_size == 2 * tokens.shape[0]:
            return one_each(tokens, *others)
        return on_device(tokens, *others)

    return jax.shard_map(
        program, mesh=mesh, in_specs=in_specs, out_specs=out_specs, check_vma=False
    )
```

```python
import functools

import jax
import jax.numpy as jnp
from jax import lax
from jax.experimental import pallas as pl
from jax.experimental.pallas import tpu as pltpu
from jax.sharding import PartitionSpec as P

HEADS = 12
KV_HEADS = 12
HEAD_DIM = 64
VMEM = 56 << 20


epsilon = 1e-05


def shortened(value):
    return jax.tree.map(lambda a: a.astype(jnp.bfloat16) if a.dtype == jnp.float32 else a, value)


def rms_scale(values_in, gain_in):
    return (
        values_in
        * lax.rsqrt(jnp.mean(values_in * values_in, axis=-1, keepdims=True) + epsilon)
        * gain_in
    )


def angle_tables(position_ids, head_size):
    half_dim = head_size // 2
    frequency = 10000.0 ** (-(jnp.arange(half_dim, dtype=jnp.float32) * 2.0 / head_size))
    angles = position_ids.astype(jnp.float32)[:, None] * frequency[None, :]
    angles = jnp.concatenate([angles, angles], axis=-1)
    return (jnp.cos(angles), jnp.sin(angles))


def rotate(values_in, cosine, sine_table):
    half_dim = values_in.shape[-1] // 2
    turned = jnp.concatenate([-values_in[..., half_dim:], values_in[..., :half_dim]], axis=-1)
    return values_in * cosine[:, None, :] + turned * sine_table[:, None, :]


def unrotate(grad_in, cosine, sine_table):
    half_dim = grad_in.shape[-1] // 2
    scaled = grad_in * sine_table[:, None, :]
    turned = jnp.concatenate([scaled[..., half_dim:], -scaled[..., :half_dim]], axis=-1)
    return grad_in * cosine[:, None, :] + turned


def gather_flat(weight_set):
    return jax.tree.map(
        lambda part, own: part.astype(own.dtype),
        lax.all_gather(shortened(weight_set), ("seq", "ctx"), axis=0, tiled=True),
        weight_set,
    )


def fetch_weights(weight_set):
    return (gather_flat(weight_set), weight_set)


def fetch_again(kept_set):
    return gather_flat(kept_set)


def reduce_grads(grad_set):
    return lax.psum_scatter(grad_set, ("seq", "ctx"), scatter_dimension=0, tiled=True)


def on_device(
    tokens,
    segments,
    positions,
    w_query,
    w_key,
    w_value,
    w_out,
    w_gate,
    w_up,
    w_down,
    gain_attn,
    gain_mlp,
    cotangent,
):
    seq_count, local_len, model_width = tokens.shape
    seq_len = segments.shape[1]
    row_count = seq_count * local_len
    head_group = HEADS // KV_HEADS
    kv_width = KV_HEADS * HEAD_DIM
    score_scale = HEAD_DIM ** (-0.5)
    first_token = lax.axis_index("ctx") * local_len
    own_tokens = first_token + jnp.arange(local_len, dtype=jnp.int32)
    all_tokens = jnp.arange(seq_len, dtype=jnp.int32)
    causal = all_tokens[None, :] <= own_tokens[:, None]
    inputs = tokens.reshape(row_count, model_width).astype(jnp.float32)
    cosine, sine_table = angle_tables(positions.reshape(row_count), HEAD_DIM)
    attn_full, attn_kept = fetch_weights((w_query, w_key, w_value, w_out, gain_attn))
    full_query, full_key, full_value, full_out, full_gain_one = attn_full
    normed = rms_scale(inputs, full_gain_one.astype(jnp.float32)).astype(jnp.bfloat16)
    query_proj = jnp.dot(normed, full_query, preferred_element_type=jnp.float32)
    key_proj = jnp.dot(normed, full_key, preferred_element_type=jnp.float32)
    value_proj = jnp.dot(normed, full_value, preferred_element_type=jnp.float32)
    query_rot = rotate(query_proj.reshape(row_count, HEADS, HEAD_DIM), cosine, sine_table).astype(
        jnp.bfloat16
    )
    key_rot = rotate(key_proj.reshape(row_count, KV_HEADS, HEAD_DIM), cosine, sine_table).astype(
        jnp.bfloat16
    )
    value_low = value_proj.astype(jnp.bfloat16)
    keys_all, values_all = (
        lax.all_gather(key_rot.reshape(seq_count, local_len, kv_width), "ctx", axis=1, tiled=True),
        lax.all_gather(
            value_low.reshape(seq_count, local_len, kv_width), "ctx", axis=1, tiled=True
        ),
    )
    queries = query_rot.reshape(seq_count, local_len, KV_HEADS, head_group, HEAD_DIM)

    def scores_of(q_seq, k_seq, seg_seq):
        own_seg = lax.dynamic_slice_in_dim(seg_seq, first_token, local_len)
        allowed = causal & (own_seg[:, None] == seg_seq[None, :])
        k_heads = k_seq.reshape(seq_len, KV_HEADS, HEAD_DIM)
        raw_scores = jnp.einsum(
            "qkgd,skd->kgqs", q_seq, k_heads, preferred_element_type=jnp.float32
        )
        return jnp.where(allowed[None, None], raw_scores * score_scale, -1e30)

    def attend(pieces):
        q_seq, k_seq, v_seq, seg_seq = pieces
        logits = scores_of(q_seq, k_seq, seg_seq)
        row_max = jnp.max(logits, axis=-1, keepdims=True)
        shifted_exp = jnp.exp(logits - row_max)
        row_sum = jnp.sum(shifted_exp, axis=-1, keepdims=True)
        probs_low = (shifted_exp / row_sum).astype(jnp.bfloat16)
        mixed_heads = jnp.einsum(
            "kgqs,skd->qkgd",
            probs_low,
            v_seq.reshape(seq_len, KV_HEADS, HEAD_DIM),
            preferred_element_type=jnp.float32,
        )
        return (
            mixed_heads.astype(jnp.bfloat16).reshape(local_len, model_width),
            (row_max + jnp.log(row_sum))[..., 0],
        )

    attended, log_totals = lax.map(attend, (queries, keys_all, values_all, segments))
    attended = attended.reshape(row_count, model_width)
    hidden_state = inputs + jnp.dot(attended, full_out, preferred_element_type=jnp.float32)
    mlp_full, mlp_kept = fetch_weights((w_gate, w_up, w_down, gain_mlp))
    full_gate, full_up, full_down, full_gain_two = mlp_full
    normed_two = rms_scale(hidden_state, full_gain_two.astype(jnp.float32)).astype(jnp.bfloat16)
    gate_proj = jnp.dot(normed_two, full_gate, preferred_element_type=jnp.float32)
    up_proj = jnp.dot(normed_two, full_up, preferred_element_type=jnp.float32)
    activated = (jax.nn.silu(gate_proj) * up_proj).astype(jnp.bfloat16)
    final_state = hidden_state + jnp.dot(activated, full_down, preferred_element_type=jnp.float32)
    output = final_state.astype(jnp.bfloat16).reshape(seq_count, local_len, model_width)
    out_grad = cotangent.reshape(row_count, model_width)
    again_gate, again_up, again_down, again_gain_two = fetch_again(mlp_kept)
    grad_down = jnp.einsum("tf,td->fd", activated, out_grad, preferred_element_type=jnp.float32)
    d_activated = jnp.einsum("td,fd->tf", out_grad, again_down, preferred_element_type=jnp.float32)

    def swiglu(gate_in, up_in):
        return jax.nn.silu(gate_in) * up_in

    unused_mlp, swiglu_back = jax.vjp(swiglu, gate_proj, up_proj)
    d_gate, d_up = swiglu_back(d_activated)
    d_gate = d_gate.astype(jnp.bfloat16)
    d_up = d_up.astype(jnp.bfloat16)
    grad_gate = jnp.einsum("td,tf->df", normed_two, d_gate, preferred_element_type=jnp.float32)
    grad_up = jnp.einsum("td,tf->df", normed_two, d_up, preferred_element_type=jnp.float32)
    d_normed_two = jnp.einsum(
        "tf,df->td", d_gate, again_gate, preferred_element_type=jnp.float32
    ) + jnp.einsum("tf,df->td", d_up, again_up, preferred_element_type=jnp.float32)
    unused_norm, norm_two_back = jax.vjp(
        rms_scale, hidden_state, again_gain_two.astype(jnp.float32)
    )
    d_hidden, grad_gain_mlp = norm_two_back(d_normed_two)
    mlp_sums = reduce_grads((grad_gate, grad_up, grad_down, grad_gain_mlp))
    d_hidden = d_hidden + out_grad.astype(jnp.float32)
    d_branch = d_hidden.astype(jnp.bfloat16)
    again_query, again_key, again_value, again_out, again_gain_one = fetch_again(attn_kept)
    grad_out = jnp.einsum("td,te->de", attended, d_branch, preferred_element_type=jnp.float32)
    d_attended = jnp.einsum(
        "te,de->td", d_branch, again_out, preferred_element_type=jnp.float32
    ).astype(jnp.bfloat16)
    d_heads = d_attended.reshape(seq_count, local_len, KV_HEADS, head_group, HEAD_DIM)

    def attend_back(pieces):
        q_seq, k_seq, v_seq, seg_seq, lse_seq, do_seq = pieces
        logits = scores_of(q_seq, k_seq, seg_seq)
        probs = jnp.exp(logits - lse_seq[..., None])
        probs_low = probs.astype(jnp.bfloat16)
        v_heads = v_seq.reshape(seq_len, KV_HEADS, HEAD_DIM)
        d_probs = jnp.einsum("qkgd,skd->kgqs", do_seq, v_heads, preferred_element_type=jnp.float32)
        d_value = jnp.einsum(
            "kgqs,qkgd->skd", probs_low, do_seq, preferred_element_type=jnp.float32
        )
        row_dot = jnp.sum(probs * d_probs, axis=-1, keepdims=True)
        d_scores = (probs * (d_probs - row_dot) * score_scale).astype(jnp.bfloat16)
        d_query = jnp.einsum(
            "kgqs,skd->qkgd",
            d_scores,
            k_seq.reshape(seq_len, KV_HEADS, HEAD_DIM),
            preferred_element_type=jnp.float32,
        )
        d_key = jnp.einsum("kgqs,qkgd->skd", d_scores, q_seq, preferred_element_type=jnp.float32)
        return (
            d_query.reshape(local_len, HEADS, HEAD_DIM),
            d_key.reshape(seq_len, kv_width),
            d_value.reshape(seq_len, kv_width),
        )

    d_query_all, d_key_part, d_value_part = lax.map(
        attend_back, (queries, keys_all, values_all, segments, log_totals, d_heads)
    )
    d_key_own, d_value_own = (
        lax.psum_scatter(d_key_part, "ctx", scatter_dimension=1, tiled=True),
        lax.psum_scatter(d_value_part, "ctx", scatter_dimension=1, tiled=True),
    )
    d_query_low = (
        unrotate(d_query_all.reshape(row_count, HEADS, HEAD_DIM), cosine, sine_table)
        .astype(jnp.bfloat16)
        .reshape(row_count, model_width)
    )
    d_key_low = (
        unrotate(d_key_own.reshape(row_count, KV_HEADS, HEAD_DIM), cosine, sine_table)
        .astype(jnp.bfloat16)
        .reshape(row_count, kv_width)
    )
    d_value_low = d_value_own.reshape(row_count, kv_width).astype(jnp.bfloat16)
    grad_query = jnp.einsum("td,te->de", normed, d_query_low, preferred_element_type=jnp.float32)
    grad_key = jnp.einsum("td,te->de", normed, d_key_low, preferred_element_type=jnp.float32)
    grad_value = jnp.einsum("td,te->de", normed, d_value_low, preferred_element_type=jnp.float32)
    d_normed = jnp.einsum("te,de->td", d_query_low, again_query, preferred_element_type=jnp.float32)
    d_normed = d_normed + jnp.einsum(
        "te,de->td", d_key_low, again_key, preferred_element_type=jnp.float32
    )
    d_normed = d_normed + jnp.einsum(
        "te,de->td", d_value_low, again_value, preferred_element_type=jnp.float32
    )
    unused_first, norm_one_back = jax.vjp(rms_scale, inputs, again_gain_one.astype(jnp.float32))
    d_inputs, grad_gain_attn = norm_one_back(d_normed)
    attn_sums = reduce_grads((grad_query, grad_key, grad_value, grad_out, grad_gain_attn))
    input_grad = (d_hidden + d_inputs).reshape(seq_count, local_len, model_width)
    return (
        output,
        input_grad,
        attn_sums[0],
        attn_sums[1],
        attn_sums[2],
        attn_sums[3],
        mlp_sums[0],
        mlp_sums[1],
        mlp_sums[2],
        attn_sums[4],
        mlp_sums[3],
    )


EPS = epsilon
NEG = -1e30


def dot32(left, right, dims=((1,), (0,))):
    return lax.dot_general(left, right, (dims, ((), ())), preferred_element_type=jnp.float32)


NT = ((1,), (1,))
TN = ((0,), (0,))


def lane_mask(rows):
    return lax.broadcasted_iota(jnp.int32, (rows, 128), 1) < HEAD_DIM


def swap_halves(u):
    half = HEAD_DIM // 2
    lanes = lax.broadcasted_iota(jnp.int32, u.shape, 1) % HEAD_DIM
    return jnp.where(lanes < half, pltpu.roll(u, 128 - half, 1), pltpu.roll(u, half, 1))


def allowed_pairs(seg_col, seg_row, first, rows, keys):
    q_ids = lax.broadcasted_iota(jnp.int32, (rows, keys), 0) + first
    k_ids = lax.broadcasted_iota(jnp.int32, (rows, keys), 1)
    return (k_ids <= q_ids) & (seg_col == seg_row)


def attend_kernel(block, qk_ref, v_ref, seg_col_ref, seg_row_ref, *refs):
    o_ref, lse_ref = refs[-2:]
    length = qk_ref.shape[0]
    first_head = lane_mask(block)
    for step in range(length // block):
        rows = slice(step * block, (step + 1) * block)
        keys = (step + 1) * block
        allowed = allowed_pairs(
            seg_col_ref[rows, :1], seg_row_ref[:, :keys], step * block, block, keys
        )
        q_pair = qk_ref[rows, :128]
        k_pair = qk_ref[:keys, 128:]
        v_pair = v_ref[:keys, :]
        outs, totals = [], []
        for head in range(2):
            mine = first_head if head == 0 else jnp.logical_not(first_head)
            q_head = jnp.where(mine, q_pair, jnp.zeros_like(q_pair))
            z = jnp.where(allowed, dot32(q_head, k_pair, NT), NEG)
            top = jnp.max(z, axis=-1, keepdims=True)
            e = jnp.exp(z - top)
            total = jnp.sum(e, axis=-1, keepdims=True)
            p = (e * (1.0 / total)).astype(jnp.bfloat16)
            outs.append(dot32(p, v_pair))
            totals.append(top + jnp.log(total))
        o_ref[rows, :] = jnp.where(first_head, outs[0], outs[1]).astype(o_ref.dtype)
        lse_ref[rows, :] = jnp.where(first_head, totals[0], totals[1])


def attend_back_kernel(
    block, qk_ref, v_ref, do_ref, lse_ref, cos_ref, sin_ref, seg_col_ref, seg_row_ref, *refs
):
    dqk_ref, dv_ref, dk_sum, dv_sum = refs[-4:]
    length = qk_ref.shape[0]
    first_head = lane_mask(block)
    for step in range(length // block):
        rows = slice(step * block, (step + 1) * block)
        keys = (step + 1) * block
        allowed = allowed_pairs(
            seg_col_ref[rows, :1], seg_row_ref[:, :keys], step * block, block, keys
        )
        q_pair = qk_ref[rows, :128]
        k_pair = qk_ref[:keys, 128:]
        v_pair = v_ref[:keys, :]
        do_pair = do_ref[rows, :]
        dq_heads = []
        dk_step = dv_step = None
        for head in range(2):
            mine = first_head if head == 0 else jnp.logical_not(first_head)
            q_head = jnp.where(mine, q_pair, jnp.zeros_like(q_pair))
            do_head = jnp.where(mine, do_pair, jnp.zeros_like(do_pair))
            lse = lse_ref[rows, head * HEAD_DIM : head * HEAD_DIM + 1]
            z = jnp.where(allowed, dot32(q_head, k_pair, NT), NEG)
            p = jnp.exp(z - lse)
            dp = dot32(do_head, v_pair, NT)
            dv_head = dot32(p.astype(jnp.bfloat16), do_head, TN)
            row_dot = jnp.sum(p * dp, axis=-1, keepdims=True)
            ds = (p * (dp - row_dot)).astype(jnp.bfloat16)
            dq_heads.append(dot32(ds, k_pair))
            dk_head = dot32(ds, q_head, TN)
            dk_step = dk_head if dk_step is None else dk_step + dk_head
            dv_step = dv_head if dv_step is None else dv_step + dv_head
        dq = jnp.where(first_head, dq_heads[0], dq_heads[1]) * (HEAD_DIM**-0.5)
        dq = dq * cos_ref[rows, :] - swap_halves(dq) * sin_ref[rows, :]
        dqk_ref[rows, :128] = dq.astype(dqk_ref.dtype)
        last = slice(step * block, keys)
        if step > 0:
            dk_sum[: step * block, :] += dk_step[: step * block]
            dv_sum[: step * block, :] += dv_step[: step * block]
        dk_sum[last, :] = dk_step[step * block :]
        dv_sum[last, :] = dv_step[step * block :]
    dk = dk_sum[...]
    dk = dk * cos_ref[...] - swap_halves(dk) * sin_ref[...]
    dqk_ref[:, 128:] = dk.astype(dqk_ref.dtype)
    dv_ref[...] = dv_sum[...].astype(dv_ref.dtype)


def qkv_kernel(x_ref, gain_ref, qk_w_ref, v_w_ref, cos_ref, sin_ref, a_ref, qk_ref, v_ref):
    x = x_ref[...].astype(jnp.float32)
    r = lax.rsqrt(jnp.mean(x * x, axis=-1, keepdims=True) + EPS)
    a = (x * r * gain_ref[...]).astype(jnp.bfloat16)
    a_ref[...] = a
    u = dot32(a, qk_w_ref[...])
    cos, sin = cos_ref[...], sin_ref[...]
    for at in range(0, u.shape[1], 256):
        q = u[:, at : at + 128]
        q = (q * cos + swap_halves(q) * sin) * (HEAD_DIM**-0.5)
        qk_ref[:, at : at + 128] = q.astype(jnp.bfloat16)
        k = u[:, at + 128 : at + 256]
        k = k * cos + swap_halves(k) * sin
        qk_ref[:, at + 128 : at + 256] = k.astype(jnp.bfloat16)
    v_ref[...] = dot32(a, v_w_ref[...]).astype(jnp.bfloat16)


def whole(shape):
    return pl.BlockSpec(shape, lambda i: (0,) * len(shape))


def row_block(rows, width):
    return pl.BlockSpec((rows, width), lambda i: (i, 0))


def lane_block(length):
    return pl.BlockSpec((length, 128), lambda i: (0, i))


def project(x, gain, w_qk, w_v, cos, sin):
    length, model = x.shape
    width = w_v.shape[1]
    rows = 256
    low = lambda n: jax.ShapeDtypeStruct((length, n), jnp.bfloat16)
    return pl.pallas_call(
        qkv_kernel,
        grid=(length // rows,),
        in_specs=[
            row_block(rows, model), whole((1, model)), whole(w_qk.shape), whole(w_v.shape),
            row_block(rows, 128), row_block(rows, 128),
        ],
        out_specs=[row_block(rows, model), row_block(rows, 2 * width), row_block(rows, width)],
        out_shape=[low(model), low(2 * width), low(width)],
        compiler_params=pltpu.CompilerParams(vmem_limit_bytes=VMEM),
        cost_estimate=pl.CostEstimate(flops=1, bytes_accessed=1, transcendentals=0),
        name="project",
    )(x, gain, w_qk, w_v, cos, sin)


def over_pairs(kernel, name, arrays, shared, outs, scratch):
    length = arrays[0].shape[0]
    pairs = arrays[1].shape[1] // 128
    of_pair = lambda width: pl.BlockSpec((length, width), lambda i: (0, i))
    return pl.pallas_call(
        functools.partial(kernel, 256),
        grid=(pairs,),
        in_specs=[of_pair(a.shape[1] // pairs) for a in arrays] + [whole(a.shape) for a in shared],
        out_specs=[of_pair(width) for width, _ in outs],
        out_shape=[jax.ShapeDtypeStruct((length, pairs * width), kind) for width, kind in outs],
        scratch_shapes=scratch,
        compiler_params=pltpu.CompilerParams(vmem_limit_bytes=VMEM),
        cost_estimate=pl.CostEstimate(flops=1, bytes_accessed=1, transcendentals=0),
        name=name,
    )(*arrays, *shared)


def attend(qk, v, seg_col, seg_row):
    return over_pairs(
        attend_kernel, "attend", (qk, v), (seg_col, seg_row),
        [(128, jnp.bfloat16), (128, jnp.float32)], [],
    )


def attend_back(qk, v, do, lse, cos, sin, seg_col, seg_row):
    length = v.shape[0]
    return over_pairs(
        attend_back_kernel, "attend_back", (qk, v, do, lse), (cos, sin, seg_col, seg_row),
        [(256, jnp.bfloat16), (128, jnp.bfloat16)],
        [pltpu.VMEM((length, 128), jnp.float32)] * 2,
    )


def by_bit(own, other, bit, axis):
    own, other = jnp.expand_dims(own, axis), jnp.expand_dims(other, axis)
    shape = [1] * own.ndim
    shape[axis] = 2
    return jnp.where(lax.broadcasted_iota(jnp.int32, shape, axis) == bit, own, other)


def pick(v, at, axis):
    return lax.dynamic_index_in_dim(v, at, axis, keepdims=False)


class Cube:
    def __init__(self, seq_size, ctx_size):
        self.sizes = {"seq": seq_size, "ctx": ctx_size}
        self.steps = {"core": ("seq", 1), "x": ("seq", 2), "y": ("seq", 4), "z0": ("ctx", 1), "z1": ("ctx", 2)}
        self.bits = {
            name: (lax.axis_index(axis) // step) % 2 for name, (axis, step) in self.steps.items()
        }
        self.last = ()

    def step(self, work, *arrays):
        if self.last:
            arrays = lax.optimization_barrier((arrays, self.last))[0]
        result = work(*arrays)
        self.last = tuple(jax.tree.leaves(result))
        return result

    def swap(self, v, name):
        axis, step = self.steps[name]
        return lax.ppermute(v, axis, [(i, i ^ step) for i in range(self.sizes[axis])])

    def mine(self, v, name, axis):
        return pick(v, self.bits[name], axis)

    def away(self, v, name, axis):
        return pick(v, 1 - self.bits[name], axis)

    def joined(self, own, other, name, axis):
        return by_bit(own, other, self.bits[name], axis)

    def traded(self, v, came, steps):
        for other, (name, axis, at) in zip(came, steps):
            v = by_bit(self.mine(v, name, axis), other, self.bits[name], at)
        return v

    def summed(self, v, came, steps):
        for other, (name, axis) in zip(came, steps):
            v = low(wide(self.mine(v, name, axis)) + wide(other))
        return v

def low(v):
    return v.astype(jnp.bfloat16)


def wide(v):
    return v.astype(jnp.float32)


def rows_of(v):
    return v.reshape(-1, v.shape[-1])


def r_of(u):
    return lax.rsqrt(jnp.mean(u * u, axis=-1, keepdims=True) + EPS)


def norm_back(u, gain, dn):
    r = r_of(u)
    gd = gain * dn
    return r * gd - u * (r * r * r) * jnp.mean(gd * u, axis=-1, keepdims=True)


def sequence_per_chip(seq_size, ctx_size):
    def on_device(
        tokens, segments, positions,
        w_query, w_key, w_value, w_out, w_gate, w_up, w_down,
        gain_attn, gain_mlp, cotangent,
    ):
        cube = Cube(seq_size, ctx_size)
        step, swap, mine, away = cube.step, cube.swap, cube.mine, cube.away
        joined, traded, summed = cube.joined, cube.traded, cube.summed
        bits = cube.bits
        core = cube.bits["core"]
        seqs, local_len, model = tokens.shape
        seq_len = segments.shape[1]
        span = local_len // 2
        own_rows = w_query.shape[0]
        half_width = w_query.shape[1] // 2
        ff_rows = w_down.shape[0]
        ff_half = w_gate.shape[1] // 2
        n_blocks = seq_size // 2
        ff_block = ff_half // n_blocks
        model_half = model // 2
        pairs = half_width // 128

        def half_of(w, half):
            return lax.dynamic_slice_in_dim(w, half * (w.shape[1] // 2), w.shape[1] // 2, axis=1)

        def owned_by(w, half):
            w = w.reshape(own_rows, n_blocks, 2, ff_block)
            return pick(w, half, 2).reshape(own_rows, ff_half)

        def attn_rows(half, query, key, value, out, gain_one, gain_two):
            query, key, value, out = (half_of(w, half) for w in (query, key, value, out))
            parts = [w[:, i * 128 : (i + 1) * 128] for i in range(pairs) for w in (query, key)]
            gains = jnp.pad(jnp.stack([gain_one, gain_two], axis=1), ((0, 0), (0, 126)))
            return jnp.concatenate(parts + [value, out, gains], axis=1)

        attn_shards = (w_query, w_key, w_value, w_out, gain_attn, gain_mlp)
        sent = step(lambda *w: attn_rows(1 - core, *w), *attn_shards)
        attn_came = swap(sent, "core")

        def pack_tokens(tokens, positions, segments):
            own_first = lax.axis_index("ctx") * local_len
            own_segments = lax.dynamic_slice_in_dim(segments, own_first, local_len, axis=1)
            numbers = low(jnp.stack([positions // 32, positions % 32, own_segments]))
            numbers = numbers.reshape(3, seqs, 2, span).transpose(1, 2, 0, 3)
            numbers = numbers.reshape(seqs, 2, 1, 3 * span)
            numbers = jnp.pad(numbers, ((0, 0), (0, 0), (0, 15), (0, model - 3 * span)))
            pack = jnp.concatenate([tokens.reshape(seqs, 2, span, model), numbers], axis=2)
            return pack, away(pack, "core", 1)

        to_chip = (("core", 1, 0), ("z0", 1, 1), ("z1", 0, 0))

        def sent_next(steps, n):
            name, axis = steps[n][:2]
            return lambda v, *came: away(traded(v, came, steps), name, axis)

        x_pack, sent = step(pack_tokens, tokens, positions, segments)
        x_came = [swap(sent, "core")]
        attn_piece = step(
            lambda came, *w: joined(attn_rows(core, *w), came, "core", 0), attn_came, *attn_shards
        )
        attn_came = swap(attn_piece, "z1")
        x_came.append(swap(step(sent_next(to_chip, 1), x_pack, *x_came), "z0"))

        def ff_both(gate, up):
            def of(half):
                return jnp.concatenate([owned_by(gate, half), owned_by(up, half)], axis=1)

            return of(core), of(1 - core)

        ff_own, sent = step(ff_both, w_gate, w_up)
        ff_came = swap(sent, "core")
        first, last = step(lambda w: (w[:, :model_half], w[:, model_half:]), w_down)
        first_came, last_came = swap(first, "x"), swap(last, "y")
        ff_piece = step(lambda v, w: joined(v, w, "core", 0), ff_own, ff_came)

        attn_half_line = step(lambda v, w: joined(v, w, "z1", 1), attn_piece, attn_came)
        attn_came = swap(attn_half_line, "z0")
        ff_came = swap(ff_piece, "z1")
        down_pair = step(
            lambda a, b, c, d: jnp.concatenate(
                [joined(a, b, "x", 0), joined(c, d, "y", 0)], axis=2
            ),
            first, first_came, last, last_came,
        )
        x_came.append(swap(step(sent_next(to_chip, 2), x_pack, *x_came), "z1"))
        dy_pack = cotangent.reshape(seqs, 2, span, model)
        dy_came = [swap(step(sent_next(to_chip, 0), dy_pack), "core")]

        def attn_to_line(v, came):
            line = joined(v, came, "z0", 2)
            return line[..., : 2 * half_width], line[..., 2 * half_width :]

        qk_line, vo_line = step(attn_to_line, attn_half_line, attn_came)
        qk_came, vo_came = swap(qk_line, "x"), swap(vo_line, "y")
        ff_half_line = step(lambda v, w: joined(v, w, "z1", 1), ff_piece, ff_came)
        ff_came = swap(ff_half_line, "z0")
        qk_plane = step(lambda v, w: joined(v, w, "x", 0), qk_line, qk_came)
        qk_came = swap(qk_plane, "y")
        vo_plane = step(lambda v, w: joined(v, w, "y", 0), vo_line, vo_came)
        vo_came = swap(vo_plane, "x")

        x_half = step(
            lambda v, *came: traded(v, came, to_chip).reshape(ctx_size, -1, model), x_pack, *x_came
        )
        x_other = swap(x_half, "core")
        down_came = swap(down_pair, "z1")

        def ff_to_line(v, came):
            line = joined(v, came, "z0", 2)
            return line[..., :ff_half], line[..., ff_half:]

        gate_line, up_line = step(ff_to_line, ff_half_line, ff_came)

        def unpack_tokens(x_half, x_other):
            x = joined(x_half[:, :span], x_other[:, :span], "core", 1).reshape(seq_len, model)
            numbers = joined(x_half[:, span, : 3 * span], x_other[:, span, : 3 * span], "core", 1)
            numbers = numbers.astype(jnp.int32).reshape(ctx_size, 2, 3, span)
            numbers = numbers.transpose(2, 0, 1, 3).reshape(3, seq_len)
            pos, seg = numbers[0] * 32 + numbers[1], numbers[2]
            lanes = jnp.arange(128, dtype=jnp.int32)
            half = HEAD_DIM // 2
            steps = (lanes % half).astype(jnp.float32) * 2.0 / HEAD_DIM
            angles = pos.astype(jnp.float32)[:, None] * (10000.0**-steps)[None, :]
            sign = jnp.where(lanes % HEAD_DIM < half, -1.0, 1.0)
            cos, sin = jnp.cos(angles), jnp.sin(angles) * sign
            seg_col = jnp.broadcast_to(seg[:, None], (seq_len, 128))
            return x, x_half[:, :span], seg_col, seg[None, :], cos, sin

        x, x_half, seg_col, seg_row, cos, sin = step(unpack_tokens, x_half, x_other)

        def attn_to_full(qk, qk_came, vo, vo_came):
            qk = rows_of(joined(qk, qk_came, "y", 0))
            vo = rows_of(joined(vo, vo_came, "x", 1))
            gains = wide(vo[:, 2 * half_width : 2 * half_width + 2])
            return (
                qk, vo[:, :half_width], vo[:, half_width : 2 * half_width],
                gains[:, 0][None, :], gains[:, 1],
            )

        qk_full, v_full, out_half, gain_one, gain_two = step(
            attn_to_full, qk_plane, qk_came, vo_plane, vo_came
        )
        out_came = swap(out_half, "core")
        gate_came, up_came = swap(gate_line, "x"), swap(up_line, "y")
        dy_came.append(swap(step(sent_next(to_chip, 1), dy_pack, *dy_came), "z0"))
        down_half_line = step(lambda v, w: joined(v, w, "z1", 1), down_pair, down_came)
        down_came = swap(down_half_line, "z0")

        def halves(own, other):
            whole = jnp.zeros((own.shape[0], 2 * own.shape[1]), own.dtype)
            whole = lax.dynamic_update_slice(whole, own, (0, core * own.shape[1]))
            return lax.dynamic_update_slice(whole, other, (0, (1 - core) * own.shape[1]))

        normed, qk, v = step(lambda *t: tuple(project(*t)), x, gain_one, qk_full, v_full, cos, sin)
        segs = (seg_col, seg_row)
        gate_plane = step(lambda v, w: joined(v, w, "x", 0), gate_line, gate_came)
        gate_came = swap(gate_plane, "y")
        up_plane = step(lambda v, w: joined(v, w, "y", 0), up_line, up_came)
        up_came = swap(up_plane, "x")
        out_full = step(halves, out_half, out_came)
        dy_came.append(swap(step(sent_next(to_chip, 2), dy_pack, *dy_came), "z1"))

        def down_to_line(v, came):
            line = joined(v, came, "z0", 2)
            return line[..., :model_half], line[..., model_half:]

        first_line, last_line = step(down_to_line, down_half_line, down_came)
        ob_half, lse = step(lambda *t: tuple(attend(*t)), qk, v, *segs)
        ob_came = swap(ob_half, "core")
        first_came, last_came = swap(first_line, "y"), swap(last_line, "x")

        def lay(into, own, bit, axis):
            return lax.dynamic_update_index_in_dim(into, own, bit, axis)

        def lay_own(gate, up):
            ff = jnp.zeros((2,) + gate.shape, gate.dtype)
            return lay(ff, gate, bits["y"], 0), lay(ff, up, bits["x"], 1)

        gate_part, up_part = step(lay_own, gate_plane, up_plane)
        dy_half = step(
            lambda v, *came: traded(v, came, to_chip).reshape(ctx_size, span, model),
            dy_pack, *dy_came,
        )
        dy_other = swap(dy_half, "core")
        gate_full, up_full = step(
            lambda a, b, c, d: (
                rows_of(lay(a, b, 1 - bits["y"], 0)), rows_of(lay(c, d, 1 - bits["x"], 1))
            ),
            gate_part, gate_came, up_part, up_came,
        )
        ob = step(halves, ob_half, ob_came)

        def own_half(t):
            return mine(t.reshape(ctx_size, 2, span, t.shape[-1]), "core", 1)

        def hidden(x, ob, out_full, gain_two):
            h1 = wide(x) + dot32(ob, out_full)
            return h1, low(h1 * r_of(h1) * gain_two)

        h1, normed_two = step(hidden, x, ob, out_full, gain_two)
        gate = step(dot32, normed_two, gate_full)

        def up_and_hidden(normed_two, up_full, gate):
            up = dot32(normed_two, up_full)
            return up, low(gate * jax.nn.sigmoid(gate) * up)

        dy = step(
            lambda a, b: joined(a, b, "core", 1).reshape(seq_len, model), dy_half, dy_other
        )
        up, hid = step(up_and_hidden, normed_two, up_full, gate)
        down_full = step(
            lambda a, b, c, d: rows_of(
                jnp.concatenate([joined(a, b, "y", 0), joined(c, d, "x", 1)], axis=-1)
            ),
            first_line, first_came, last_line, last_came,
        )

        def rows_view(g):
            return g.reshape(2, 2, 2, 2, 2, own_rows, g.shape[-1])

        def back(dy, down_full, gate, up):
            d_hid = dot32(dy, down_full, NT)
            s = jax.nn.sigmoid(gate)
            return low(d_hid * up * s * (1.0 + gate * (1.0 - s))), low(d_hid * gate * s)

        by_x = (("x", 1), ("y", 0), ("z0", 2), ("z1", 1), ("core", 0))
        by_y = (("y", 0), ("x", 0), ("z0", 2), ("z1", 1), ("core", 0))
        down_by_x = (("x", 1), ("y", 0), ("z0", 1), ("z1", 0))
        down_by_y = (("y", 0), ("x", 0), ("z0", 1), ("z1", 0))

        def to_send(steps, n):
            name, axis = steps[n]
            return lambda v, *came: away(summed(v, came, steps), name, axis)

        def grad_and_send(steps):
            def work(c, d):
                g = rows_view(low(dot32(c, d, TN)))
                return g, away(g, *steps[0])

            return work

        d_gate, d_up = step(back, dy, down_full, gate, up)
        grad_gate, sent = step(grad_and_send(by_x), normed_two, d_gate)
        gate_came = [swap(sent, "x")]
        grad_up, sent = step(grad_and_send(by_y), normed_two, d_up)
        up_came = [swap(sent, "y")]

        def dc_of(d_gate, gate_full, d_up, up_full):
            dc = dot32(d_gate, gate_full, NT) + dot32(d_up, up_full, NT)
            return dc, away(dc.reshape(ctx_size, 2, span, model), "core", 1)

        dc, sent = step(dc_of, d_gate, gate_full, d_up, up_full)
        dc_came = swap(sent, "core")

        def down_of(hid, down_full):
            down = dot32(hid, down_full).reshape(ctx_size, 2, span, model)
            return down, away(down, "core", 1)

        down, sent = step(down_of, hid, down_full)
        down_came = swap(sent, "core")

        def attn_side(dc, came, h1, dy_half, gain_two):
            dc_half = own_half(dc) + came
            dh1 = wide(dy_half) + norm_back(own_half(h1), gain_two, dc_half)
            return dh1, low(dh1), jnp.sum(dc * h1 * r_of(h1), axis=0)

        dh1_half, db_half, gain_two_grad = step(attn_side, dc, dc_came, h1, dy_half, gain_two)
        db_came = swap(db_half, "core")
        home_steps = (("z0", 1, 1), ("z1", 0, 0), ("core", 0, 1))

        def out_of(h1, down, came):
            out = low(own_half(h1) + mine(down, "core", 1) + came).reshape(2, 2, span, model)
            return out, away(out, "z0", 1)

        home, sent = step(out_of, h1, down, down_came)
        home_came = [swap(sent, "z0")]

        def down_grads(hid, dy):
            g = low(dot32(hid, dy, TN)).reshape(2, 2, 2, 2, ff_rows, model)
            first, last = g[..., :model_half], g[..., model_half:]
            return g, away(first, "x", 1), away(last, "y", 0)

        grad_down, sent_first, sent_last = step(down_grads, hid, dy)

        def d_attended_of(db_half, db_came, out_full):
            db = joined(db_half, db_came, "core", 1).reshape(seq_len, model)
            out_rows = lax.dynamic_slice_in_dim(out_full, core * half_width, half_width, axis=0)
            return db, low(dot32(db, out_rows, NT))

        db, d_attended = step(d_attended_of, db_half, db_came, out_full)
        first_came, last_came = [swap(sent_first, "x")], [swap(sent_last, "y")]

        def second(over_x, x_came, over_y, y_came):
            return to_send(by_x, 1)(over_x, x_came), to_send(by_y, 1)(over_y, y_came)

        sent_gate, sent_up = step(second, grad_gate, *gate_came, grad_up, *up_came)
        gate_came.append(swap(sent_gate, "y"))
        up_came.append(swap(sent_up, "x"))
        home_came.append(swap(step(sent_next(home_steps, 1), home, *home_came), "z1"))
        dqk, dv = step(
            lambda *t: tuple(attend_back(*t)), qk, v, d_attended, lse, cos, sin, *segs
        )

        def down_second(g, x_came, y_came):
            return (
                to_send(down_by_x, 1)(g[..., :model_half], x_came),
                to_send(down_by_y, 1)(g[..., model_half:], y_came),
            )

        sent_first, sent_last = step(down_second, grad_down, *first_came, *last_came)
        first_came.append(swap(sent_first, "y"))
        last_came.append(swap(sent_last, "x"))

        def line_of(over_x, x_came, over_y, y_came):
            return jnp.concatenate(
                [summed(over_x, x_came, by_x), summed(over_y, y_came, by_y)], axis=-1
            )

        def line_to_send(over_x, x_came, x_last, over_y, y_came, y_last):
            line = line_of(over_x, (x_came, x_last), over_y, (y_came, y_last))
            return line, away(line, "z0", 2)

        g_ff, sent = step(line_to_send, grad_gate, *gate_came, grad_up, *up_came)
        ff_came = [swap(sent, "z0")]

        def da_of(qk_full, v_full, dqk, dv, x):
            da = dot32(dqk, qk_full, NT) + dot32(dv, v_full, NT)
            x = wide(x)
            gain = jnp.sum(da * x * r_of(x), axis=0)
            return da, away(da.reshape(ctx_size, 2, span, model), "core", 1), gain

        da, sent, gain_one_grad = step(da_of, qk_full, v_full, dqk, dv, x)
        da_came = swap(sent, "core")
        grad_qk, sent = step(grad_and_send(by_x), normed, dqk)
        home_came.append(swap(step(sent_next(home_steps, 2), home, *home_came), "core"))
        qk_came = [swap(sent, "x")]

        def input_side(x_half, da, came, gain_one, dh1_half):
            da_half = own_half(da) + came
            du1 = norm_back(wide(x_half), gain_one, da_half)
            du = low(dh1_half + du1).reshape(2, 2, span, model)
            return du, away(du, "z0", 1)

        inward, sent = step(input_side, x_half, da, da_came, gain_one, dh1_half)
        inward_came = [swap(sent, "z0")]

        def vo_grads(normed, dv, ob, db, gain_one, gain_two):
            db_cols = lax.dynamic_slice_in_dim(db, core * half_width, half_width, axis=1)
            gains = jnp.pad(jnp.stack([gain_one, gain_two], axis=1), ((0, 0), (0, 126)))
            g = [low(dot32(normed, dv, TN)), low(dot32(ob, db_cols, TN)), low(gains)]
            g = rows_view(jnp.concatenate(g, axis=1))
            return g, away(g, "y", 0)

        grad_vo, sent = step(vo_grads, normed, dv, ob, db, gain_one_grad, gain_two_grad)
        vo_came = [swap(sent, "y")]

        def down_line_of(g, x_came, x_last, y_came, y_last):
            parts = [
                summed(g[..., :model_half], (x_came, x_last), down_by_x),
                summed(g[..., model_half:], (y_came, y_last), down_by_y),
            ]
            line = jnp.concatenate(parts, axis=-1)
            return line, away(line, "z0", 1)

        g_down, sent = step(down_line_of, grad_down, *first_came, *last_came)
        down_came = [swap(sent, "z0")]
        ff_came.append(swap(step(to_send(by_x[2:], 1), g_ff, *ff_came), "z1"))
        output = step(
            lambda v, *came: traded(v, came, home_steps).reshape(seqs, local_len, model),
            home, *home_came,
        )
        inward_came.append(swap(step(sent_next(home_steps, 1), inward, *inward_came), "z1"))
        down_came.append(swap(step(to_send(down_by_x[2:], 1), g_down, *down_came), "z1"))
        sent_qk, sent_vo = step(second, grad_qk, *qk_came, grad_vo, *vo_came)
        qk_came.append(swap(sent_qk, "y"))
        vo_came.append(swap(sent_vo, "x"))

        def own_rows_of(v, z0_came, z1_came):
            v = summed(v, (z0_came,), by_x[2:])
            v = wide(mine(v, "z1", 1)) + wide(z1_came)
            return v, away(v, "core", 0)

        g_ff, sent = step(own_rows_of, g_ff, *ff_came)
        ff_came = swap(sent, "core")
        g_attn, sent = step(line_to_send, grad_qk, *qk_came, grad_vo, *vo_came)
        attn_came = [swap(sent, "z0")]
        grad_down = step(
            lambda v, z0_came, z1_came: wide(mine(summed(v, (z0_came,), down_by_x[2:]), "z1", 0))
            + wide(z1_came),
            g_down, *down_came,
        )
        inward_came.append(swap(step(sent_next(home_steps, 2), inward, *inward_came), "core"))

        def columns(own, other, first, size):
            own, other = own[:, first : first + size], other[:, first : first + size]
            return [jnp.where(core == 0, own, other), jnp.where(core == 0, other, own)]

        def ff_rows_home(own, other):
            def whole_rows(first):
                parts = []
                for block in range(n_blocks):
                    parts += columns(own, other, first + block * ff_block, ff_block)
                return jnp.concatenate(parts, axis=1)

            return whole_rows(0), whole_rows(ff_half)

        grad_gate, grad_up = step(lambda v, w: ff_rows_home(mine(v, "core", 0), w), g_ff, ff_came)
        attn_came.append(swap(step(to_send(by_x[2:], 1), g_attn, *attn_came), "z1"))
        input_grad = step(
            lambda v, *came: wide(traded(v, came, home_steps)).reshape(seqs, local_len, model),
            inward, *inward_came,
        )
        g_attn, sent = step(own_rows_of, g_attn, *attn_came)
        attn_came = swap(sent, "core")

        def attn_rows_home(own, other):
            def whole_rows(starts, size):
                first, last = zip(*(columns(own, other, at, size) for at in starts))
                return jnp.concatenate(first + last, axis=1)

            query = whole_rows(range(0, 256 * pairs, 256), 128)
            key = whole_rows(range(128, 256 * pairs, 256), 128)
            at = 2 * half_width
            value = whole_rows([at], half_width)
            out = whole_rows([at + half_width], half_width)
            at += 2 * half_width
            gains = (own + other)[:, at : at + 2]
            return query, key, value, out, gains[:, 0], gains[:, 1]

        home_rows = step(lambda v, w: attn_rows_home(mine(v, "core", 0), w), g_attn, attn_came)
        return (output, input_grad) + home_rows[:4] + (grad_gate, grad_up, grad_down) + home_rows[4:]

    return on_device


def solution(mesh):
    in_specs = (
        P("seq", "ctx", None),
        P("seq", None),
        P("seq", "ctx"),
        P(("seq", "ctx"), None),
        P(("seq", "ctx"), None),
        P(("seq", "ctx"), None),
        P(("seq", "ctx"), None),
        P(("seq", "ctx"), None),
        P(("seq", "ctx"), None),
        P(("seq", "ctx"), None),
        P(("seq", "ctx")),
        P(("seq", "ctx")),
        P("seq", "ctx", None),
    )
    out_specs = (
        P("seq", "ctx", None),
        P("seq", "ctx", None),
        P(("seq", "ctx"), None),
        P(("seq", "ctx"), None),
        P(("seq", "ctx"), None),
        P(("seq", "ctx"), None),
        P(("seq", "ctx"), None),
        P(("seq", "ctx"), None),
        P(("seq", "ctx"), None),
        P(("seq", "ctx")),
        P(("seq", "ctx")),
    )
    seq_size, ctx_size = mesh.shape["seq"], mesh.shape["ctx"]
    one_each = sequence_per_chip(seq_size, ctx_size)

    def program(tokens, *others):
        if (seq_size, ctx_size, tokens.shape[0]) == (8, 4, 2):
            return one_each(tokens, *others)
        return on_device(tokens, *others)

    return jax.shard_map(
        program, mesh=mesh, in_specs=in_specs, out_specs=out_specs, check_vma=False
    )
```

```python
import functools

import jax
import jax.numpy as jnp
from jax import lax
from jax.experimental import pallas as pl
from jax.experimental.pallas import tpu as pltpu
from jax.sharding import PartitionSpec as P

HEADS = 12
KV_HEADS = 12
HEAD_DIM = 64
VMEM = 56 << 20


epsilon = 1e-05


def shortened(value):
    return jax.tree.map(lambda a: a.astype(jnp.bfloat16) if a.dtype == jnp.float32 else a, value)


def rms_scale(values_in, gain_in):
    return (
        values_in
        * lax.rsqrt(jnp.mean(values_in * values_in, axis=-1, keepdims=True) + epsilon)
        * gain_in
    )


def angle_tables(position_ids, head_size):
    half_dim = head_size // 2
    frequency = 10000.0 ** (-(jnp.arange(half_dim, dtype=jnp.float32) * 2.0 / head_size))
    angles = position_ids.astype(jnp.float32)[:, None] * frequency[None, :]
    angles = jnp.concatenate([angles, angles], axis=-1)
    return (jnp.cos(angles), jnp.sin(angles))


def rotate(values_in, cosine, sine_table):
    half_dim = values_in.shape[-1] // 2
    turned = jnp.concatenate([-values_in[..., half_dim:], values_in[..., :half_dim]], axis=-1)
    return values_in * cosine[:, None, :] + turned * sine_table[:, None, :]


def unrotate(grad_in, cosine, sine_table):
    half_dim = grad_in.shape[-1] // 2
    scaled = grad_in * sine_table[:, None, :]
    turned = jnp.concatenate([scaled[..., half_dim:], -scaled[..., :half_dim]], axis=-1)
    return grad_in * cosine[:, None, :] + turned


def gather_flat(weight_set):
    return jax.tree.map(
        lambda part, own: part.astype(own.dtype),
        lax.all_gather(shortened(weight_set), ("seq", "ctx"), axis=0, tiled=True),
        weight_set,
    )


def fetch_weights(weight_set):
    return (gather_flat(weight_set), weight_set)


def fetch_again(kept_set):
    return gather_flat(kept_set)


def reduce_grads(grad_set):
    return lax.psum_scatter(grad_set, ("seq", "ctx"), scatter_dimension=0, tiled=True)


def on_device(
    tokens,
    segments,
    positions,
    w_query,
    w_key,
    w_value,
    w_out,
    w_gate,
    w_up,
    w_down,
    gain_attn,
    gain_mlp,
    cotangent,
):
    seq_count, local_len, model_width = tokens.shape
    seq_len = segments.shape[1]
    row_count = seq_count * local_len
    head_group = HEADS // KV_HEADS
    kv_width = KV_HEADS * HEAD_DIM
    score_scale = HEAD_DIM ** (-0.5)
    first_token = lax.axis_index("ctx") * local_len
    own_tokens = first_token + jnp.arange(local_len, dtype=jnp.int32)
    all_tokens = jnp.arange(seq_len, dtype=jnp.int32)
    causal = all_tokens[None, :] <= own_tokens[:, None]
    inputs = tokens.reshape(row_count, model_width).astype(jnp.float32)
    cosine, sine_table = angle_tables(positions.reshape(row_count), HEAD_DIM)
    attn_full, attn_kept = fetch_weights((w_query, w_key, w_value, w_out, gain_attn))
    full_query, full_key, full_value, full_out, full_gain_one = attn_full
    normed = rms_scale(inputs, full_gain_one.astype(jnp.float32)).astype(jnp.bfloat16)
    query_proj = jnp.dot(normed, full_query, preferred_element_type=jnp.float32)
    key_proj = jnp.dot(normed, full_key, preferred_element_type=jnp.float32)
    value_proj = jnp.dot(normed, full_value, preferred_element_type=jnp.float32)
    query_rot = rotate(query_proj.reshape(row_count, HEADS, HEAD_DIM), cosine, sine_table).astype(
        jnp.bfloat16
    )
    key_rot = rotate(key_proj.reshape(row_count, KV_HEADS, HEAD_DIM), cosine, sine_table).astype(
        jnp.bfloat16
    )
    value_low = value_proj.astype(jnp.bfloat16)
    keys_all, values_all = (
        lax.all_gather(key_rot.reshape(seq_count, local_len, kv_width), "ctx", axis=1, tiled=True),
        lax.all_gather(
            value_low.reshape(seq_count, local_len, kv_width), "ctx", axis=1, tiled=True
        ),
    )
    queries = query_rot.reshape(seq_count, local_len, KV_HEADS, head_group, HEAD_DIM)

    def scores_of(q_seq, k_seq, seg_seq):
        own_seg = lax.dynamic_slice_in_dim(seg_seq, first_token, local_len)
        allowed = causal & (own_seg[:, None] == seg_seq[None, :])
        k_heads = k_seq.reshape(seq_len, KV_HEADS, HEAD_DIM)
        raw_scores = jnp.einsum(
            "qkgd,skd->kgqs", q_seq, k_heads, preferred_element_type=jnp.float32
        )
        return jnp.where(allowed[None, None], raw_scores * score_scale, -1e30)

    def attend(pieces):
        q_seq, k_seq, v_seq, seg_seq = pieces
        logits = scores_of(q_seq, k_seq, seg_seq)
        row_max = jnp.max(logits, axis=-1, keepdims=True)
        shifted_exp = jnp.exp(logits - row_max)
        row_sum = jnp.sum(shifted_exp, axis=-1, keepdims=True)
        probs_low = (shifted_exp / row_sum).astype(jnp.bfloat16)
        mixed_heads = jnp.einsum(
            "kgqs,skd->qkgd",
            probs_low,
            v_seq.reshape(seq_len, KV_HEADS, HEAD_DIM),
            preferred_element_type=jnp.float32,
        )
        return (
            mixed_heads.astype(jnp.bfloat16).reshape(local_len, model_width),
            (row_max + jnp.log(row_sum))[..., 0],
        )

    attended, log_totals = lax.map(attend, (queries, keys_all, values_all, segments))
    attended = attended.reshape(row_count, model_width)
    hidden_state = inputs + jnp.dot(attended, full_out, preferred_element_type=jnp.float32)
    mlp_full, mlp_kept = fetch_weights((w_gate, w_up, w_down, gain_mlp))
    full_gate, full_up, full_down, full_gain_two = mlp_full
    normed_two = rms_scale(hidden_state, full_gain_two.astype(jnp.float32)).astype(jnp.bfloat16)
    gate_proj = jnp.dot(normed_two, full_gate, preferred_element_type=jnp.float32)
    up_proj = jnp.dot(normed_two, full_up, preferred_element_type=jnp.float32)
    activated = (jax.nn.silu(gate_proj) * up_proj).astype(jnp.bfloat16)
    final_state = hidden_state + jnp.dot(activated, full_down, preferred_element_type=jnp.float32)
    output = final_state.astype(jnp.bfloat16).reshape(seq_count, local_len, model_width)
    out_grad = cotangent.reshape(row_count, model_width)
    again_gate, again_up, again_down, again_gain_two = fetch_again(mlp_kept)
    grad_down = jnp.einsum("tf,td->fd", activated, out_grad, preferred_element_type=jnp.float32)
    d_activated = jnp.einsum("td,fd->tf", out_grad, again_down, preferred_element_type=jnp.float32)

    def swiglu(gate_in, up_in):
        return jax.nn.silu(gate_in) * up_in

    unused_mlp, swiglu_back = jax.vjp(swiglu, gate_proj, up_proj)
    d_gate, d_up = swiglu_back(d_activated)
    d_gate = d_gate.astype(jnp.bfloat16)
    d_up = d_up.astype(jnp.bfloat16)
    grad_gate = jnp.einsum("td,tf->df", normed_two, d_gate, preferred_element_type=jnp.float32)
    grad_up = jnp.einsum("td,tf->df", normed_two, d_up, preferred_element_type=jnp.float32)
    d_normed_two = jnp.einsum(
        "tf,df->td", d_gate, again_gate, preferred_element_type=jnp.float32
    ) + jnp.einsum("tf,df->td", d_up, again_up, preferred_element_type=jnp.float32)
    unused_norm, norm_two_back = jax.vjp(
        rms_scale, hidden_state, again_gain_two.astype(jnp.float32)
    )
    d_hidden, grad_gain_mlp = norm_two_back(d_normed_two)
    mlp_sums = reduce_grads((grad_gate, grad_up, grad_down, grad_gain_mlp))
    d_hidden = d_hidden + out_grad.astype(jnp.float32)
    d_branch = d_hidden.astype(jnp.bfloat16)
    again_query, again_key, again_value, again_out, again_gain_one = fetch_again(attn_kept)
    grad_out = jnp.einsum("td,te->de", attended, d_branch, preferred_element_type=jnp.float32)
    d_attended = jnp.einsum(
        "te,de->td", d_branch, again_out, preferred_element_type=jnp.float32
    ).astype(jnp.bfloat16)
    d_heads = d_attended.reshape(seq_count, local_len, KV_HEADS, head_group, HEAD_DIM)

    def attend_back(pieces):
        q_seq, k_seq, v_seq, seg_seq, lse_seq, do_seq = pieces
        logits = scores_of(q_seq, k_seq, seg_seq)
        probs = jnp.exp(logits - lse_seq[..., None])
        probs_low = probs.astype(jnp.bfloat16)
        v_heads = v_seq.reshape(seq_len, KV_HEADS, HEAD_DIM)
        d_probs = jnp.einsum("qkgd,skd->kgqs", do_seq, v_heads, preferred_element_type=jnp.float32)
        d_value = jnp.einsum(
            "kgqs,qkgd->skd", probs_low, do_seq, preferred_element_type=jnp.float32
        )
        row_dot = jnp.sum(probs * d_probs, axis=-1, keepdims=True)
        d_scores = (probs * (d_probs - row_dot) * score_scale).astype(jnp.bfloat16)
        d_query = jnp.einsum(
            "kgqs,skd->qkgd",
            d_scores,
            k_seq.reshape(seq_len, KV_HEADS, HEAD_DIM),
            preferred_element_type=jnp.float32,
        )
        d_key = jnp.einsum("kgqs,qkgd->skd", d_scores, q_seq, preferred_element_type=jnp.float32)
        return (
            d_query.reshape(local_len, HEADS, HEAD_DIM),
            d_key.reshape(seq_len, kv_width),
            d_value.reshape(seq_len, kv_width),
        )

    d_query_all, d_key_part, d_value_part = lax.map(
        attend_back, (queries, keys_all, values_all, segments, log_totals, d_heads)
    )
    d_key_own, d_value_own = (
        lax.psum_scatter(d_key_part, "ctx", scatter_dimension=1, tiled=True),
        lax.psum_scatter(d_value_part, "ctx", scatter_dimension=1, tiled=True),
    )
    d_query_low = (
        unrotate(d_query_all.reshape(row_count, HEADS, HEAD_DIM), cosine, sine_table)
        .astype(jnp.bfloat16)
        .reshape(row_count, model_width)
    )
    d_key_low = (
        unrotate(d_key_own.reshape(row_count, KV_HEADS, HEAD_DIM), cosine, sine_table)
        .astype(jnp.bfloat16)
        .reshape(row_count, kv_width)
    )
    d_value_low = d_value_own.reshape(row_count, kv_width).astype(jnp.bfloat16)
    grad_query = jnp.einsum("td,te->de", normed, d_query_low, preferred_element_type=jnp.float32)
    grad_key = jnp.einsum("td,te->de", normed, d_key_low, preferred_element_type=jnp.float32)
    grad_value = jnp.einsum("td,te->de", normed, d_value_low, preferred_element_type=jnp.float32)
    d_normed = jnp.einsum("te,de->td", d_query_low, again_query, preferred_element_type=jnp.float32)
    d_normed = d_normed + jnp.einsum(
        "te,de->td", d_key_low, again_key, preferred_element_type=jnp.float32
    )
    d_normed = d_normed + jnp.einsum(
        "te,de->td", d_value_low, again_value, preferred_element_type=jnp.float32
    )
    unused_first, norm_one_back = jax.vjp(rms_scale, inputs, again_gain_one.astype(jnp.float32))
    d_inputs, grad_gain_attn = norm_one_back(d_normed)
    attn_sums = reduce_grads((grad_query, grad_key, grad_value, grad_out, grad_gain_attn))
    input_grad = (d_hidden + d_inputs).reshape(seq_count, local_len, model_width)
    return (
        output,
        input_grad,
        attn_sums[0],
        attn_sums[1],
        attn_sums[2],
        attn_sums[3],
        mlp_sums[0],
        mlp_sums[1],
        mlp_sums[2],
        attn_sums[4],
        mlp_sums[3],
    )


EPS = epsilon
NEG = -1e30


def dot32(left, right, dims=((1,), (0,))):
    return lax.dot_general(left, right, (dims, ((), ())), preferred_element_type=jnp.float32)


NT = ((1,), (1,))
TN = ((0,), (0,))


def lane_mask(rows):
    return lax.broadcasted_iota(jnp.int32, (rows, 128), 1) < HEAD_DIM


def swap_halves(u):
    half = HEAD_DIM // 2
    lanes = lax.broadcasted_iota(jnp.int32, u.shape, 1) % HEAD_DIM
    return jnp.where(lanes < half, pltpu.roll(u, 128 - half, 1), pltpu.roll(u, half, 1))


def allowed_pairs(seg_col, seg_row, first, rows, keys):
    q_ids = lax.broadcasted_iota(jnp.int32, (rows, keys), 0) + first
    k_ids = lax.broadcasted_iota(jnp.int32, (rows, keys), 1)
    return (k_ids <= q_ids) & (seg_col == seg_row)


def attend_kernel(block, qk_ref, v_ref, seg_col_ref, seg_row_ref, *refs):
    o_ref, lse_ref = refs[-2:]
    length = qk_ref.shape[0]
    first_head = lane_mask(block)
    for step in range(length // block):
        rows = slice(step * block, (step + 1) * block)
        keys = (step + 1) * block
        allowed = allowed_pairs(
            seg_col_ref[rows, :1], seg_row_ref[:, :keys], step * block, block, keys
        )
        q_pair = qk_ref[rows, :128]
        k_pair = qk_ref[:keys, 128:]
        v_pair = v_ref[:keys, :]
        outs, totals = [], []
        for head in range(2):
            mine = first_head if head == 0 else jnp.logical_not(first_head)
            q_head = jnp.where(mine, q_pair, jnp.zeros_like(q_pair))
            z = jnp.where(allowed, dot32(q_head, k_pair, NT), NEG)
            top = jnp.max(z, axis=-1, keepdims=True)
            e = jnp.exp(z - top)
            total = jnp.sum(e, axis=-1, keepdims=True)
            p = (e * (1.0 / total)).astype(jnp.bfloat16)
            outs.append(dot32(p, v_pair))
            totals.append(top + jnp.log(total))
        o_ref[rows, :] = jnp.where(first_head, outs[0], outs[1]).astype(o_ref.dtype)
        lse_ref[rows, :] = jnp.where(first_head, totals[0], totals[1])


def attend_back_kernel(
    block, qk_ref, v_ref, do_ref, lse_ref, cos_ref, sin_ref, seg_col_ref, seg_row_ref, *refs
):
    dqk_ref, dv_ref, dk_sum, dv_sum = refs[-4:]
    length = qk_ref.shape[0]
    first_head = lane_mask(block)
    for step in range(length // block):
        rows = slice(step * block, (step + 1) * block)
        keys = (step + 1) * block
        allowed = allowed_pairs(
            seg_col_ref[rows, :1], seg_row_ref[:, :keys], step * block, block, keys
        )
        q_pair = qk_ref[rows, :128]
        k_pair = qk_ref[:keys, 128:]
        v_pair = v_ref[:keys, :]
        do_pair = do_ref[rows, :]
        dq_heads = []
        dk_step = dv_step = None
        for head in range(2):
            mine = first_head if head == 0 else jnp.logical_not(first_head)
            q_head = jnp.where(mine, q_pair, jnp.zeros_like(q_pair))
            do_head = jnp.where(mine, do_pair, jnp.zeros_like(do_pair))
            lse = lse_ref[rows, head * HEAD_DIM : head * HEAD_DIM + 1]
            z = jnp.where(allowed, dot32(q_head, k_pair, NT), NEG)
            p = jnp.exp(z - lse)
            dp = dot32(do_head, v_pair, NT)
            dv_head = dot32(p.astype(jnp.bfloat16), do_head, TN)
            row_dot = jnp.sum(p * dp, axis=-1, keepdims=True)
            ds = (p * (dp - row_dot)).astype(jnp.bfloat16)
            dq_heads.append(dot32(ds, k_pair))
            dk_head = dot32(ds, q_head, TN)
            dk_step = dk_head if dk_step is None else dk_step + dk_head
            dv_step = dv_head if dv_step is None else dv_step + dv_head
        dq = jnp.where(first_head, dq_heads[0], dq_heads[1]) * (HEAD_DIM**-0.5)
        dq = dq * cos_ref[rows, :] - swap_halves(dq) * sin_ref[rows, :]
        dqk_ref[rows, :128] = dq.astype(dqk_ref.dtype)
        last = slice(step * block, keys)
        if step > 0:
            dk_sum[: step * block, :] += dk_step[: step * block]
            dv_sum[: step * block, :] += dv_step[: step * block]
        dk_sum[last, :] = dk_step[step * block :]
        dv_sum[last, :] = dv_step[step * block :]
    dk = dk_sum[...]
    dk = dk * cos_ref[...] - swap_halves(dk) * sin_ref[...]
    dqk_ref[:, 128:] = dk.astype(dqk_ref.dtype)
    dv_ref[...] = dv_sum[...].astype(dv_ref.dtype)


def qkv_kernel(x_ref, gain_ref, qk_w_ref, v_w_ref, cos_ref, sin_ref, a_ref, qk_ref, v_ref):
    x = x_ref[...].astype(jnp.float32)
    r = lax.rsqrt(jnp.mean(x * x, axis=-1, keepdims=True) + EPS)
    a = (x * r * gain_ref[...]).astype(jnp.bfloat16)
    a_ref[...] = a
    u = dot32(a, qk_w_ref[...])
    cos, sin = cos_ref[...], sin_ref[...]
    for at in range(0, u.shape[1], 256):
        q = u[:, at : at + 128]
        q = (q * cos + swap_halves(q) * sin) * (HEAD_DIM**-0.5)
        qk_ref[:, at : at + 128] = q.astype(jnp.bfloat16)
        k = u[:, at + 128 : at + 256]
        k = k * cos + swap_halves(k) * sin
        qk_ref[:, at + 128 : at + 256] = k.astype(jnp.bfloat16)
    v_ref[...] = dot32(a, v_w_ref[...]).astype(jnp.bfloat16)


def whole(shape):
    return pl.BlockSpec(shape, lambda i: (0,) * len(shape))


def row_block(rows, width):
    return pl.BlockSpec((rows, width), lambda i: (i, 0))


def lane_block(length):
    return pl.BlockSpec((length, 128), lambda i: (0, i))


def project(x, gain, w_qk, w_v, cos, sin):
    length, model = x.shape
    width = w_v.shape[1]
    rows = 256
    low = lambda n: jax.ShapeDtypeStruct((length, n), jnp.bfloat16)
    return pl.pallas_call(
        qkv_kernel,
        grid=(length // rows,),
        in_specs=[
            row_block(rows, model), whole((1, model)), whole(w_qk.shape), whole(w_v.shape),
            row_block(rows, 128), row_block(rows, 128),
        ],
        out_specs=[row_block(rows, model), row_block(rows, 2 * width), row_block(rows, width)],
        out_shape=[low(model), low(2 * width), low(width)],
        compiler_params=pltpu.CompilerParams(vmem_limit_bytes=VMEM),
        cost_estimate=pl.CostEstimate(flops=1, bytes_accessed=1, transcendentals=0),
        name="project",
    )(x, gain, w_qk, w_v, cos, sin)


def over_pairs(kernel, name, some, arrays, shared, outs, scratch, into=()):
    length = arrays[0].shape[0]
    pairs = arrays[1].shape[1] // 128
    first, last = some
    of_pair = lambda width: pl.BlockSpec((length, width), lambda i: (0, first + i))
    inputs = tuple(arrays) + tuple(shared)
    return pl.pallas_call(
        functools.partial(kernel, 256),
        grid=(last - first,),
        in_specs=[of_pair(a.shape[1] // pairs) for a in arrays]
        + [whole(a.shape) for a in shared]
        + [pl.BlockSpec(memory_space=pl.ANY)] * len(into),
        out_specs=[of_pair(width) for width, _ in outs],
        out_shape=[jax.ShapeDtypeStruct((length, pairs * width), kind) for width, kind in outs],
        scratch_shapes=scratch,
        input_output_aliases={len(inputs) + i: i for i in range(len(into))},
        compiler_params=pltpu.CompilerParams(vmem_limit_bytes=VMEM),
        cost_estimate=pl.CostEstimate(flops=1, bytes_accessed=1, transcendentals=0),
        name=name,
    )(*inputs, *into)


def attend(some, qk, v, seg_col, seg_row, *into):
    return over_pairs(
        attend_kernel, "attend", some, (qk, v), (seg_col, seg_row),
        [(128, jnp.bfloat16), (128, jnp.float32)], [], into,
    )


def attend_back(some, arrays, into):
    length = arrays[0].shape[0]
    return over_pairs(
        attend_back_kernel, "attend_back", some, arrays[:4], arrays[4:],
        [(256, jnp.bfloat16), (128, jnp.bfloat16)],
        [pltpu.VMEM((length, 128), jnp.float32)] * 2, into,
    )


def cut_kernel(core_ref, wq, wk, wv, wo, wg, wu, wd, g1, g2, own, away, ff_own, ff_away, first, last):
    core = core_ref[0]
    rows, width = wq.shape
    half = width // 2
    eye = lax.broadcasted_iota(jnp.int32, (rows, rows), 0) == lax.broadcasted_iota(
        jnp.int32, (rows, rows), 1
    )

    def column(g):
        spread = jnp.where(eye, jnp.broadcast_to(g[...].astype(jnp.float32), (rows, rows)), 0.0)
        return jnp.sum(spread, axis=1, keepdims=True)

    lane = lax.broadcasted_iota(jnp.int32, (rows, 128), 1)
    gains = jnp.where(lane == 0, column(g1), jnp.where(lane == 1, column(g2), 0.0))
    for out, ff, side in ((own, ff_own, core), (away, ff_away, 1 - core)):
        for at in range(0, half, 128):
            for i, w in enumerate((wq, wk)):
                cols = pl.ds(pl.multiple_of(side * half + at, 128), 128)
                out[:, 2 * at + i * 128 : 2 * at + (i + 1) * 128] = w[:, cols]
        cols = pl.ds(pl.multiple_of(side * half, 128), half)
        out[:, width : width + half] = wv[:, cols]
        out[:, width + half : 2 * width] = wo[:, cols]
        out[:, 2 * width :] = gains.astype(jnp.bfloat16)
        n_blocks = ff.shape[1] // half
        for i in range(n_blocks):
            w = wg if i < n_blocks // 2 else wu
            block = 2 * (i % (n_blocks // 2)) + side
            ff[:, i * half : (i + 1) * half] = w[:, pl.ds(pl.multiple_of(block * half, 128), half)]
    first[...] = wd[:, : width // 2]
    last[...] = wd[:, width // 2 :]


def cut_shards(core, weights, gains):
    rows, width = weights[0].shape
    ff = weights[4].shape[1]
    down_rows = weights[6].shape[0]
    shape = lambda *dims: jax.ShapeDtypeStruct(dims, jnp.bfloat16)
    in_vmem = pl.BlockSpec(memory_space=pltpu.VMEM)
    return pl.pallas_call(
        cut_kernel,
        in_specs=[pl.BlockSpec(memory_space=pltpu.SMEM)] + [in_vmem] * 9,
        out_specs=[in_vmem] * 6,
        out_shape=[shape(rows, 2 * width + 128)] * 2
        + [shape(rows, ff)] * 2
        + [shape(down_rows, width // 2)] * 2,
        cost_estimate=pl.CostEstimate(flops=1, bytes_accessed=1, transcendentals=0),
        name="cut_shards",
    )(core.reshape(1).astype(jnp.int32), *weights, *(g[None, :] for g in gains))


def rounded_sum(*parts):
    total = parts[0]
    for part in parts[1:]:
        total = total + part
    return total


def ff_grads_kernel(bits, c, d_gate, d_up, hid, dy, x_out, x_keep, y_out, y_keep, ff, down):
    rows, cols = x_out.shape[-2:]
    n_wide = d_gate.shape[1] // cols
    n_down = x_out.shape[1] - 2 * n_wide
    away = pl.program_id(0) != bits[1]

    def cut_side(out, lead, side, first):
        for block in range(2):
            here = pl.ds(pl.multiple_of((side * 2 + block) * rows, rows), rows)
            for k in range(n_wide):
                slab = ff[here, k * cols : (k + 1) * cols]
                out[lead, block * n_wide + k] = slab.astype(jnp.bfloat16)
        for j in range(n_down):
            here = pl.ds(pl.multiple_of((side * n_down + j) * rows, rows), rows)
            out[lead, 2 * n_wide + j] = down[here, first : first + cols].astype(jnp.bfloat16)

    down[...] = dot32(hid[...], dy[...], TN)
    ff[...] = dot32(c[...], d_gate[...], TN)
    cut_side(x_out, 0, 1 - bits[0], 0)
    cut_side(x_keep, 0, bits[0], 0)
    ff[...] = dot32(c[...], d_up[...], TN)

    def by_y(out):
        for x in range(2):
            cut_side(out, x, x, cols)

    pl.when(away)(lambda: by_y(y_out))
    pl.when(jnp.logical_not(away))(lambda: by_y(y_keep))


def ff_grads(bits, c, d_gate, d_up, hid, dy, slabs):
    length, model = c.shape
    ff = d_gate.shape[1]
    half = lambda width: pl.BlockSpec((length, width // 2), lambda y, bits: (0, y))
    full = lambda a: pl.BlockSpec(a.shape, lambda y, bits: (0, 0), pipeline_mode=pl.Buffered(1))
    one = pl.BlockSpec((1,) + slabs, lambda y, bits: (y, 0, 0, 0))
    both = pl.BlockSpec((2,) + slabs, lambda y, bits: (0,) * 4)
    return pl.pallas_call(
        ff_grads_kernel,
        grid_spec=pltpu.PrefetchScalarGridSpec(
            num_scalar_prefetch=1,
            grid=(2,),
            in_specs=[half(model), full(d_gate), full(d_up), half(ff), full(dy)],
            out_specs=[one, one, both, both],
            scratch_shapes=[
                pltpu.VMEM((model // 2, ff), jnp.float32), pltpu.VMEM((ff // 2, model), jnp.float32)
            ],
        ),
        out_shape=[jax.ShapeDtypeStruct((2,) + slabs, jnp.bfloat16)] * 4,
        compiler_params=pltpu.CompilerParams(vmem_limit_bytes=VMEM),
        cost_estimate=pl.CostEstimate(flops=1, bytes_accessed=1, transcendentals=0),
        name="ff_grads",
    )(bits, c, d_gate, d_up, hid, dy)


def ff_second_kernel(bits, x_keep, x_came, y_keep, y_came, x_out, y_out):
    for p in range(x_out.shape[0]):
        x_out[p] = rounded_sum(x_keep[0, p], x_came[0, p])
        y_out[p] = rounded_sum(y_keep[0, p], y_came[0, p])


def ff_line_kernel(bits, x_keep, x_came, x_last, y_keep, y_came, y_last, kept, sent, slab):
    n_slabs, rows = x_last.shape[:2]
    shard = kept.shape[2]
    n_down = rows // shard
    n_ff = n_slabs - n_down
    for at, keep, came, last in ((0, x_keep, x_came, x_last), (n_slabs, y_keep, y_came, y_last)):
        for p in range(n_slabs):
            slab[...] = rounded_sum(keep[0, p], came[0, p], last[p]).astype(jnp.float32)
            for i in range(n_down):
                piece = slab[i * shard : (i + 1) * shard, :].astype(jnp.bfloat16)
                if p < n_ff:
                    z1, z0, to = i // 2, i % 2, at + p
                else:
                    z1, z0, to = (p - n_ff) // 2, (p - n_ff) % 2, at + n_ff + i

                def put(out, z1=z1, to=to, piece=piece):
                    out[z1, to] = piece

                pl.when(bits[2] == z0)(functools.partial(put, kept))
                pl.when(bits[2] != z0)(functools.partial(put, sent))


def ff_call(kernel, name, bits, inputs, outs, scratch=()):
    def spec(array, at):
        block = tuple(1 if i in at else n for i, n in enumerate(array.shape))
        return pl.BlockSpec(
            block,
            lambda i, bits: tuple(at[d](bits) if d in at else 0 for d in range(array.ndim)),
        )

    return pl.pallas_call(
        kernel,
        grid_spec=pltpu.PrefetchScalarGridSpec(
            num_scalar_prefetch=1,
            grid=(1,),
            in_specs=[spec(*pair) for pair in inputs],
            out_specs=[pl.BlockSpec(o, lambda i, bits, n=len(o): (0,) * n) for o in outs],
            scratch_shapes=scratch,
        ),
        out_shape=[jax.ShapeDtypeStruct(o, jnp.bfloat16) for o in outs],
        compiler_params=pltpu.CompilerParams(vmem_limit_bytes=VMEM),
        cost_estimate=pl.CostEstimate(flops=1, bytes_accessed=1, transcendentals=0),
        name=name,
    )(bits, *[array for array, _ in inputs])


def by_bit(own, other, bit, axis):
    own, other = jnp.expand_dims(own, axis), jnp.expand_dims(other, axis)
    shape = [1] * own.ndim
    shape[axis] = 2
    return jnp.where(lax.broadcasted_iota(jnp.int32, shape, axis) == bit, own, other)


def pick(v, at, axis):
    return lax.dynamic_index_in_dim(v, at, axis, keepdims=False)


def pick_static(v, at, axis):
    return lax.index_in_dim(v, at, axis, keepdims=False)


class Cube:
    def __init__(self, seq_size, ctx_size):
        self.sizes = {"seq": seq_size, "ctx": ctx_size}
        self.steps = {"core": ("seq", 1), "x": ("seq", 2), "y": ("seq", 4), "z0": ("ctx", 1), "z1": ("ctx", 2)}
        self.bits = {
            name: (lax.axis_index(axis) // step) % 2 for name, (axis, step) in self.steps.items()
        }
        self.last = ()

    def step(self, work, *arrays):
        if self.last:
            arrays = lax.optimization_barrier((arrays, self.last))[0]
        result = work(*arrays)
        self.last = tuple(jax.tree.leaves(result))
        return result

    def settle(self):
        names = tuple(self.bits)
        values = self.hold(*self.bits.values())
        self.bits = dict(zip(names, values))

    def hold(self, *arrays):
        return lax.optimization_barrier((arrays, self.last))[0]

    def swap(self, v, name):
        axis, step = self.steps[name]
        return lax.ppermute(v, axis, [(i, i ^ step) for i in range(self.sizes[axis])])

    def mine(self, v, name, axis):
        return pick(v, self.bits[name], axis)

    def away(self, v, name, axis):
        return pick(v, 1 - self.bits[name], axis)

    def joined(self, own, other, name, axis):
        return lax.optimization_barrier(by_bit(own, other, self.bits[name], axis))

    def traded(self, v, came, steps):
        for other, (name, axis, at) in zip(came, steps):
            v = by_bit(self.mine(v, name, axis), other, self.bits[name], at)
        return v

    def summed(self, v, came, steps):
        for other, (name, axis) in zip(came, steps):
            v = low(wide(self.mine(v, name, axis)) + wide(other))
        return v

def low(v):
    return v.astype(jnp.bfloat16)


def wide(v):
    return v.astype(jnp.float32)


def rows_of(v):
    return v.reshape(-1, v.shape[-1])


def r_of(u):
    return lax.rsqrt(jnp.mean(u * u, axis=-1, keepdims=True) + EPS)


def norm_back(u, gain, dn):
    r = r_of(u)
    gd = gain * dn
    return r * gd - u * (r * r * r) * jnp.mean(gd * u, axis=-1, keepdims=True)


def sequence_per_chip(seq_size, ctx_size):
    def on_device(
        tokens, segments, positions,
        w_query, w_key, w_value, w_out, w_gate, w_up, w_down,
        gain_attn, gain_mlp, cotangent,
    ):
        cube = Cube(seq_size, ctx_size)
        step, swap, hold, mine, away = cube.step, cube.swap, cube.hold, cube.mine, cube.away
        joined, traded, summed = cube.joined, cube.traded, cube.summed
        bits = cube.bits
        core = cube.bits["core"]
        seqs, local_len, model = tokens.shape
        seq_len = segments.shape[1]
        span = local_len // 2
        own_rows = w_query.shape[0]
        half_width = w_query.shape[1] // 2
        ff_rows = w_down.shape[0]
        ff_half = w_gate.shape[1] // 2
        n_blocks = seq_size // 2
        ff_block = ff_half // n_blocks
        model_half = model // 2
        pairs = half_width // 128

        attn_own, attn_away, ff_own, ff_away, first, last = step(
            lambda *w: tuple(cut_shards(core, w[:7], w[7:])),
            w_query, w_key, w_value, w_out, w_gate, w_up, w_down, gain_attn, gain_mlp,
        )
        attn_came = swap(attn_away, "core")

        def pack_tokens(tokens, positions, segments):
            own_first = lax.axis_index("ctx") * local_len
            own_segments = lax.dynamic_slice_in_dim(segments, own_first, local_len, axis=1)
            numbers = low(jnp.stack([positions // 32, positions % 32, own_segments]))
            numbers = numbers.reshape(3, seqs, 2, span).transpose(1, 2, 0, 3)
            numbers = numbers.reshape(seqs, 2, 1, 3 * span)
            numbers = jnp.pad(numbers, ((0, 0), (0, 0), (0, 15), (0, model - 3 * span)))
            pack = jnp.concatenate([tokens.reshape(seqs, 2, span, model), numbers], axis=2)
            return pack, away(pack, "core", 1)

        to_chip = (("core", 1, 0), ("z0", 1, 1), ("z1", 0, 0))

        def sent_next(steps, n):
            name, axis = steps[n][:2]
            return lambda v, *came: away(traded(v, came, steps), name, axis)

        x_pack, sent = step(pack_tokens, tokens, positions, segments)
        x_came = [swap(sent, "core")]

        attn_piece = step(lambda v, w: joined(v, w, "core", 0), attn_own, attn_came)
        attn_came = swap(attn_piece, "z1")

        x_came.append(swap(step(sent_next(to_chip, 1), x_pack, *x_came), "z0"))

        cube.settle()
        bits = cube.bits

        ff_came = swap(*hold(ff_away), "core")
        ff_piece = step(lambda v, w: joined(v, w, "core", 0), ff_own, ff_came)

        attn_half_line = step(lambda v, w: joined(v, w, "z1", 1), attn_piece, attn_came)
        attn_came = swap(attn_half_line, "z0")

        first_came, last_came = swap(*hold(first), "x"), swap(*hold(last), "y")

        ff_came = swap(*hold(ff_piece), "z1")

        x_came.append(swap(step(sent_next(to_chip, 2), x_pack, *x_came), "z1"))

        down_pair = step(
            lambda a, b, c, d: jnp.concatenate(
                [joined(a, b, "x", 0), joined(c, d, "y", 0)], axis=2
            ),
            first, first_came, last, last_came,
        )

        def attn_to_line(v, came):
            line = joined(v, came, "z0", 2)
            return line[..., : 2 * half_width], line[..., 2 * half_width :]

        qk_line, vo_line = step(attn_to_line, attn_half_line, attn_came)
        qk_came, vo_came = swap(qk_line, "x"), swap(vo_line, "y")

        dy_pack = cotangent.reshape(seqs, 2, span, model)
        dy_came = [swap(step(sent_next(to_chip, 0), dy_pack), "core")]

        ff_half_line = step(lambda v, w: joined(v, w, "z1", 1), ff_piece, ff_came)
        ff_came = swap(ff_half_line, "z0")

        qk_plane = step(lambda v, w: joined(v, w, "x", 0), qk_line, qk_came)
        qk_came = swap(qk_plane, "y")
        vo_plane = step(lambda v, w: joined(v, w, "y", 0), vo_line, vo_came)
        vo_came = swap(vo_plane, "x")

        x_half = step(
            lambda v, *came: traded(v, came, to_chip).reshape(ctx_size, -1, model), x_pack, *x_came
        )
        x_other = swap(x_half, "core")

        down_came = swap(*hold(down_pair), "z1")

        def attn_to_full(qk, qk_came, vo, vo_came):
            qk = rows_of(joined(qk, qk_came, "y", 0))
            vo = rows_of(joined(vo, vo_came, "x", 1))
            gains = wide(vo[:, 2 * half_width : 2 * half_width + 2])
            return (
                qk, vo[:, :half_width], vo[:, half_width : 2 * half_width],
                gains[:, 0][None, :], gains[:, 1],
            )

        qk_full, v_full, out_half, gain_one, gain_two = step(
            attn_to_full, qk_plane, qk_came, vo_plane, vo_came
        )
        out_came = swap(out_half, "core")

        def ff_to_line(v, came):
            line = joined(v, came, "z0", 2)
            return line[..., :ff_half], line[..., ff_half:]

        gate_line, up_line = step(ff_to_line, ff_half_line, ff_came)

        gate_came, up_came = swap(gate_line, "x"), swap(up_line, "y")

        dy_came.append(swap(step(sent_next(to_chip, 1), dy_pack, *dy_came), "z0"))

        def unpack_tokens(x_half, x_other):
            x = joined(x_half[:, :span], x_other[:, :span], "core", 1).reshape(seq_len, model)
            numbers = joined(x_half[:, span, : 3 * span], x_other[:, span, : 3 * span], "core", 1)
            numbers = numbers.astype(jnp.int32).reshape(ctx_size, 2, 3, span)
            numbers = numbers.transpose(2, 0, 1, 3).reshape(3, seq_len)
            pos, seg = numbers[0] * 32 + numbers[1], numbers[2]
            lanes = jnp.arange(128, dtype=jnp.int32)
            half = HEAD_DIM // 2
            steps = (lanes % half).astype(jnp.float32) * 2.0 / HEAD_DIM
            angles = pos.astype(jnp.float32)[:, None] * (10000.0**-steps)[None, :]
            sign = jnp.where(lanes % HEAD_DIM < half, -1.0, 1.0)
            cos, sin = jnp.cos(angles), jnp.sin(angles) * sign
            seg_col = jnp.broadcast_to(seg[:, None], (seq_len, 128))
            return x, x_half[:, :span], seg_col, seg[None, :], cos, sin

        x, x_half, seg_col, seg_row, cos, sin = step(unpack_tokens, x_half, x_other)

        down_half_line = step(lambda v, w: joined(v, w, "z1", 1), down_pair, down_came)
        down_came = swap(down_half_line, "z0")

        def halves(own, other):
            whole = jnp.zeros((own.shape[0], 2 * own.shape[1]), own.dtype)
            whole = lax.dynamic_update_slice(whole, own, (0, core * own.shape[1]))
            return lax.dynamic_update_slice(whole, other, (0, (1 - core) * own.shape[1]))

        normed, qk, v = step(lambda *t: tuple(project(*t)), x, gain_one, qk_full, v_full, cos, sin)
        segs = (seg_col, seg_row)

        gate_plane = step(lambda v, w: joined(v, w, "x", 0), gate_line, gate_came)
        gate_came = swap(gate_plane, "y")
        up_plane = step(lambda v, w: joined(v, w, "y", 0), up_line, up_came)
        up_came = swap(up_plane, "x")

        dy_came.append(swap(step(sent_next(to_chip, 2), dy_pack, *dy_came), "z1"))


        ob_half, lse = step(lambda *t: tuple(attend((0, pairs), *t)), qk, v, *segs)
        ob_came = swap(ob_half, "core")

        def lay(into, own, bit, axis):
            return lax.dynamic_update_index_in_dim(into, own, bit, axis)

        def lay_own(gate, up):
            ff = jnp.zeros((2,) + gate.shape, gate.dtype)
            return lay(ff, gate, bits["y"], 0), lay(ff, up, bits["x"], 1)

        gate_part, up_part = step(lay_own, gate_plane, up_plane)

        out_full = step(halves, out_half, out_came)

        def down_to_line(v, came):
            line = joined(v, came, "z0", 2)
            return line[..., :model_half], line[..., model_half:]

        first_line, last_line = step(down_to_line, down_half_line, down_came)
        first_came, last_came = swap(first_line, "y"), swap(last_line, "x")

        dy_half = step(
            lambda v, *came: traded(v, came, to_chip).reshape(ctx_size, span, model),
            dy_pack, *dy_came,
        )
        dy_other = swap(dy_half, "core")

        gate_full, up_full = step(
            lambda a, b, c, d: (
                rows_of(lay(a, b, 1 - bits["y"], 0)), rows_of(lay(c, d, 1 - bits["x"], 1))
            ),
            gate_part, gate_came, up_part, up_came,
        )

        ob = step(halves, ob_half, ob_came)

        def own_half(t):
            return mine(t.reshape(ctx_size, 2, span, t.shape[-1]), "core", 1)

        def hidden(x, ob, out_full, gain_two):
            h1 = wide(x) + dot32(ob, out_full)
            return h1, low(h1 * r_of(h1) * gain_two)

        h1, normed_two = step(hidden, x, ob, out_full, gain_two)

        gate = step(dot32, normed_two, gate_full)

        dy = step(
            lambda a, b: joined(a, b, "core", 1).reshape(seq_len, model), dy_half, dy_other
        )

        def up_and_hidden(normed_two, up_full, gate):
            up = dot32(normed_two, up_full)
            s = jax.nn.sigmoid(gate)
            silu = gate * s
            return low(silu), low(up * s * (1.0 + gate * (1.0 - s))), low(silu * up)

        up_factor, gate_factor, hid = step(up_and_hidden, normed_two, up_full, gate)

        down_full = step(
            lambda a, b, c, d: rows_of(
                jnp.concatenate([joined(a, b, "y", 0), joined(c, d, "x", 1)], axis=-1)
            ),
            first_line, first_came, last_line, last_came,
        )

        def rows_view(g):
            return g.reshape(2, 2, 2, 2, 2, own_rows, g.shape[-1])

        def back(dy, down_full, gate_factor, up_factor):
            d_hid = dot32(dy, down_full, NT)
            return low(d_hid * wide(gate_factor)), low(d_hid * wide(up_factor))

        by_x = (("x", 1), ("y", 0), ("z0", 2), ("z1", 1), ("core", 0))
        by_y = (("y", 0), ("x", 0), ("z0", 2), ("z1", 1), ("core", 0))

        def to_send(steps, n):
            name, axis = steps[n]
            return lambda v, *came: away(summed(v, came, steps), name, axis)

        def grad_of(c, d):
            return rows_view(low(dot32(c, d, TN)))

        def grad_and_send(steps):
            def work(c, d):
                g = grad_of(c, d)
                return g, away(g, *steps[0])

            return work

        d_gate, d_up = step(back, dy, down_full, gate_factor, up_factor)
        n_wide = ff_half // ff_block
        n_down = ff_rows // own_rows
        n_pieces = 2 * n_wide + n_down
        slabs = (n_pieces, ctx_size * own_rows, ff_block)
        bit_array = jnp.stack([bits["x"], bits["y"], bits["z0"]]).astype(jnp.int32)
        x_mine, x_away = (lambda b: b[0]), (lambda b: 1 - b[0])
        y_mine, y_away = (lambda b: b[1]), (lambda b: 1 - b[1])
        sent_x, x_keep, sent_y, y_keep = step(
            lambda *t: tuple(ff_grads(bit_array, *t, slabs)), normed_two, d_gate, d_up, hid, dy
        )
        x_came, y_came = [swap(sent_x, "x")], [swap(sent_y, "y")]

        def dc_of(d_gate, gate_full, d_up, up_full):
            dc = dot32(d_gate, gate_full, NT) + dot32(d_up, up_full, NT)
            return dc, away(dc.reshape(ctx_size, 2, span, model), "core", 1)

        dc, sent = step(dc_of, d_gate, gate_full, d_up, up_full)
        dc_came = swap(sent, "core")

        def down_of(hid, down_full):
            down = dot32(hid, down_full).reshape(ctx_size, 2, span, model)
            return down, away(down, "core", 1)

        down, sent = step(down_of, hid, down_full)
        down_came = swap(sent, "core")

        def attn_side(dc, came, h1, dy_half, gain_two):
            dc_half = own_half(dc) + came
            dh1 = wide(dy_half) + norm_back(own_half(h1), gain_two, dc_half)
            return dh1, low(dh1), jnp.sum(dc * h1 * r_of(h1), axis=0)

        dh1_half, db_half, gain_two_grad = step(attn_side, dc, dc_came, h1, dy_half, gain_two)
        db_came = swap(db_half, "core")
        home_steps = (("z0", 1, 1), ("z1", 0, 0), ("core", 0, 1))

        def out_of(h1, down, came):
            out = low(own_half(h1) + mine(down, "core", 1) + came).reshape(2, 2, span, model)
            return out, away(out, "z0", 1)

        home, sent = step(out_of, h1, down, down_came)
        home_came = [swap(sent, "z0")]

        def d_attended_of(db_half, db_came, out_full):
            db = joined(db_half, db_came, "core", 1).reshape(seq_len, model)
            out_rows = lax.dynamic_slice_in_dim(out_full, core * half_width, half_width, axis=0)
            return db, low(dot32(db, out_rows, NT))

        db, d_attended = step(d_attended_of, db_half, db_came, out_full)

        backs = (qk, v, d_attended, lse, cos, sin, *segs)
        heads = step(lambda *t: tuple(attend_back((0, pairs - 1), t[:8], t[8:])), *backs)

        home_came.append(swap(step(sent_next(home_steps, 1), home, *home_came), "z1"))

        def second(over_x, x_came, over_y, y_came):
            return to_send(by_x, 1)(over_x, x_came), to_send(by_y, 1)(over_y, y_came)

        def ff_second(x_keep, x_came, y_keep, y_came):
            return tuple(
                ff_call(
                    ff_second_kernel, "ff_second", bit_array,
                    [(x_keep, {0: y_away}), (x_came, {0: y_away}),
                     (y_keep, {0: x_away}), (y_came, {0: x_away})],
                    [slabs] * 2,
                )
            )

        sent_x, sent_y = step(ff_second, x_keep, *x_came, y_keep, *y_came)
        x_came.append(swap(sent_x, "y"))
        y_came.append(swap(sent_y, "x"))

        dqk, dv = step(
            lambda *t: tuple(attend_back((pairs - 1, pairs), t[:8], t[8:])), *backs, *heads
        )

        home_came.append(swap(step(sent_next(home_steps, 2), home, *home_came), "core"))

        def da_of(qk_full, v_full, dqk, dv, x):
            da = dot32(dqk, qk_full, NT) + dot32(dv, v_full, NT)
            x = wide(x)
            gain = jnp.sum(da * x * r_of(x), axis=0)
            return da, away(da.reshape(ctx_size, 2, span, model), "core", 1), gain

        da, sent, gain_one_grad = step(da_of, qk_full, v_full, dqk, dv, x)
        da_came = swap(sent, "core")

        output = step(
            lambda v, *came: traded(v, came, home_steps).reshape(seqs, local_len, model),
            home, *home_came,
        )

        grad_qk, sent = step(grad_and_send(by_x), normed, dqk)
        qk_came = [swap(sent, "x")]

        def vo_grads(normed, dv, ob, db, gain_one, gain_two):
            db_cols = lax.dynamic_slice_in_dim(db, core * half_width, half_width, axis=1)
            gains = jnp.pad(jnp.stack([gain_one, gain_two], axis=1), ((0, 0), (0, 126)))
            g = [low(dot32(normed, dv, TN)), low(dot32(ob, db_cols, TN)), low(gains)]
            g = rows_view(jnp.concatenate(g, axis=1))
            return g, away(g, "y", 0)

        grad_vo, sent = step(vo_grads, normed, dv, ob, db, gain_one_grad, gain_two_grad)
        vo_came = [swap(sent, "y")]

        def input_side(x_half, da, came, gain_one, dh1_half):
            da_half = own_half(da) + came
            du1 = norm_back(wide(x_half), gain_one, da_half)
            du = low(dh1_half + du1).reshape(2, 2, span, model)
            return du, away(du, "z0", 1)

        inward, sent = step(input_side, x_half, da, da_came, gain_one, dh1_half)
        inward_came = [swap(sent, "z0")]

        def line_of(over_x, x_came, over_y, y_came):
            return jnp.concatenate(
                [summed(over_x, x_came, by_x), summed(over_y, y_came, by_y)], axis=-1
            )

        def line_to_send(over_x, x_came, x_last, over_y, y_came, y_last):
            line = line_of(over_x, (x_came, x_last), over_y, (y_came, y_last))
            return line, away(line, "z0", 2)

        def ff_line(x_keep, x_came, x_last, y_keep, y_came, y_last):
            return tuple(
                ff_call(
                    ff_line_kernel, "ff_line", bit_array,
                    [(x_keep, {0: y_mine}), (x_came, {0: y_mine}), (x_last, {}),
                     (y_keep, {0: x_mine}), (y_came, {0: x_mine}), (y_last, {})],
                    [(2, 2 * n_pieces, own_rows, ff_block)] * 2,
                    [pltpu.VMEM(slabs[1:], jnp.float32)],
                )
            )

        g_ff, sent = step(ff_line, x_keep, *x_came, y_keep, *y_came)
        ff_came = [swap(sent, "z0")]

        sent_qk, sent_vo = step(second, grad_qk, *qk_came, grad_vo, *vo_came)
        qk_came.append(swap(sent_qk, "y"))
        vo_came.append(swap(sent_vo, "x"))

        inward_came.append(swap(step(sent_next(home_steps, 1), inward, *inward_came), "z1"))

        g_attn, sent = step(line_to_send, grad_qk, *qk_came, grad_vo, *vo_came)
        attn_came = [swap(sent, "z0")]

        def ff_to_z1(v, came):
            return low(wide(away(v, "z1", 0)) + wide(away(came, "z1", 0)))

        ff_came.append(swap(step(ff_to_z1, g_ff, *ff_came), "z1"))

        inward_came.append(swap(step(sent_next(home_steps, 2), inward, *inward_came), "core"))

        attn_came.append(swap(step(to_send(by_x[2:], 1), g_attn, *attn_came), "z1"))

        input_grad = step(
            lambda v, *came: wide(traded(v, came, home_steps)).reshape(seqs, local_len, model),
            inward, *inward_came,
        )

        def own_rows_of(v, z0_came, z1_came):
            v = summed(v, (z0_came,), by_x[2:])
            v = wide(mine(v, "z1", 1)) + wide(z1_came)
            return v, away(v, "core", 0)

        def ff_rows_of(v, z0_came, z1_came):
            v = low(wide(mine(v, "z1", 0)) + wide(mine(z0_came, "z1", 0)))
            v = (wide(v) + wide(z1_came)).reshape(2, -1, own_rows, ff_block)
            ff = v[:, : 2 * n_wide].reshape(2, 2, n_wide, own_rows, ff_block)
            down = v[:, 2 * n_wide :].reshape(2, ff_rows, ff_block)
            return ff, away(ff, "core", 1), jnp.concatenate([down[0], down[1]], axis=1)

        g_ff, sent, grad_down = step(ff_rows_of, g_ff, *ff_came)
        ff_came = swap(sent, "core")

        def columns(own, other, first, size):
            own, other = own[:, first : first + size], other[:, first : first + size]
            return [jnp.where(core == 0, own, other), jnp.where(core == 0, other, own)]

        def ff_rows_home(ff, other):
            own = mine(ff, "core", 1)

            def whole_rows(i):
                parts = []
                for block in range(n_blocks):
                    parts += columns(own[i, block], other[i, block], 0, ff_block)
                return jnp.concatenate(parts, axis=1)

            return whole_rows(0), whole_rows(1)

        grad_gate, grad_up = step(ff_rows_home, g_ff, ff_came)

        g_attn, sent = step(own_rows_of, g_attn, *attn_came)
        attn_came = swap(sent, "core")
        def attn_rows_home(own, other):
            def whole_rows(starts, size):
                first, last = zip(*(columns(own, other, at, size) for at in starts))
                return jnp.concatenate(first + last, axis=1)

            query = whole_rows(range(0, 256 * pairs, 256), 128)
            key = whole_rows(range(128, 256 * pairs, 256), 128)
            at = 2 * half_width
            value = whole_rows([at], half_width)
            out = whole_rows([at + half_width], half_width)
            at += 2 * half_width
            gains = (own + other)[:, at : at + 2]
            return query, key, value, out, gains[:, 0], gains[:, 1]

        home_rows = step(lambda v, w: attn_rows_home(mine(v, "core", 0), w), g_attn, attn_came)
        return (output, input_grad) + home_rows[:4] + (grad_gate, grad_up, grad_down) + home_rows[4:]

    return on_device


def solution(mesh):
    in_specs = (
        P("seq", "ctx", None),
        P("seq", None),
        P("seq", "ctx"),
        P(("seq", "ctx"), None),
        P(("seq", "ctx"), None),
        P(("seq", "ctx"), None),
        P(("seq", "ctx"), None),
        P(("seq", "ctx"), None),
        P(("seq", "ctx"), None),
        P(("seq", "ctx"), None),
        P(("seq", "ctx")),
        P(("seq", "ctx")),
        P("seq", "ctx", None),
    )
    out_specs = (
        P("seq", "ctx", None),
        P("seq", "ctx", None),
        P(("seq", "ctx"), None),
        P(("seq", "ctx"), None),
        P(("seq", "ctx"), None),
        P(("seq", "ctx"), None),
        P(("seq", "ctx"), None),
        P(("seq", "ctx"), None),
        P(("seq", "ctx"), None),
        P(("seq", "ctx")),
        P(("seq", "ctx")),
    )
    seq_size, ctx_size = mesh.shape["seq"], mesh.shape["ctx"]
    one_each = sequence_per_chip(seq_size, ctx_size)

    def program(tokens, *others):
        if (seq_size, ctx_size, tokens.shape[0]) == (8, 4, 2):
            return one_each(tokens, *others)
        return on_device(tokens, *others)

    return jax.shard_map(
        program, mesh=mesh, in_specs=in_specs, out_specs=out_specs, check_vma=False
    )
```

```python
import functools

import jax
import jax.numpy as jnp
import numpy as np
from jax import lax
from jax.experimental import pallas as pl
from jax.experimental.pallas import tpu as pltpu
from jax.sharding import PartitionSpec as P

HEADS = 12
KV_HEADS = 12
HEAD_DIM = 64
VMEM = 56 << 20


epsilon = 1e-05


def shortened(value):
    return jax.tree.map(lambda a: a.astype(jnp.bfloat16) if a.dtype == jnp.float32 else a, value)


def rms_scale(values_in, gain_in):
    return (
        values_in
        * lax.rsqrt(jnp.mean(values_in * values_in, axis=-1, keepdims=True) + epsilon)
        * gain_in
    )


def angle_tables(position_ids, head_size):
    half_dim = head_size // 2
    frequency = 10000.0 ** (-(jnp.arange(half_dim, dtype=jnp.float32) * 2.0 / head_size))
    angles = position_ids.astype(jnp.float32)[:, None] * frequency[None, :]
    angles = jnp.concatenate([angles, angles], axis=-1)
    return (jnp.cos(angles), jnp.sin(angles))


def rotate(values_in, cosine, sine_table):
    half_dim = values_in.shape[-1] // 2
    turned = jnp.concatenate([-values_in[..., half_dim:], values_in[..., :half_dim]], axis=-1)
    return values_in * cosine[:, None, :] + turned * sine_table[:, None, :]


def unrotate(grad_in, cosine, sine_table):
    half_dim = grad_in.shape[-1] // 2
    scaled = grad_in * sine_table[:, None, :]
    turned = jnp.concatenate([scaled[..., half_dim:], -scaled[..., :half_dim]], axis=-1)
    return grad_in * cosine[:, None, :] + turned


def gather_flat(weight_set):
    return jax.tree.map(
        lambda part, own: part.astype(own.dtype),
        lax.all_gather(shortened(weight_set), ("seq", "ctx"), axis=0, tiled=True),
        weight_set,
    )


def fetch_weights(weight_set):
    return (gather_flat(weight_set), weight_set)


def fetch_again(kept_set):
    return gather_flat(kept_set)


def reduce_grads(grad_set):
    return lax.psum_scatter(grad_set, ("seq", "ctx"), scatter_dimension=0, tiled=True)


def on_device(
    tokens,
    segments,
    positions,
    w_query,
    w_key,
    w_value,
    w_out,
    w_gate,
    w_up,
    w_down,
    gain_attn,
    gain_mlp,
    cotangent,
):
    seq_count, local_len, model_width = tokens.shape
    seq_len = segments.shape[1]
    row_count = seq_count * local_len
    head_group = HEADS // KV_HEADS
    kv_width = KV_HEADS * HEAD_DIM
    score_scale = HEAD_DIM ** (-0.5)
    first_token = lax.axis_index("ctx") * local_len
    own_tokens = first_token + jnp.arange(local_len, dtype=jnp.int32)
    all_tokens = jnp.arange(seq_len, dtype=jnp.int32)
    causal = all_tokens[None, :] <= own_tokens[:, None]
    inputs = tokens.reshape(row_count, model_width).astype(jnp.float32)
    cosine, sine_table = angle_tables(positions.reshape(row_count), HEAD_DIM)
    attn_full, attn_kept = fetch_weights((w_query, w_key, w_value, w_out, gain_attn))
    full_query, full_key, full_value, full_out, full_gain_one = attn_full
    normed = rms_scale(inputs, full_gain_one.astype(jnp.float32)).astype(jnp.bfloat16)
    query_proj = jnp.dot(normed, full_query, preferred_element_type=jnp.float32)
    key_proj = jnp.dot(normed, full_key, preferred_element_type=jnp.float32)
    value_proj = jnp.dot(normed, full_value, preferred_element_type=jnp.float32)
    query_rot = rotate(query_proj.reshape(row_count, HEADS, HEAD_DIM), cosine, sine_table).astype(
        jnp.bfloat16
    )
    key_rot = rotate(key_proj.reshape(row_count, KV_HEADS, HEAD_DIM), cosine, sine_table).astype(
        jnp.bfloat16
    )
    value_low = value_proj.astype(jnp.bfloat16)
    keys_all, values_all = (
        lax.all_gather(key_rot.reshape(seq_count, local_len, kv_width), "ctx", axis=1, tiled=True),
        lax.all_gather(
            value_low.reshape(seq_count, local_len, kv_width), "ctx", axis=1, tiled=True
        ),
    )
    queries = query_rot.reshape(seq_count, local_len, KV_HEADS, head_group, HEAD_DIM)

    def scores_of(q_seq, k_seq, seg_seq):
        own_seg = lax.dynamic_slice_in_dim(seg_seq, first_token, local_len)
        allowed = causal & (own_seg[:, None] == seg_seq[None, :])
        k_heads = k_seq.reshape(seq_len, KV_HEADS, HEAD_DIM)
        raw_scores = jnp.einsum(
            "qkgd,skd->kgqs", q_seq, k_heads, preferred_element_type=jnp.float32
        )
        return jnp.where(allowed[None, None], raw_scores * score_scale, -1e30)

    def attend(pieces):
        q_seq, k_seq, v_seq, seg_seq = pieces
        logits = scores_of(q_seq, k_seq, seg_seq)
        row_max = jnp.max(logits, axis=-1, keepdims=True)
        shifted_exp = jnp.exp(logits - row_max)
        row_sum = jnp.sum(shifted_exp, axis=-1, keepdims=True)
        probs_low = (shifted_exp / row_sum).astype(jnp.bfloat16)
        mixed_heads = jnp.einsum(
            "kgqs,skd->qkgd",
            probs_low,
            v_seq.reshape(seq_len, KV_HEADS, HEAD_DIM),
            preferred_element_type=jnp.float32,
        )
        return (
            mixed_heads.astype(jnp.bfloat16).reshape(local_len, model_width),
            (row_max + jnp.log(row_sum))[..., 0],
        )

    attended, log_totals = lax.map(attend, (queries, keys_all, values_all, segments))
    attended = attended.reshape(row_count, model_width)
    hidden_state = inputs + jnp.dot(attended, full_out, preferred_element_type=jnp.float32)
    mlp_full, mlp_kept = fetch_weights((w_gate, w_up, w_down, gain_mlp))
    full_gate, full_up, full_down, full_gain_two = mlp_full
    normed_two = rms_scale(hidden_state, full_gain_two.astype(jnp.float32)).astype(jnp.bfloat16)
    gate_proj = jnp.dot(normed_two, full_gate, preferred_element_type=jnp.float32)
    up_proj = jnp.dot(normed_two, full_up, preferred_element_type=jnp.float32)
    activated = (jax.nn.silu(gate_proj) * up_proj).astype(jnp.bfloat16)
    final_state = hidden_state + jnp.dot(activated, full_down, preferred_element_type=jnp.float32)
    output = final_state.astype(jnp.bfloat16).reshape(seq_count, local_len, model_width)
    out_grad = cotangent.reshape(row_count, model_width)
    again_gate, again_up, again_down, again_gain_two = fetch_again(mlp_kept)
    grad_down = jnp.einsum("tf,td->fd", activated, out_grad, preferred_element_type=jnp.float32)
    d_activated = jnp.einsum("td,fd->tf", out_grad, again_down, preferred_element_type=jnp.float32)

    def swiglu(gate_in, up_in):
        return jax.nn.silu(gate_in) * up_in

    unused_mlp, swiglu_back = jax.vjp(swiglu, gate_proj, up_proj)
    d_gate, d_up = swiglu_back(d_activated)
    d_gate = d_gate.astype(jnp.bfloat16)
    d_up = d_up.astype(jnp.bfloat16)
    grad_gate = jnp.einsum("td,tf->df", normed_two, d_gate, preferred_element_type=jnp.float32)
    grad_up = jnp.einsum("td,tf->df", normed_two, d_up, preferred_element_type=jnp.float32)
    d_normed_two = jnp.einsum(
        "tf,df->td", d_gate, again_gate, preferred_element_type=jnp.float32
    ) + jnp.einsum("tf,df->td", d_up, again_up, preferred_element_type=jnp.float32)
    unused_norm, norm_two_back = jax.vjp(
        rms_scale, hidden_state, again_gain_two.astype(jnp.float32)
    )
    d_hidden, grad_gain_mlp = norm_two_back(d_normed_two)
    mlp_sums = reduce_grads((grad_gate, grad_up, grad_down, grad_gain_mlp))
    d_hidden = d_hidden + out_grad.astype(jnp.float32)
    d_branch = d_hidden.astype(jnp.bfloat16)
    again_query, again_key, again_value, again_out, again_gain_one = fetch_again(attn_kept)
    grad_out = jnp.einsum("td,te->de", attended, d_branch, preferred_element_type=jnp.float32)
    d_attended = jnp.einsum(
        "te,de->td", d_branch, again_out, preferred_element_type=jnp.float32
    ).astype(jnp.bfloat16)
    d_heads = d_attended.reshape(seq_count, local_len, KV_HEADS, head_group, HEAD_DIM)

    def attend_back(pieces):
        q_seq, k_seq, v_seq, seg_seq, lse_seq, do_seq = pieces
        logits = scores_of(q_seq, k_seq, seg_seq)
        probs = jnp.exp(logits - lse_seq[..., None])
        probs_low = probs.astype(jnp.bfloat16)
        v_heads = v_seq.reshape(seq_len, KV_HEADS, HEAD_DIM)
        d_probs = jnp.einsum("qkgd,skd->kgqs", do_seq, v_heads, preferred_element_type=jnp.float32)
        d_value = jnp.einsum(
            "kgqs,qkgd->skd", probs_low, do_seq, preferred_element_type=jnp.float32
        )
        row_dot = jnp.sum(probs * d_probs, axis=-1, keepdims=True)
        d_scores = (probs * (d_probs - row_dot) * score_scale).astype(jnp.bfloat16)
        d_query = jnp.einsum(
            "kgqs,skd->qkgd",
            d_scores,
            k_seq.reshape(seq_len, KV_HEADS, HEAD_DIM),
            preferred_element_type=jnp.float32,
        )
        d_key = jnp.einsum("kgqs,qkgd->skd", d_scores, q_seq, preferred_element_type=jnp.float32)
        return (
            d_query.reshape(local_len, HEADS, HEAD_DIM),
            d_key.reshape(seq_len, kv_width),
            d_value.reshape(seq_len, kv_width),
        )

    d_query_all, d_key_part, d_value_part = lax.map(
        attend_back, (queries, keys_all, values_all, segments, log_totals, d_heads)
    )
    d_key_own, d_value_own = (
        lax.psum_scatter(d_key_part, "ctx", scatter_dimension=1, tiled=True),
        lax.psum_scatter(d_value_part, "ctx", scatter_dimension=1, tiled=True),
    )
    d_query_low = (
        unrotate(d_query_all.reshape(row_count, HEADS, HEAD_DIM), cosine, sine_table)
        .astype(jnp.bfloat16)
        .reshape(row_count, model_width)
    )
    d_key_low = (
        unrotate(d_key_own.reshape(row_count, KV_HEADS, HEAD_DIM), cosine, sine_table)
        .astype(jnp.bfloat16)
        .reshape(row_count, kv_width)
    )
    d_value_low = d_value_own.reshape(row_count, kv_width).astype(jnp.bfloat16)
    grad_query = jnp.einsum("td,te->de", normed, d_query_low, preferred_element_type=jnp.float32)
    grad_key = jnp.einsum("td,te->de", normed, d_key_low, preferred_element_type=jnp.float32)
    grad_value = jnp.einsum("td,te->de", normed, d_value_low, preferred_element_type=jnp.float32)
    d_normed = jnp.einsum("te,de->td", d_query_low, again_query, preferred_element_type=jnp.float32)
    d_normed = d_normed + jnp.einsum(
        "te,de->td", d_key_low, again_key, preferred_element_type=jnp.float32
    )
    d_normed = d_normed + jnp.einsum(
        "te,de->td", d_value_low, again_value, preferred_element_type=jnp.float32
    )
    unused_first, norm_one_back = jax.vjp(rms_scale, inputs, again_gain_one.astype(jnp.float32))
    d_inputs, grad_gain_attn = norm_one_back(d_normed)
    attn_sums = reduce_grads((grad_query, grad_key, grad_value, grad_out, grad_gain_attn))
    input_grad = (d_hidden + d_inputs).reshape(seq_count, local_len, model_width)
    return (
        output,
        input_grad,
        attn_sums[0],
        attn_sums[1],
        attn_sums[2],
        attn_sums[3],
        mlp_sums[0],
        mlp_sums[1],
        mlp_sums[2],
        attn_sums[4],
        mlp_sums[3],
    )


EPS = epsilon
NEG = -1e30


def dot32(left, right, dims=((1,), (0,))):
    return lax.dot_general(left, right, (dims, ((), ())), preferred_element_type=jnp.float32)


NT = ((1,), (1,))
TN = ((0,), (0,))


def lane_mask(rows):
    return lax.broadcasted_iota(jnp.int32, (rows, 128), 1) < HEAD_DIM


def swap_halves(u):
    half = HEAD_DIM // 2
    lanes = lax.broadcasted_iota(jnp.int32, u.shape, 1) % HEAD_DIM
    return jnp.where(lanes < half, pltpu.roll(u, 128 - half, 1), pltpu.roll(u, half, 1))


def allowed_pairs(seg_col, seg_row, first, rows, keys):
    q_ids = lax.broadcasted_iota(jnp.int32, (rows, keys), 0) + first
    k_ids = lax.broadcasted_iota(jnp.int32, (rows, keys), 1)
    return (k_ids <= q_ids) & (seg_col == seg_row)


def attend_kernel(block, qk_ref, v_ref, seg_col_ref, seg_row_ref, *refs):
    o_ref, lse_ref = refs[-2:]
    length = qk_ref.shape[0]
    first_head = lane_mask(block)
    for step in range(length // block):
        rows = slice(step * block, (step + 1) * block)
        keys = (step + 1) * block
        allowed = allowed_pairs(
            seg_col_ref[rows, :1], seg_row_ref[:, :keys], step * block, block, keys
        )
        q_pair = qk_ref[rows, :128]
        k_pair = qk_ref[:keys, 128:]
        v_pair = v_ref[:keys, :]
        outs, totals = [], []
        for head in range(2):
            mine = first_head if head == 0 else jnp.logical_not(first_head)
            q_head = jnp.where(mine, q_pair, jnp.zeros_like(q_pair))
            z = jnp.where(allowed, dot32(q_head, k_pair, NT), NEG)
            top = jnp.max(z, axis=-1, keepdims=True)
            e = jnp.exp(z - top)
            total = jnp.sum(e, axis=-1, keepdims=True)
            p = (e * (1.0 / total)).astype(jnp.bfloat16)
            outs.append(dot32(p, v_pair))
            totals.append(top + jnp.log(total))
        o_ref[rows, :] = jnp.where(first_head, outs[0], outs[1]).astype(o_ref.dtype)
        lse_ref[rows, :] = jnp.where(first_head, totals[0], totals[1])


def attend_back_kernel(
    block, qk_ref, v_ref, do_ref, lse_ref, cos_ref, sin_ref, seg_col_ref, seg_row_ref, *refs
):
    dqk_ref, dv_ref, dk_sum, dv_sum = refs[-4:]
    length = qk_ref.shape[0]
    first_head = lane_mask(block)
    for step in range(length // block):
        rows = slice(step * block, (step + 1) * block)
        keys = (step + 1) * block
        allowed = allowed_pairs(
            seg_col_ref[rows, :1], seg_row_ref[:, :keys], step * block, block, keys
        )
        q_pair = qk_ref[rows, :128]
        k_pair = qk_ref[:keys, 128:]
        v_pair = v_ref[:keys, :]
        do_pair = do_ref[rows, :]
        dq_heads = []
        dk_step = dv_step = None
        for head in range(2):
            mine = first_head if head == 0 else jnp.logical_not(first_head)
            q_head = jnp.where(mine, q_pair, jnp.zeros_like(q_pair))
            do_head = jnp.where(mine, do_pair, jnp.zeros_like(do_pair))
            lse = lse_ref[rows, head * HEAD_DIM : head * HEAD_DIM + 1]
            z = jnp.where(allowed, dot32(q_head, k_pair, NT), NEG)
            p = jnp.exp(z - lse)
            dp = dot32(do_head, v_pair, NT)
            dv_head = dot32(p.astype(jnp.bfloat16), do_head, TN)
            row_dot = jnp.sum(p * dp, axis=-1, keepdims=True)
            ds = (p * (dp - row_dot)).astype(jnp.bfloat16)
            dq_heads.append(dot32(ds, k_pair))
            dk_head = dot32(ds, q_head, TN)
            dk_step = dk_head if dk_step is None else dk_step + dk_head
            dv_step = dv_head if dv_step is None else dv_step + dv_head
        dq = jnp.where(first_head, dq_heads[0], dq_heads[1]) * (HEAD_DIM**-0.5)
        dq = dq * cos_ref[rows, :] - swap_halves(dq) * sin_ref[rows, :]
        dqk_ref[rows, :128] = dq.astype(dqk_ref.dtype)
        last = slice(step * block, keys)
        if step > 0:
            dk_sum[: step * block, :] += dk_step[: step * block]
            dv_sum[: step * block, :] += dv_step[: step * block]
        dk_sum[last, :] = dk_step[step * block :]
        dv_sum[last, :] = dv_step[step * block :]
    dk = dk_sum[...]
    dk = dk * cos_ref[...] - swap_halves(dk) * sin_ref[...]
    dqk_ref[:, 128:] = dk.astype(dqk_ref.dtype)
    dv_ref[...] = dv_sum[...].astype(dv_ref.dtype)


def qkv_kernel(x_ref, gain_ref, qk_w_ref, v_w_ref, cos_ref, sin_ref, a_ref, qk_ref, v_ref):
    x = x_ref[...].astype(jnp.float32)
    r = lax.rsqrt(jnp.mean(x * x, axis=-1, keepdims=True) + EPS)
    a = (x * r * gain_ref[...]).astype(jnp.bfloat16)
    a_ref[...] = a
    u = dot32(a, qk_w_ref[...])
    cos, sin = cos_ref[...], sin_ref[...]
    for at in range(0, u.shape[1], 256):
        q = u[:, at : at + 128]
        q = (q * cos + swap_halves(q) * sin) * (HEAD_DIM**-0.5)
        qk_ref[:, at : at + 128] = q.astype(jnp.bfloat16)
        k = u[:, at + 128 : at + 256]
        k = k * cos + swap_halves(k) * sin
        qk_ref[:, at + 128 : at + 256] = k.astype(jnp.bfloat16)
    v_ref[...] = dot32(a, v_w_ref[...]).astype(jnp.bfloat16)


def whole(shape):
    return pl.BlockSpec(shape, lambda i: (0,) * len(shape))


def row_block(rows, width):
    return pl.BlockSpec((rows, width), lambda i: (i, 0))


def lane_block(length):
    return pl.BlockSpec((length, 128), lambda i: (0, i))


def project(x, gain, w_qk, w_v, cos, sin):
    length, model = x.shape
    width = w_v.shape[1]
    rows = 256
    low = lambda n: jax.ShapeDtypeStruct((length, n), jnp.bfloat16)
    return pl.pallas_call(
        qkv_kernel,
        grid=(length // rows,),
        in_specs=[
            row_block(rows, model), whole((1, model)), whole(w_qk.shape), whole(w_v.shape),
            row_block(rows, 128), row_block(rows, 128),
        ],
        out_specs=[row_block(rows, model), row_block(rows, 2 * width), row_block(rows, width)],
        out_shape=[low(model), low(2 * width), low(width)],
        compiler_params=pltpu.CompilerParams(vmem_limit_bytes=VMEM),
        cost_estimate=pl.CostEstimate(flops=1, bytes_accessed=1, transcendentals=0),
        name="project",
    )(x, gain, w_qk, w_v, cos, sin)


def over_pairs(kernel, name, some, arrays, shared, outs, scratch, into=()):
    length = arrays[0].shape[0]
    pairs = arrays[1].shape[1] // 128
    first, last = some
    of_pair = lambda width: pl.BlockSpec((length, width), lambda i: (0, first + i))
    inputs = tuple(arrays) + tuple(shared)
    return pl.pallas_call(
        functools.partial(kernel, 256),
        grid=(last - first,),
        in_specs=[of_pair(a.shape[1] // pairs) for a in arrays]
        + [whole(a.shape) for a in shared]
        + [pl.BlockSpec(memory_space=pl.ANY)] * len(into),
        out_specs=[of_pair(width) for width, _ in outs],
        out_shape=[jax.ShapeDtypeStruct((length, pairs * width), kind) for width, kind in outs],
        scratch_shapes=scratch,
        input_output_aliases={len(inputs) + i: i for i in range(len(into))},
        compiler_params=pltpu.CompilerParams(vmem_limit_bytes=VMEM),
        cost_estimate=pl.CostEstimate(flops=1, bytes_accessed=1, transcendentals=0),
        name=name,
    )(*inputs, *into)


def attend(some, qk, v, seg_col, seg_row, *into):
    return over_pairs(
        attend_kernel, "attend", some, (qk, v), (seg_col, seg_row),
        [(128, jnp.bfloat16), (128, jnp.float32)], [], into,
    )


def attend_back(some, arrays, into):
    length = arrays[0].shape[0]
    return over_pairs(
        attend_back_kernel, "attend_back", some, arrays[:4], arrays[4:],
        [(256, jnp.bfloat16), (128, jnp.bfloat16)],
        [pltpu.VMEM((length, 128), jnp.float32)] * 2, into,
    )


def cut_kernel(core_ref, wq, wk, wv, wo, wg, wu, wd, g1, g2, own, away, ff_own, ff_away, first, last):
    core = core_ref[0]
    rows, width = wq.shape
    half = width // 2
    eye = lax.broadcasted_iota(jnp.int32, (rows, rows), 0) == lax.broadcasted_iota(
        jnp.int32, (rows, rows), 1
    )

    def column(g):
        spread = jnp.where(eye, jnp.broadcast_to(g[...].astype(jnp.float32), (rows, rows)), 0.0)
        return jnp.sum(spread, axis=1, keepdims=True)

    lane = lax.broadcasted_iota(jnp.int32, (rows, 128), 1)
    gains = jnp.where(lane == 0, column(g1), jnp.where(lane == 1, column(g2), 0.0))
    for out, ff, side in ((own, ff_own, core), (away, ff_away, 1 - core)):
        for at in range(0, half, 128):
            for i, w in enumerate((wq, wk)):
                cols = pl.ds(pl.multiple_of(side * half + at, 128), 128)
                out[:, 2 * at + i * 128 : 2 * at + (i + 1) * 128] = w[:, cols]
        cols = pl.ds(pl.multiple_of(side * half, 128), half)
        out[:, width : width + half] = wv[:, cols]
        out[:, width + half : 2 * width] = wo[:, cols]
        out[:, 2 * width :] = gains.astype(jnp.bfloat16)
        n_blocks = ff.shape[1] // half
        for i in range(n_blocks):
            w = wg if i < n_blocks // 2 else wu
            block = 2 * (i % (n_blocks // 2)) + side
            ff[:, i * half : (i + 1) * half] = w[:, pl.ds(pl.multiple_of(block * half, 128), half)]
    first[...] = wd[:, : width // 2]
    last[...] = wd[:, width // 2 :]


def cut_shards(core, weights, gains):
    rows, width = weights[0].shape
    ff = weights[4].shape[1]
    down_rows = weights[6].shape[0]
    shape = lambda *dims: jax.ShapeDtypeStruct(dims, jnp.bfloat16)
    in_vmem = pl.BlockSpec(memory_space=pltpu.VMEM)
    return pl.pallas_call(
        cut_kernel,
        in_specs=[pl.BlockSpec(memory_space=pltpu.SMEM)] + [in_vmem] * 9,
        out_specs=[in_vmem] * 6,
        out_shape=[shape(rows, 2 * width + 128)] * 2
        + [shape(rows, ff)] * 2
        + [shape(down_rows, width // 2)] * 2,
        cost_estimate=pl.CostEstimate(flops=1, bytes_accessed=1, transcendentals=0),
        name="cut_shards",
    )(core.reshape(1).astype(jnp.int32), *weights, *(g[None, :] for g in gains))


STEP = 32


def turn_tables():
    lanes = np.arange(128) % (HEAD_DIM // 2)
    frequency = 10000.0 ** -(lanes * 2.0 / HEAD_DIM)
    tables = []
    for unit in (STEP, 1):
        angles = unit * np.arange(STEP)[:, None] * frequency[None, :]
        rest = np.concatenate([np.cos(angles), np.sin(angles)], axis=1)
        for _ in range(3):
            part = rest.astype(jnp.bfloat16)
            tables.append(part)
            rest = rest - part.astype(np.float64)
    return jnp.asarray(np.stack(tables))


def unpack_kernel(core_ref, own, other, tables, x, cos_ref, sin_ref, seg_col, seg_row):
    first = core_ref[0] == 0
    span = x.shape[0] // 2
    eye = lax.broadcasted_iota(jnp.int32, (span, span), 0) == lax.broadcasted_iota(
        jnp.int32, (span, span), 1
    )
    lanes = lax.broadcasted_iota(jnp.int32, (span, STEP), 1).astype(jnp.float32)
    half = HEAD_DIM // 2
    turned = lax.broadcasted_iota(jnp.int32, (span, 128), 1) % HEAD_DIM < half
    for h in range(2):
        rows = slice(h * span, (h + 1) * span)
        mine, theirs = (own, other) if h == 0 else (other, own)
        x[rows, :] = jnp.where(first, mine[0, :span, :], theirs[0, :span, :])
        numbers = [r[0, span : span + 16, : 3 * span].astype(jnp.float32)[:1] for r in (mine, theirs)]
        numbers = jnp.where(first, numbers[0], numbers[1])

        def column(i):
            row = numbers[:, i * span : (i + 1) * span]
            spread = jnp.where(eye, jnp.broadcast_to(row, (span, span)), 0.0)
            return jnp.sum(spread, axis=1, keepdims=True)

        def table(i):
            chosen = jnp.where(column(i) == lanes, 1.0, 0.0).astype(jnp.bfloat16)
            t = sum(dot32(chosen, tables[3 * i + j]) for j in range(3))
            return t[:, :128], t[:, 128:]

        (cos_a, sin_a), (cos_b, sin_b) = table(0), table(1)
        cos_ref[rows, :] = cos_a * cos_b - sin_a * sin_b
        sine = sin_a * cos_b + cos_a * sin_b
        sin_ref[rows, :] = jnp.where(turned, -sine, sine)
        seg_col[rows, :] = jnp.broadcast_to(column(2), (span, 128)).astype(jnp.int32)
        seg_row[:, rows] = numbers[:, 2 * span : 3 * span].astype(jnp.int32)


def unpack_blocks(core, own, other):
    blocks, packed_rows, model = own.shape
    span = 128
    length = blocks * 2 * span
    tables = turn_tables()
    shape = lambda width, kind: jax.ShapeDtypeStruct((length, width), kind)
    of_block = pl.BlockSpec((1, packed_rows, model), lambda i, s: (i, 0, 0))
    rows = lambda width: pl.BlockSpec((2 * span, width), lambda i, s: (i, 0))
    return pl.pallas_call(
        unpack_kernel,
        grid_spec=pltpu.PrefetchScalarGridSpec(
            num_scalar_prefetch=1,
            grid=(blocks,),
            in_specs=[of_block, of_block, pl.BlockSpec(tables.shape, lambda i, s: (0, 0, 0))],
            out_specs=[rows(model), rows(128), rows(128), rows(128)]
            + [pl.BlockSpec((1, 2 * span), lambda i, s: (0, i))],
        ),
        out_shape=[
            shape(model, jnp.bfloat16), shape(128, jnp.float32), shape(128, jnp.float32),
            shape(128, jnp.int32), jax.ShapeDtypeStruct((1, length), jnp.int32),
        ],
        cost_estimate=pl.CostEstimate(flops=1, bytes_accessed=1, transcendentals=0),
        name="unpack",
    )(core.reshape(1).astype(jnp.int32), own, other, tables)


def rounded_sum(*parts):
    total = parts[0]
    for part in parts[1:]:
        total = total + part
    return total


def ff_grads_kernel(bits, c, d_gate, d_up, hid, dy, x_out, x_keep, y_out, y_keep, ff, down):
    rows, cols = x_out.shape[-2:]
    n_wide = d_gate.shape[1] // cols
    n_down = x_out.shape[1] - 2 * n_wide
    away = pl.program_id(0) != bits[1]

    def cut_side(out, lead, side, first):
        for block in range(2):
            here = pl.ds(pl.multiple_of((side * 2 + block) * rows, rows), rows)
            for k in range(n_wide):
                slab = ff[here, k * cols : (k + 1) * cols]
                out[lead, block * n_wide + k] = slab.astype(jnp.bfloat16)
        for j in range(n_down):
            here = pl.ds(pl.multiple_of((side * n_down + j) * rows, rows), rows)
            out[lead, 2 * n_wide + j] = down[here, first : first + cols].astype(jnp.bfloat16)

    down[...] = dot32(hid[...], dy[...], TN)
    ff[...] = dot32(c[...], d_gate[...], TN)
    cut_side(x_out, 0, 1 - bits[0], 0)
    cut_side(x_keep, 0, bits[0], 0)
    ff[...] = dot32(c[...], d_up[...], TN)

    def by_y(out):
        for x in range(2):
            cut_side(out, x, x, cols)

    pl.when(away)(lambda: by_y(y_out))
    pl.when(jnp.logical_not(away))(lambda: by_y(y_keep))


def ff_grads(bits, c, d_gate, d_up, hid, dy, slabs):
    length, model = c.shape
    ff = d_gate.shape[1]
    half = lambda width: pl.BlockSpec((length, width // 2), lambda y, bits: (0, y))
    full = lambda a: pl.BlockSpec(a.shape, lambda y, bits: (0, 0), pipeline_mode=pl.Buffered(1))
    one = pl.BlockSpec((1,) + slabs, lambda y, bits: (y, 0, 0, 0))
    both = pl.BlockSpec((2,) + slabs, lambda y, bits: (0,) * 4)
    return pl.pallas_call(
        ff_grads_kernel,
        grid_spec=pltpu.PrefetchScalarGridSpec(
            num_scalar_prefetch=1,
            grid=(2,),
            in_specs=[half(model), full(d_gate), full(d_up), half(ff), full(dy)],
            out_specs=[one, one, both, both],
            scratch_shapes=[
                pltpu.VMEM((model // 2, ff), jnp.float32), pltpu.VMEM((ff // 2, model), jnp.float32)
            ],
        ),
        out_shape=[jax.ShapeDtypeStruct((2,) + slabs, jnp.bfloat16)] * 4,
        compiler_params=pltpu.CompilerParams(vmem_limit_bytes=VMEM),
        cost_estimate=pl.CostEstimate(flops=1, bytes_accessed=1, transcendentals=0),
        name="ff_grads",
    )(bits, c, d_gate, d_up, hid, dy)


def attn_grads_kernel(
    bits, a, dqk, dv, ob, db, gains, qk_out, qk_keep, vo_out, vo_keep, qk
):
    side = qk.shape[0] // 2
    width = dv.shape[1]
    qk[...] = dot32(a[...], dqk[...], TN)
    for out, x in ((qk_out, 1 - bits[0]), (qk_keep, bits[0])):
        here = pl.ds(pl.multiple_of(x * side, side), side)
        out[0] = qk[here, :].astype(jnp.bfloat16)

    def by_y(out):
        out[:, :width] = dot32(a[...], dv[...], TN).astype(jnp.bfloat16)
        out[:, width : 2 * width] = dot32(ob[...], db[...], TN).astype(jnp.bfloat16)
        out[:, 2 * width :] = gains[...].astype(jnp.bfloat16)

    away = pl.program_id(0) != bits[1]
    pl.when(away)(lambda: by_y(vo_out))
    pl.when(jnp.logical_not(away))(lambda: by_y(vo_keep))


def attn_grads(bits, a, dqk, dv, ob, db, gains):
    length, model = a.shape
    width = dv.shape[1]
    half = lambda: pl.BlockSpec((length, model // 2), lambda y, bits: (0, y))
    full = lambda t: pl.BlockSpec(t.shape, lambda y, bits: (0, 0))
    qk_rows = pl.BlockSpec((1, model // 4, 2 * width), lambda y, bits: (y, 0, 0))
    vo_rows = pl.BlockSpec((model // 2, 2 * width + 128), lambda y, bits: (0, 0))
    return pl.pallas_call(
        attn_grads_kernel,
        grid_spec=pltpu.PrefetchScalarGridSpec(
            num_scalar_prefetch=1,
            grid=(2,),
            in_specs=[
                half(), full(dqk), full(dv), half(),
                pl.BlockSpec((length, width), lambda y, bits: (0, bits[3])),
                pl.BlockSpec((model // 2, 128), lambda y, bits: (y, 0)),
            ],
            out_specs=[qk_rows, qk_rows, vo_rows, vo_rows],
            scratch_shapes=[pltpu.VMEM((model // 2, 2 * width), jnp.float32)],
        ),
        out_shape=[jax.ShapeDtypeStruct((2, model // 4, 2 * width), jnp.bfloat16)] * 2
        + [jax.ShapeDtypeStruct((model // 2, 2 * width + 128), jnp.bfloat16)] * 2,
        compiler_params=pltpu.CompilerParams(vmem_limit_bytes=VMEM),
        cost_estimate=pl.CostEstimate(flops=1, bytes_accessed=1, transcendentals=0),
        name="attn_grads",
    )(bits, a, dqk, dv, ob, db, gains)


def ff_second_kernel(bits, x_keep, x_came, y_keep, y_came, x_out, y_out):
    for p in range(x_out.shape[0]):
        x_out[p] = rounded_sum(x_keep[0, p], x_came[0, p])
        y_out[p] = rounded_sum(y_keep[0, p], y_came[0, p])


def ff_line_kernel(bits, x_keep, x_came, x_last, y_keep, y_came, y_last, kept, sent, slab):
    n_slabs, rows = x_last.shape[:2]
    shard = kept.shape[2]
    n_down = rows // shard
    n_ff = n_slabs - n_down
    for at, keep, came, last in ((0, x_keep, x_came, x_last), (n_slabs, y_keep, y_came, y_last)):
        for p in range(n_slabs):
            slab[...] = rounded_sum(keep[0, p], came[0, p], last[p]).astype(jnp.float32)
            for i in range(n_down):
                piece = slab[i * shard : (i + 1) * shard, :].astype(jnp.bfloat16)
                if p < n_ff:
                    z1, z0, to = i // 2, i % 2, at + p
                else:
                    z1, z0, to = (p - n_ff) // 2, (p - n_ff) % 2, at + n_ff + i

                def put(out, z1=z1, to=to, piece=piece):
                    out[z1, to] = piece

                pl.when(bits[2] == z0)(functools.partial(put, kept))
                pl.when(bits[2] != z0)(functools.partial(put, sent))


def ff_call(kernel, name, bits, inputs, outs, scratch=()):
    def spec(array, at):
        block = tuple(1 if i in at else n for i, n in enumerate(array.shape))
        return pl.BlockSpec(
            block,
            lambda i, bits: tuple(at[d](bits) if d in at else 0 for d in range(array.ndim)),
        )

    return pl.pallas_call(
        kernel,
        grid_spec=pltpu.PrefetchScalarGridSpec(
            num_scalar_prefetch=1,
            grid=(1,),
            in_specs=[spec(*pair) for pair in inputs],
            out_specs=[pl.BlockSpec(o, lambda i, bits, n=len(o): (0,) * n) for o in outs],
            scratch_shapes=scratch,
        ),
        out_shape=[jax.ShapeDtypeStruct(o, jnp.bfloat16) for o in outs],
        compiler_params=pltpu.CompilerParams(vmem_limit_bytes=VMEM),
        cost_estimate=pl.CostEstimate(flops=1, bytes_accessed=1, transcendentals=0),
        name=name,
    )(bits, *[array for array, _ in inputs])


def by_bit(own, other, bit, axis):
    own, other = jnp.expand_dims(own, axis), jnp.expand_dims(other, axis)
    shape = [1] * own.ndim
    shape[axis] = 2
    return jnp.where(lax.broadcasted_iota(jnp.int32, shape, axis) == bit, own, other)


def pick(v, at, axis):
    return lax.dynamic_index_in_dim(v, at, axis, keepdims=False)


def pick_static(v, at, axis):
    return lax.index_in_dim(v, at, axis, keepdims=False)


class Cube:
    def __init__(self, seq_size, ctx_size):
        self.sizes = {"seq": seq_size, "ctx": ctx_size}
        self.steps = {"core": ("seq", 1), "x": ("seq", 2), "y": ("seq", 4), "z0": ("ctx", 1), "z1": ("ctx", 2)}
        self.bits = {
            name: (lax.axis_index(axis) // step) % 2 for name, (axis, step) in self.steps.items()
        }
        self.last = ()

    def step(self, work, *arrays):
        if self.last:
            arrays = lax.optimization_barrier((arrays, self.last))[0]
        result = work(*arrays)
        self.last = tuple(jax.tree.leaves(result))
        return result

    def settle(self):
        names = tuple(self.bits)
        values = self.hold(*self.bits.values())
        self.bits = dict(zip(names, values))

    def hold(self, *arrays):
        return lax.optimization_barrier((arrays, self.last))[0]

    def swap(self, v, name):
        axis, step = self.steps[name]
        return lax.ppermute(v, axis, [(i, i ^ step) for i in range(self.sizes[axis])])

    def mine(self, v, name, axis):
        return pick(v, self.bits[name], axis)

    def away(self, v, name, axis):
        return pick(v, 1 - self.bits[name], axis)

    def joined(self, own, other, name, axis):
        return lax.optimization_barrier(by_bit(own, other, self.bits[name], axis))

    def traded(self, v, came, steps):
        for other, (name, axis, at) in zip(came, steps):
            v = by_bit(self.mine(v, name, axis), other, self.bits[name], at)
        return v

    def summed(self, v, came, steps):
        for other, (name, axis) in zip(came, steps):
            v = low(wide(self.mine(v, name, axis)) + wide(other))
        return v

def low(v):
    return v.astype(jnp.bfloat16)


def wide(v):
    return v.astype(jnp.float32)


def rows_of(v):
    return v.reshape(-1, v.shape[-1])


def r_of(u):
    return lax.rsqrt(jnp.mean(u * u, axis=-1, keepdims=True) + EPS)


def norm_back(u, gain, dn):
    r = r_of(u)
    gd = gain * dn
    return r * gd - u * (r * r * r) * jnp.mean(gd * u, axis=-1, keepdims=True)


def sequence_per_chip(seq_size, ctx_size):
    def on_device(
        tokens, segments, positions,
        w_query, w_key, w_value, w_out, w_gate, w_up, w_down,
        gain_attn, gain_mlp, cotangent,
    ):
        cube = Cube(seq_size, ctx_size)
        step, swap, hold, mine, away = cube.step, cube.swap, cube.hold, cube.mine, cube.away
        joined, traded, summed = cube.joined, cube.traded, cube.summed
        bits = cube.bits
        core = cube.bits["core"]
        seqs, local_len, model = tokens.shape
        seq_len = segments.shape[1]
        span = local_len // 2
        own_rows = w_query.shape[0]
        half_width = w_query.shape[1] // 2
        ff_rows = w_down.shape[0]
        ff_half = w_gate.shape[1] // 2
        n_blocks = seq_size // 2
        ff_block = ff_half // n_blocks
        model_half = model // 2
        pairs = half_width // 128

        attn_own, attn_away, ff_own, ff_away, first, last = step(
            lambda *w: tuple(cut_shards(core, w[:7], w[7:])),
            w_query, w_key, w_value, w_out, w_gate, w_up, w_down, gain_attn, gain_mlp,
        )
        attn_came = swap(attn_away, "core")

        def pack_tokens(tokens, positions, segments):
            own_first = lax.axis_index("ctx") * local_len
            own_segments = lax.dynamic_slice_in_dim(segments, own_first, local_len, axis=1)
            numbers = low(jnp.stack([positions // STEP, positions % STEP, own_segments]))
            numbers = numbers.reshape(3, seqs, 2, span).transpose(1, 2, 0, 3)
            numbers = numbers.reshape(seqs, 2, 1, 3 * span)
            numbers = jnp.pad(numbers, ((0, 0), (0, 0), (0, 15), (0, model - 3 * span)))
            pack = jnp.concatenate([tokens.reshape(seqs, 2, span, model), numbers], axis=2)
            return pack, away(pack, "core", 1)

        to_chip = (("core", 1, 0), ("z0", 1, 1), ("z1", 0, 0))

        def sent_next(steps, n):
            name, axis = steps[n][:2]
            return lambda v, *came: away(traded(v, came, steps), name, axis)

        x_pack, sent = step(pack_tokens, tokens, positions, segments)
        x_came = [swap(sent, "core")]

        attn_piece = step(lambda v, w: joined(v, w, "core", 0), attn_own, attn_came)
        attn_came = swap(attn_piece, "z1")

        x_came.append(swap(step(sent_next(to_chip, 1), x_pack, *x_came), "z0"))

        cube.settle()
        bits = cube.bits

        ff_came = swap(*hold(ff_away), "core")
        ff_piece = step(lambda v, w: joined(v, w, "core", 0), ff_own, ff_came)

        attn_half_line = step(lambda v, w: joined(v, w, "z1", 1), attn_piece, attn_came)
        attn_came = swap(attn_half_line, "z0")

        first_came, last_came = swap(*hold(first), "x"), swap(*hold(last), "y")

        ff_came = swap(*hold(ff_piece), "z1")

        x_came.append(swap(step(sent_next(to_chip, 2), x_pack, *x_came), "z1"))

        down_pair = step(
            lambda a, b, c, d: jnp.concatenate(
                [joined(a, b, "x", 0), joined(c, d, "y", 0)], axis=2
            ),
            first, first_came, last, last_came,
        )

        def attn_to_line(v, came):
            line = joined(v, came, "z0", 2)
            return line[..., : 2 * half_width], line[..., 2 * half_width :]

        qk_line, vo_line = step(attn_to_line, attn_half_line, attn_came)
        qk_came, vo_came = swap(qk_line, "x"), swap(vo_line, "y")

        dy_pack = cotangent.reshape(seqs, 2, span, model)
        dy_came = [swap(step(sent_next(to_chip, 0), dy_pack), "core")]

        ff_half_line = step(lambda v, w: joined(v, w, "z1", 1), ff_piece, ff_came)
        ff_came = swap(ff_half_line, "z0")

        qk_plane = step(lambda v, w: joined(v, w, "x", 0), qk_line, qk_came)
        qk_came = swap(qk_plane, "y")
        vo_plane = step(lambda v, w: joined(v, w, "y", 0), vo_line, vo_came)
        vo_came = swap(vo_plane, "x")

        x_half = step(
            lambda v, *came: traded(v, came, to_chip).reshape(ctx_size, -1, model), x_pack, *x_came
        )
        x_other = swap(x_half, "core")

        down_came = swap(*hold(down_pair), "z1")

        def attn_to_full(qk, qk_came, vo, vo_came):
            qk = rows_of(joined(qk, qk_came, "y", 0))
            vo = rows_of(joined(vo, vo_came, "x", 1))
            gains = wide(vo[:, 2 * half_width : 2 * half_width + 2])
            return (
                qk, vo[:, :half_width], vo[:, half_width : 2 * half_width],
                gains[:, 0][None, :], gains[:, 1],
            )

        qk_full, v_full, out_half, gain_one, gain_two = step(
            attn_to_full, qk_plane, qk_came, vo_plane, vo_came
        )
        out_came = swap(out_half, "core")

        def ff_to_line(v, came):
            line = joined(v, came, "z0", 2)
            return line[..., :ff_half], line[..., ff_half:]

        gate_line, up_line = step(ff_to_line, ff_half_line, ff_came)

        gate_came, up_came = swap(gate_line, "x"), swap(up_line, "y")

        dy_came.append(swap(step(sent_next(to_chip, 1), dy_pack, *dy_came), "z0"))

        def unpack_tokens(x_half, x_other):
            x, cos, sin, seg_col, seg_row = unpack_blocks(core, x_half, x_other)
            return x, x_half[:, :span], seg_col, seg_row, cos, sin

        x, x_half, seg_col, seg_row, cos, sin = step(unpack_tokens, x_half, x_other)

        down_half_line = step(lambda v, w: joined(v, w, "z1", 1), down_pair, down_came)
        down_came = swap(down_half_line, "z0")

        def halves(own, other):
            whole = jnp.zeros((own.shape[0], 2 * own.shape[1]), own.dtype)
            whole = lax.dynamic_update_slice(whole, own, (0, core * own.shape[1]))
            return lax.dynamic_update_slice(whole, other, (0, (1 - core) * own.shape[1]))

        normed, qk, v = step(lambda *t: tuple(project(*t)), x, gain_one, qk_full, v_full, cos, sin)
        segs = (seg_col, seg_row)

        gate_plane = step(lambda v, w: joined(v, w, "x", 0), gate_line, gate_came)
        gate_came = swap(gate_plane, "y")
        up_plane = step(lambda v, w: joined(v, w, "y", 0), up_line, up_came)
        up_came = swap(up_plane, "x")

        dy_came.append(swap(step(sent_next(to_chip, 2), dy_pack, *dy_came), "z1"))


        ob_half, lse = step(lambda *t: tuple(attend((0, pairs), *t)), qk, v, *segs)
        ob_came = swap(ob_half, "core")

        def lay(into, own, bit, axis):
            return lax.dynamic_update_index_in_dim(into, own, bit, axis)

        def lay_own(gate, up):
            ff = jnp.zeros((2,) + gate.shape, gate.dtype)
            return lay(ff, gate, bits["y"], 0), lay(ff, up, bits["x"], 1)

        gate_part, up_part = step(lay_own, gate_plane, up_plane)

        out_full = step(halves, out_half, out_came)

        def down_to_line(v, came):
            line = joined(v, came, "z0", 2)
            return line[..., :model_half], line[..., model_half:]

        first_line, last_line = step(down_to_line, down_half_line, down_came)
        first_came, last_came = swap(first_line, "y"), swap(last_line, "x")

        gate_full, up_full = step(
            lambda a, b, c, d: (
                rows_of(lay(a, b, 1 - bits["y"], 0)), rows_of(lay(c, d, 1 - bits["x"], 1))
            ),
            gate_part, gate_came, up_part, up_came,
        )

        dy_half = step(
            lambda v, *came: traded(v, came, to_chip).reshape(ctx_size, span, model),
            dy_pack, *dy_came,
        )
        dy_other = swap(dy_half, "core")

        ob = step(halves, ob_half, ob_came)

        def own_half(t):
            return mine(t.reshape(ctx_size, 2, span, t.shape[-1]), "core", 1)

        def hidden(x, ob, out_full, gain_two):
            h1 = wide(x) + dot32(ob, out_full)
            return h1, low(h1 * r_of(h1) * gain_two)

        h1, normed_two = step(hidden, x, ob, out_full, gain_two)

        gate = step(dot32, normed_two, gate_full)

        dy = step(
            lambda a, b: joined(a, b, "core", 1).reshape(seq_len, model), dy_half, dy_other
        )

        def up_and_hidden(normed_two, up_full, gate):
            up = dot32(normed_two, up_full)
            s = jax.nn.sigmoid(gate)
            silu = gate * s
            return low(silu), low(up * s * (1.0 + gate * (1.0 - s))), low(silu * up)

        up_factor, gate_factor, hid = step(up_and_hidden, normed_two, up_full, gate)

        down_full = step(
            lambda a, b, c, d: rows_of(
                jnp.concatenate([joined(a, b, "y", 0), joined(c, d, "x", 1)], axis=-1)
            ),
            first_line, first_came, last_line, last_came,
        )

        def back(dy, down_full, gate_factor, up_factor):
            d_hid = dot32(dy, down_full, NT)
            return low(d_hid * wide(gate_factor)), low(d_hid * wide(up_factor))

        by_x = (("x", 1), ("y", 0), ("z0", 2), ("z1", 1), ("core", 0))
        by_y = (("y", 0), ("x", 0), ("z0", 2), ("z1", 1), ("core", 0))

        def to_send(steps, n):
            name, axis = steps[n]
            return lambda v, *came: away(summed(v, came, steps), name, axis)

        d_gate, d_up = step(back, dy, down_full, gate_factor, up_factor)
        n_wide = ff_half // ff_block
        n_down = ff_rows // own_rows
        n_pieces = 2 * n_wide + n_down
        slabs = (n_pieces, ctx_size * own_rows, ff_block)
        bit_array = jnp.stack([bits["x"], bits["y"], bits["z0"], core]).astype(jnp.int32)
        x_mine, x_away = (lambda b: b[0]), (lambda b: 1 - b[0])
        y_mine, y_away = (lambda b: b[1]), (lambda b: 1 - b[1])
        sent_x, x_keep, sent_y, y_keep = step(
            lambda *t: tuple(ff_grads(bit_array, *t, slabs)), normed_two, d_gate, d_up, hid, dy
        )
        x_came, y_came = [swap(sent_x, "x")], [swap(sent_y, "y")]

        def dc_of(d_gate, gate_full, d_up, up_full):
            dc = dot32(d_gate, gate_full, NT) + dot32(d_up, up_full, NT)
            return dc, away(dc.reshape(ctx_size, 2, span, model), "core", 1)

        dc, sent = step(dc_of, d_gate, gate_full, d_up, up_full)
        dc_came = swap(sent, "core")

        def down_of(hid, down_full):
            down = dot32(hid, down_full).reshape(ctx_size, 2, span, model)
            return down, away(down, "core", 1)

        down, sent = step(down_of, hid, down_full)
        down_came = swap(sent, "core")

        def attn_side(dc, came, h1, dy_half, gain_two):
            dc_half = own_half(dc) + came
            dh1 = wide(dy_half) + norm_back(own_half(h1), gain_two, dc_half)
            return dh1, low(dh1), jnp.sum(dc * h1 * r_of(h1), axis=0)

        dh1_half, db_half, gain_two_grad = step(attn_side, dc, dc_came, h1, dy_half, gain_two)
        db_came = swap(db_half, "core")
        home_steps = (("z0", 1, 1), ("z1", 0, 0), ("core", 0, 1))

        def out_of(h1, down, came):
            out = low(own_half(h1) + mine(down, "core", 1) + came).reshape(2, 2, span, model)
            return out, away(out, "z0", 1)

        home, sent = step(out_of, h1, down, down_came)
        home_came = [swap(sent, "z0")]

        def d_attended_of(db_half, db_came, out_full):
            db = joined(db_half, db_came, "core", 1).reshape(seq_len, model)
            out_rows = lax.dynamic_slice_in_dim(out_full, core * half_width, half_width, axis=0)
            return db, low(dot32(db, out_rows, NT))

        db, d_attended = step(d_attended_of, db_half, db_came, out_full)

        backs = (qk, v, d_attended, lse, cos, sin, *segs)
        heads = step(lambda *t: tuple(attend_back((0, pairs - 1), t[:8], t[8:])), *backs)

        home_came.append(swap(step(sent_next(home_steps, 1), home, *home_came), "z1"))

        dqk, dv = step(
            lambda *t: tuple(attend_back((pairs - 1, pairs), t[:8], t[8:])), *backs, *heads
        )

        def plus(v, came):
            return low(wide(v) + wide(came))

        def ff_second(x_keep, x_came, y_keep, y_came):
            return tuple(
                ff_call(
                    ff_second_kernel, "ff_second", bit_array,
                    [(x_keep, {0: y_away}), (x_came, {0: y_away}),
                     (y_keep, {0: x_away}), (y_came, {0: x_away})],
                    [slabs] * 2,
                )
            )

        sent_x, sent_y = step(ff_second, x_keep, *x_came, y_keep, *y_came)
        x_came.append(swap(sent_x, "y"))
        y_came.append(swap(sent_y, "x"))

        home_came.append(swap(step(sent_next(home_steps, 2), home, *home_came), "core"))

        def da_of(qk_full, v_full, dqk, dv, x):
            da = dot32(dqk, qk_full, NT) + dot32(dv, v_full, NT)
            x = wide(x)
            gain = jnp.sum(da * x * r_of(x), axis=0)
            return da, away(da.reshape(ctx_size, 2, span, model), "core", 1), gain

        da, sent, gain_one_grad = step(da_of, qk_full, v_full, dqk, dv, x)
        da_came = swap(sent, "core")

        output = step(
            lambda v, *came: traded(v, came, home_steps).reshape(seqs, local_len, model),
            home, *home_came,
        )

        def input_side(x_half, da, came, gain_one, dh1_half):
            da_half = own_half(da) + came
            du1 = norm_back(wide(x_half), gain_one, da_half)
            du = low(dh1_half + du1).reshape(2, 2, span, model)
            return du, away(du, "z0", 1)

        inward, sent = step(input_side, x_half, da, da_came, gain_one, dh1_half)
        inward_came = [swap(sent, "z0")]

        def attn_grads_of(normed, dqk, dv, ob, db, gain_one, gain_two):
            gains = jnp.pad(jnp.stack([gain_one, gain_two], axis=1), ((0, 0), (0, 126)))
            out = attn_grads(bit_array, normed, dqk, dv, ob, db, gains)
            by_block = lambda v: v.reshape(2, 2, 2, 2, own_rows, v.shape[-1])
            return tuple(by_block(v) for v in out)

        sent_qk, qk_keep, sent_vo, vo_keep = step(
            attn_grads_of, normed, dqk, dv, ob, db, gain_one_grad, gain_two_grad
        )
        qk_came, vo_came = [swap(sent_qk, "x")], [swap(sent_vo, "y")]

        def line_to_send(qk, qk_first, qk_second, vo, vo_first, vo_second):
            qk = summed(plus(qk, qk_first), (qk_second,), by_x[1:])
            vo = summed(plus(vo, vo_first), (vo_second,), by_y[1:])
            line = jnp.concatenate([qk, vo], axis=-1)
            return line, away(line, "z0", 2)

        def ff_line(x_keep, x_came, x_last, y_keep, y_came, y_last):
            return tuple(
                ff_call(
                    ff_line_kernel, "ff_line", bit_array,
                    [(x_keep, {0: y_mine}), (x_came, {0: y_mine}), (x_last, {}),
                     (y_keep, {0: x_mine}), (y_came, {0: x_mine}), (y_last, {})],
                    [(2, 2 * n_pieces, own_rows, ff_block)] * 2,
                    [pltpu.VMEM(slabs[1:], jnp.float32)],
                )
            )

        g_ff, sent = step(ff_line, x_keep, *x_came, y_keep, *y_came)
        ff_came = [swap(sent, "z0")]

        def second_attn(qk, qk_came, vo, vo_came):
            return away(plus(qk, qk_came), "y", 0), away(plus(vo, vo_came), "x", 0)

        sent_qk, sent_vo = step(second_attn, qk_keep, *qk_came, vo_keep, *vo_came)
        qk_came.append(swap(sent_qk, "y"))
        vo_came.append(swap(sent_vo, "x"))

        inward_came.append(swap(step(sent_next(home_steps, 1), inward, *inward_came), "z1"))

        def ff_to_z1(v, came):
            return low(wide(away(v, "z1", 0)) + wide(away(came, "z1", 0)))

        ff_came.append(swap(step(ff_to_z1, g_ff, *ff_came), "z1"))

        g_attn, sent = step(line_to_send, qk_keep, *qk_came, vo_keep, *vo_came)
        attn_came = [swap(sent, "z0")]

        inward_came.append(swap(step(sent_next(home_steps, 2), inward, *inward_came), "core"))

        attn_came.append(swap(step(to_send(by_x[2:], 1), g_attn, *attn_came), "z1"))

        input_grad = step(
            lambda v, *came: wide(traded(v, came, home_steps)).reshape(seqs, local_len, model),
            inward, *inward_came,
        )

        def own_rows_of(v, z0_came, z1_came):
            v = summed(v, (z0_came,), by_x[2:])
            v = wide(mine(v, "z1", 1)) + wide(z1_came)
            return v, away(v, "core", 0)

        def ff_rows_of(v, z0_came, z1_came):
            v = low(wide(mine(v, "z1", 0)) + wide(mine(z0_came, "z1", 0)))
            v = (wide(v) + wide(z1_came)).reshape(2, -1, own_rows, ff_block)
            ff = v[:, : 2 * n_wide].reshape(2, 2, n_wide, own_rows, ff_block)
            down = v[:, 2 * n_wide :].reshape(2, ff_rows, ff_block)
            return ff, away(ff, "core", 1), jnp.concatenate([down[0], down[1]], axis=1)

        g_ff, sent, grad_down = step(ff_rows_of, g_ff, *ff_came)
        ff_came = swap(sent, "core")

        def columns(own, other, first, size):
            own, other = own[:, first : first + size], other[:, first : first + size]
            return [jnp.where(core == 0, own, other), jnp.where(core == 0, other, own)]

        def ff_rows_home(ff, other):
            own = mine(ff, "core", 1)

            def whole_rows(i):
                parts = []
                for block in range(n_blocks):
                    parts += columns(own[i, block], other[i, block], 0, ff_block)
                return jnp.concatenate(parts, axis=1)

            return whole_rows(0), whole_rows(1)

        grad_gate, grad_up = step(ff_rows_home, g_ff, ff_came)

        g_attn, sent = step(own_rows_of, g_attn, *attn_came)
        attn_came = swap(sent, "core")
        def attn_rows_home(own, other):
            def whole_rows(starts, size):
                first, last = zip(*(columns(own, other, at, size) for at in starts))
                return jnp.concatenate(first + last, axis=1)

            query = whole_rows(range(0, 256 * pairs, 256), 128)
            key = whole_rows(range(128, 256 * pairs, 256), 128)
            at = 2 * half_width
            value = whole_rows([at], half_width)
            out = whole_rows([at + half_width], half_width)
            at += 2 * half_width
            gains = (own + other)[:, at : at + 2]
            return query, key, value, out, gains[:, 0], gains[:, 1]

        home_rows = step(lambda v, w: attn_rows_home(mine(v, "core", 0), w), g_attn, attn_came)
        return (output, input_grad) + home_rows[:4] + (grad_gate, grad_up, grad_down) + home_rows[4:]

    return on_device


def solution(mesh):
    in_specs = (
        P("seq", "ctx", None),
        P("seq", None),
        P("seq", "ctx"),
        P(("seq", "ctx"), None),
        P(("seq", "ctx"), None),
        P(("seq", "ctx"), None),
        P(("seq", "ctx"), None),
        P(("seq", "ctx"), None),
        P(("seq", "ctx"), None),
        P(("seq", "ctx"), None),
        P(("seq", "ctx")),
        P(("seq", "ctx")),
        P("seq", "ctx", None),
    )
    out_specs = (
        P("seq", "ctx", None),
        P("seq", "ctx", None),
        P(("seq", "ctx"), None),
        P(("seq", "ctx"), None),
        P(("seq", "ctx"), None),
        P(("seq", "ctx"), None),
        P(("seq", "ctx"), None),
        P(("seq", "ctx"), None),
        P(("seq", "ctx"), None),
        P(("seq", "ctx")),
        P(("seq", "ctx")),
    )
    seq_size, ctx_size = mesh.shape["seq"], mesh.shape["ctx"]
    one_each = sequence_per_chip(seq_size, ctx_size)

    def program(tokens, *others):
        if (seq_size, ctx_size, tokens.shape[0]) == (8, 4, 2):
            return one_each(tokens, *others)
        return on_device(tokens, *others)

    return jax.shard_map(
        program, mesh=mesh, in_specs=in_specs, out_specs=out_specs, check_vma=False
    )
```

```python
import functools

import jax
import jax.numpy as jnp
import numpy as np
from jax import lax
from jax.experimental import pallas as pl
from jax.experimental.pallas import tpu as pltpu
from jax.sharding import PartitionSpec as P

HEADS = 12
KV_HEADS = 12
HEAD_DIM = 64
VMEM = 56 << 20


epsilon = 1e-05


def shortened(value):
    return jax.tree.map(lambda a: a.astype(jnp.bfloat16) if a.dtype == jnp.float32 else a, value)


def rms_scale(values_in, gain_in):
    return (
        values_in
        * lax.rsqrt(jnp.mean(values_in * values_in, axis=-1, keepdims=True) + epsilon)
        * gain_in
    )


def angle_tables(position_ids, head_size):
    half_dim = head_size // 2
    frequency = 10000.0 ** (-(jnp.arange(half_dim, dtype=jnp.float32) * 2.0 / head_size))
    angles = position_ids.astype(jnp.float32)[:, None] * frequency[None, :]
    angles = jnp.concatenate([angles, angles], axis=-1)
    return (jnp.cos(angles), jnp.sin(angles))


def rotate(values_in, cosine, sine_table):
    half_dim = values_in.shape[-1] // 2
    turned = jnp.concatenate([-values_in[..., half_dim:], values_in[..., :half_dim]], axis=-1)
    return values_in * cosine[:, None, :] + turned * sine_table[:, None, :]


def unrotate(grad_in, cosine, sine_table):
    half_dim = grad_in.shape[-1] // 2
    scaled = grad_in * sine_table[:, None, :]
    turned = jnp.concatenate([scaled[..., half_dim:], -scaled[..., :half_dim]], axis=-1)
    return grad_in * cosine[:, None, :] + turned


def gather_flat(weight_set):
    return jax.tree.map(
        lambda part, own: part.astype(own.dtype),
        lax.all_gather(shortened(weight_set), ("seq", "ctx"), axis=0, tiled=True),
        weight_set,
    )


def fetch_weights(weight_set):
    return (gather_flat(weight_set), weight_set)


def fetch_again(kept_set):
    return gather_flat(kept_set)


def reduce_grads(grad_set):
    return lax.psum_scatter(grad_set, ("seq", "ctx"), scatter_dimension=0, tiled=True)


def on_device(
    tokens,
    segments,
    positions,
    w_query,
    w_key,
    w_value,
    w_out,
    w_gate,
    w_up,
    w_down,
    gain_attn,
    gain_mlp,
    cotangent,
):
    seq_count, local_len, model_width = tokens.shape
    seq_len = segments.shape[1]
    row_count = seq_count * local_len
    head_group = HEADS // KV_HEADS
    kv_width = KV_HEADS * HEAD_DIM
    score_scale = HEAD_DIM ** (-0.5)
    first_token = lax.axis_index("ctx") * local_len
    own_tokens = first_token + jnp.arange(local_len, dtype=jnp.int32)
    all_tokens = jnp.arange(seq_len, dtype=jnp.int32)
    causal = all_tokens[None, :] <= own_tokens[:, None]
    inputs = tokens.reshape(row_count, model_width).astype(jnp.float32)
    cosine, sine_table = angle_tables(positions.reshape(row_count), HEAD_DIM)
    attn_full, attn_kept = fetch_weights((w_query, w_key, w_value, w_out, gain_attn))
    full_query, full_key, full_value, full_out, full_gain_one = attn_full
    normed = rms_scale(inputs, full_gain_one.astype(jnp.float32)).astype(jnp.bfloat16)
    query_proj = jnp.dot(normed, full_query, preferred_element_type=jnp.float32)
    key_proj = jnp.dot(normed, full_key, preferred_element_type=jnp.float32)
    value_proj = jnp.dot(normed, full_value, preferred_element_type=jnp.float32)
    query_rot = rotate(query_proj.reshape(row_count, HEADS, HEAD_DIM), cosine, sine_table).astype(
        jnp.bfloat16
    )
    key_rot = rotate(key_proj.reshape(row_count, KV_HEADS, HEAD_DIM), cosine, sine_table).astype(
        jnp.bfloat16
    )
    value_low = value_proj.astype(jnp.bfloat16)
    keys_all, values_all = (
        lax.all_gather(key_rot.reshape(seq_count, local_len, kv_width), "ctx", axis=1, tiled=True),
        lax.all_gather(
            value_low.reshape(seq_count, local_len, kv_width), "ctx", axis=1, tiled=True
        ),
    )
    queries = query_rot.reshape(seq_count, local_len, KV_HEADS, head_group, HEAD_DIM)

    def scores_of(q_seq, k_seq, seg_seq):
        own_seg = lax.dynamic_slice_in_dim(seg_seq, first_token, local_len)
        allowed = causal & (own_seg[:, None] == seg_seq[None, :])
        k_heads = k_seq.reshape(seq_len, KV_HEADS, HEAD_DIM)
        raw_scores = jnp.einsum(
            "qkgd,skd->kgqs", q_seq, k_heads, preferred_element_type=jnp.float32
        )
        return jnp.where(allowed[None, None], raw_scores * score_scale, -1e30)

    def attend(pieces):
        q_seq, k_seq, v_seq, seg_seq = pieces
        logits = scores_of(q_seq, k_seq, seg_seq)
        row_max = jnp.max(logits, axis=-1, keepdims=True)
        shifted_exp = jnp.exp(logits - row_max)
        row_sum = jnp.sum(shifted_exp, axis=-1, keepdims=True)
        probs_low = (shifted_exp / row_sum).astype(jnp.bfloat16)
        mixed_heads = jnp.einsum(
            "kgqs,skd->qkgd",
            probs_low,
            v_seq.reshape(seq_len, KV_HEADS, HEAD_DIM),
            preferred_element_type=jnp.float32,
        )
        return (
            mixed_heads.astype(jnp.bfloat16).reshape(local_len, model_width),
            (row_max + jnp.log(row_sum))[..., 0],
        )

    attended, log_totals = lax.map(attend, (queries, keys_all, values_all, segments))
    attended = attended.reshape(row_count, model_width)
    hidden_state = inputs + jnp.dot(attended, full_out, preferred_element_type=jnp.float32)
    mlp_full, mlp_kept = fetch_weights((w_gate, w_up, w_down, gain_mlp))
    full_gate, full_up, full_down, full_gain_two = mlp_full
    normed_two = rms_scale(hidden_state, full_gain_two.astype(jnp.float32)).astype(jnp.bfloat16)
    gate_proj = jnp.dot(normed_two, full_gate, preferred_element_type=jnp.float32)
    up_proj = jnp.dot(normed_two, full_up, preferred_element_type=jnp.float32)
    activated = (jax.nn.silu(gate_proj) * up_proj).astype(jnp.bfloat16)
    final_state = hidden_state + jnp.dot(activated, full_down, preferred_element_type=jnp.float32)
    output = final_state.astype(jnp.bfloat16).reshape(seq_count, local_len, model_width)
    out_grad = cotangent.reshape(row_count, model_width)
    again_gate, again_up, again_down, again_gain_two = fetch_again(mlp_kept)
    grad_down = jnp.einsum("tf,td->fd", activated, out_grad, preferred_element_type=jnp.float32)
    d_activated = jnp.einsum("td,fd->tf", out_grad, again_down, preferred_element_type=jnp.float32)

    def swiglu(gate_in, up_in):
        return jax.nn.silu(gate_in) * up_in

    unused_mlp, swiglu_back = jax.vjp(swiglu, gate_proj, up_proj)
    d_gate, d_up = swiglu_back(d_activated)
    d_gate = d_gate.astype(jnp.bfloat16)
    d_up = d_up.astype(jnp.bfloat16)
    grad_gate = jnp.einsum("td,tf->df", normed_two, d_gate, preferred_element_type=jnp.float32)
    grad_up = jnp.einsum("td,tf->df", normed_two, d_up, preferred_element_type=jnp.float32)
    d_normed_two = jnp.einsum(
        "tf,df->td", d_gate, again_gate, preferred_element_type=jnp.float32
    ) + jnp.einsum("tf,df->td", d_up, again_up, preferred_element_type=jnp.float32)
    unused_norm, norm_two_back = jax.vjp(
        rms_scale, hidden_state, again_gain_two.astype(jnp.float32)
    )
    d_hidden, grad_gain_mlp = norm_two_back(d_normed_two)
    mlp_sums = reduce_grads((grad_gate, grad_up, grad_down, grad_gain_mlp))
    d_hidden = d_hidden + out_grad.astype(jnp.float32)
    d_branch = d_hidden.astype(jnp.bfloat16)
    again_query, again_key, again_value, again_out, again_gain_one = fetch_again(attn_kept)
    grad_out = jnp.einsum("td,te->de", attended, d_branch, preferred_element_type=jnp.float32)
    d_attended = jnp.einsum(
        "te,de->td", d_branch, again_out, preferred_element_type=jnp.float32
    ).astype(jnp.bfloat16)
    d_heads = d_attended.reshape(seq_count, local_len, KV_HEADS, head_group, HEAD_DIM)

    def attend_back(pieces):
        q_seq, k_seq, v_seq, seg_seq, lse_seq, do_seq = pieces
        logits = scores_of(q_seq, k_seq, seg_seq)
        probs = jnp.exp(logits - lse_seq[..., None])
        probs_low = probs.astype(jnp.bfloat16)
        v_heads = v_seq.reshape(seq_len, KV_HEADS, HEAD_DIM)
        d_probs = jnp.einsum("qkgd,skd->kgqs", do_seq, v_heads, preferred_element_type=jnp.float32)
        d_value = jnp.einsum(
            "kgqs,qkgd->skd", probs_low, do_seq, preferred_element_type=jnp.float32
        )
        row_dot = jnp.sum(probs * d_probs, axis=-1, keepdims=True)
        d_scores = (probs * (d_probs - row_dot) * score_scale).astype(jnp.bfloat16)
        d_query = jnp.einsum(
            "kgqs,skd->qkgd",
            d_scores,
            k_seq.reshape(seq_len, KV_HEADS, HEAD_DIM),
            preferred_element_type=jnp.float32,
        )
        d_key = jnp.einsum("kgqs,qkgd->skd", d_scores, q_seq, preferred_element_type=jnp.float32)
        return (
            d_query.reshape(local_len, HEADS, HEAD_DIM),
            d_key.reshape(seq_len, kv_width),
            d_value.reshape(seq_len, kv_width),
        )

    d_query_all, d_key_part, d_value_part = lax.map(
        attend_back, (queries, keys_all, values_all, segments, log_totals, d_heads)
    )
    d_key_own, d_value_own = (
        lax.psum_scatter(d_key_part, "ctx", scatter_dimension=1, tiled=True),
        lax.psum_scatter(d_value_part, "ctx", scatter_dimension=1, tiled=True),
    )
    d_query_low = (
        unrotate(d_query_all.reshape(row_count, HEADS, HEAD_DIM), cosine, sine_table)
        .astype(jnp.bfloat16)
        .reshape(row_count, model_width)
    )
    d_key_low = (
        unrotate(d_key_own.reshape(row_count, KV_HEADS, HEAD_DIM), cosine, sine_table)
        .astype(jnp.bfloat16)
        .reshape(row_count, kv_width)
    )
    d_value_low = d_value_own.reshape(row_count, kv_width).astype(jnp.bfloat16)
    grad_query = jnp.einsum("td,te->de", normed, d_query_low, preferred_element_type=jnp.float32)
    grad_key = jnp.einsum("td,te->de", normed, d_key_low, preferred_element_type=jnp.float32)
    grad_value = jnp.einsum("td,te->de", normed, d_value_low, preferred_element_type=jnp.float32)
    d_normed = jnp.einsum("te,de->td", d_query_low, again_query, preferred_element_type=jnp.float32)
    d_normed = d_normed + jnp.einsum(
        "te,de->td", d_key_low, again_key, preferred_element_type=jnp.float32
    )
    d_normed = d_normed + jnp.einsum(
        "te,de->td", d_value_low, again_value, preferred_element_type=jnp.float32
    )
    unused_first, norm_one_back = jax.vjp(rms_scale, inputs, again_gain_one.astype(jnp.float32))
    d_inputs, grad_gain_attn = norm_one_back(d_normed)
    attn_sums = reduce_grads((grad_query, grad_key, grad_value, grad_out, grad_gain_attn))
    input_grad = (d_hidden + d_inputs).reshape(seq_count, local_len, model_width)
    return (
        output,
        input_grad,
        attn_sums[0],
        attn_sums[1],
        attn_sums[2],
        attn_sums[3],
        mlp_sums[0],
        mlp_sums[1],
        mlp_sums[2],
        attn_sums[4],
        mlp_sums[3],
    )


EPS = epsilon
NEG = -1e30


def dot32(left, right, dims=((1,), (0,))):
    return lax.dot_general(left, right, (dims, ((), ())), preferred_element_type=jnp.float32)


NT = ((1,), (1,))
TN = ((0,), (0,))


def lane_mask(rows):
    return lax.broadcasted_iota(jnp.int32, (rows, 128), 1) < HEAD_DIM


def swap_halves(u):
    half = HEAD_DIM // 2
    lanes = lax.broadcasted_iota(jnp.int32, u.shape, 1) % HEAD_DIM
    return jnp.where(lanes < half, pltpu.roll(u, 128 - half, 1), pltpu.roll(u, half, 1))


def allowed_pairs(seg_col, seg_row, first, rows, keys):
    q_ids = lax.broadcasted_iota(jnp.int32, (rows, keys), 0) + first
    k_ids = lax.broadcasted_iota(jnp.int32, (rows, keys), 1)
    return (k_ids <= q_ids) & (seg_col == seg_row)


def attend_kernel(block, qk_ref, v_ref, seg_col_ref, seg_row_ref, *refs):
    o_ref, lse_ref = refs[-2:]
    length = qk_ref.shape[0]
    first_head = lane_mask(block)
    for step in range(length // block):
        rows = slice(step * block, (step + 1) * block)
        keys = (step + 1) * block
        allowed = allowed_pairs(
            seg_col_ref[rows, :1], seg_row_ref[:, :keys], step * block, block, keys
        )
        q_pair = qk_ref[rows, :128]
        k_pair = qk_ref[:keys, 128:]
        v_pair = v_ref[:keys, :]
        outs, totals = [], []
        for head in range(2):
            mine = first_head if head == 0 else jnp.logical_not(first_head)
            q_head = jnp.where(mine, q_pair, jnp.zeros_like(q_pair))
            z = jnp.where(allowed, dot32(q_head, k_pair, NT), NEG)
            top = jnp.max(z, axis=-1, keepdims=True)
            e = jnp.exp(z - top)
            total = jnp.sum(e, axis=-1, keepdims=True)
            outs.append(dot32(e.astype(jnp.bfloat16), v_pair) * (1.0 / total))
            totals.append(top + jnp.log(total))
        o_ref[rows, :] = jnp.where(first_head, outs[0], outs[1]).astype(o_ref.dtype)
        lse_ref[rows, :] = jnp.where(first_head, totals[0], totals[1])


def attend_back_kernel(
    block, qk_ref, v_ref, do_ref, lse_ref, cos_ref, sin_ref, seg_col_ref, seg_row_ref, *refs
):
    dqk_ref, dv_ref, dk_sum, dv_sum = refs[-4:]
    length = qk_ref.shape[0]
    first_head = lane_mask(block)
    for step in range(length // block):
        rows = slice(step * block, (step + 1) * block)
        keys = (step + 1) * block
        allowed = allowed_pairs(
            seg_col_ref[rows, :1], seg_row_ref[:, :keys], step * block, block, keys
        )
        q_pair = qk_ref[rows, :128]
        k_pair = qk_ref[:keys, 128:]
        v_pair = v_ref[:keys, :]
        do_pair = do_ref[rows, :]
        dq_heads = []
        dk_step = dv_step = None
        for head in range(2):
            mine = first_head if head == 0 else jnp.logical_not(first_head)
            q_head = jnp.where(mine, q_pair, jnp.zeros_like(q_pair))
            do_head = jnp.where(mine, do_pair, jnp.zeros_like(do_pair))
            lse = lse_ref[rows, head * HEAD_DIM : head * HEAD_DIM + 1]
            z = jnp.where(allowed, dot32(q_head, k_pair, NT), NEG)
            p = jnp.exp(z - lse)
            dp = dot32(do_head, v_pair, NT)
            dv_head = dot32(p.astype(jnp.bfloat16), do_head, TN)
            row_dot = jnp.sum(p * dp, axis=-1, keepdims=True)
            ds = (p * (dp - row_dot)).astype(jnp.bfloat16)
            dq_heads.append(dot32(ds, k_pair))
            dk_head = dot32(ds, q_head, TN)
            dk_step = dk_head if dk_step is None else dk_step + dk_head
            dv_step = dv_head if dv_step is None else dv_step + dv_head
        dq = jnp.where(first_head, dq_heads[0], dq_heads[1]) * (HEAD_DIM**-0.5)
        dq = dq * cos_ref[rows, :] - swap_halves(dq) * sin_ref[rows, :]
        dqk_ref[rows, :128] = dq.astype(dqk_ref.dtype)
        last = slice(step * block, keys)
        if step > 0:
            dk_sum[: step * block, :] += dk_step[: step * block]
            dv_sum[: step * block, :] += dv_step[: step * block]
        dk_sum[last, :] = dk_step[step * block :]
        dv_sum[last, :] = dv_step[step * block :]
    dk = dk_sum[...]
    dk = dk * cos_ref[...] - swap_halves(dk) * sin_ref[...]
    dqk_ref[:, 128:] = dk.astype(dqk_ref.dtype)
    dv_ref[...] = dv_sum[...].astype(dv_ref.dtype)


def qkv_kernel(x_ref, gain_ref, qk_w_ref, v_w_ref, cos_ref, sin_ref, a_ref, qk_ref, v_ref):
    x = x_ref[...].astype(jnp.float32)
    r = lax.rsqrt(jnp.mean(x * x, axis=-1, keepdims=True) + EPS)
    a = (x * r * gain_ref[...]).astype(jnp.bfloat16)
    a_ref[...] = a
    u = dot32(a, qk_w_ref[...])
    cos, sin = cos_ref[...], sin_ref[...]
    for at in range(0, u.shape[1], 256):
        q = u[:, at : at + 128]
        q = (q * cos + swap_halves(q) * sin) * (HEAD_DIM**-0.5)
        qk_ref[:, at : at + 128] = q.astype(jnp.bfloat16)
        k = u[:, at + 128 : at + 256]
        k = k * cos + swap_halves(k) * sin
        qk_ref[:, at + 128 : at + 256] = k.astype(jnp.bfloat16)
    v_ref[...] = dot32(a, v_w_ref[...]).astype(jnp.bfloat16)


def whole(shape):
    return pl.BlockSpec(shape, lambda i: (0,) * len(shape))


def row_block(rows, width):
    return pl.BlockSpec((rows, width), lambda i: (i, 0))


def lane_block(length):
    return pl.BlockSpec((length, 128), lambda i: (0, i))


def project(x, gain, w_qk, w_v, cos, sin):
    length, model = x.shape
    width = w_v.shape[1]
    rows = 256
    low = lambda n: jax.ShapeDtypeStruct((length, n), jnp.bfloat16)
    return pl.pallas_call(
        qkv_kernel,
        grid=(length // rows,),
        in_specs=[
            row_block(rows, model), whole((1, model)), whole(w_qk.shape), whole(w_v.shape),
            row_block(rows, 128), row_block(rows, 128),
        ],
        out_specs=[row_block(rows, model), row_block(rows, 2 * width), row_block(rows, width)],
        out_shape=[low(model), low(2 * width), low(width)],
        compiler_params=pltpu.CompilerParams(vmem_limit_bytes=VMEM),
        cost_estimate=pl.CostEstimate(flops=1, bytes_accessed=1, transcendentals=0),
        name="project",
    )(x, gain, w_qk, w_v, cos, sin)


def over_pairs(kernel, name, some, arrays, shared, outs, scratch, into=()):
    length = arrays[0].shape[0]
    pairs = arrays[1].shape[1] // 128
    first, last = some
    of_pair = lambda width: pl.BlockSpec((length, width), lambda i: (0, first + i))
    inputs = tuple(arrays) + tuple(shared)
    return pl.pallas_call(
        functools.partial(kernel, 256),
        grid=(last - first,),
        in_specs=[of_pair(a.shape[1] // pairs) for a in arrays]
        + [whole(a.shape) for a in shared]
        + [pl.BlockSpec(memory_space=pl.ANY)] * len(into),
        out_specs=[of_pair(width) for width, _ in outs],
        out_shape=[jax.ShapeDtypeStruct((length, pairs * width), kind) for width, kind in outs],
        scratch_shapes=scratch,
        input_output_aliases={len(inputs) + i: i for i in range(len(into))},
        compiler_params=pltpu.CompilerParams(vmem_limit_bytes=VMEM),
        cost_estimate=pl.CostEstimate(flops=1, bytes_accessed=1, transcendentals=0),
        name=name,
    )(*inputs, *into)


def attend(some, qk, v, seg_col, seg_row, *into):
    return over_pairs(
        attend_kernel, "attend", some, (qk, v), (seg_col, seg_row),
        [(128, jnp.bfloat16), (128, jnp.float32)], [], into,
    )


def attend_back(some, arrays, into):
    length = arrays[0].shape[0]
    return over_pairs(
        attend_back_kernel, "attend_back", some, arrays[:4], arrays[4:],
        [(256, jnp.bfloat16), (128, jnp.bfloat16)],
        [pltpu.VMEM((length, 128), jnp.float32)] * 2, into,
    )


def cut_kernel(core_ref, wq, wk, wv, wo, wg, wu, wd, g1, g2, own, away, ff_own, ff_away, first, last):
    core = core_ref[0]
    rows, width = wq.shape
    half = width // 2
    eye = lax.broadcasted_iota(jnp.int32, (rows, rows), 0) == lax.broadcasted_iota(
        jnp.int32, (rows, rows), 1
    )

    def column(g):
        spread = jnp.where(eye, jnp.broadcast_to(g[...].astype(jnp.float32), (rows, rows)), 0.0)
        return jnp.sum(spread, axis=1, keepdims=True)

    lane = lax.broadcasted_iota(jnp.int32, (rows, 128), 1)
    gains = jnp.where(lane == 0, column(g1), jnp.where(lane == 1, column(g2), 0.0))
    for out, ff, side in ((own, ff_own, core), (away, ff_away, 1 - core)):
        for at in range(0, half, 128):
            for i, w in enumerate((wq, wk)):
                cols = pl.ds(pl.multiple_of(side * half + at, 128), 128)
                out[:, 2 * at + i * 128 : 2 * at + (i + 1) * 128] = w[:, cols]
        cols = pl.ds(pl.multiple_of(side * half, 128), half)
        out[:, width : width + half] = wv[:, cols]
        out[:, width + half : 2 * width] = wo[:, cols]
        out[:, 2 * width :] = gains.astype(jnp.bfloat16)
        n_blocks = ff.shape[1] // half
        for i in range(n_blocks):
            w = wg if i < n_blocks // 2 else wu
            block = 2 * (i % (n_blocks // 2)) + side
            ff[:, i * half : (i + 1) * half] = w[:, pl.ds(pl.multiple_of(block * half, 128), half)]
    first[...] = wd[:, : width // 2]
    last[...] = wd[:, width // 2 :]


def cut_shards(core, weights, gains):
    rows, width = weights[0].shape
    ff = weights[4].shape[1]
    down_rows = weights[6].shape[0]
    shape = lambda *dims: jax.ShapeDtypeStruct(dims, jnp.bfloat16)
    in_vmem = pl.BlockSpec(memory_space=pltpu.VMEM)
    return pl.pallas_call(
        cut_kernel,
        in_specs=[pl.BlockSpec(memory_space=pltpu.SMEM)] + [in_vmem] * 9,
        out_specs=[in_vmem] * 6,
        out_shape=[shape(rows, 2 * width + 128)] * 2
        + [shape(rows, ff)] * 2
        + [shape(down_rows, width // 2)] * 2,
        cost_estimate=pl.CostEstimate(flops=1, bytes_accessed=1, transcendentals=0),
        name="cut_shards",
    )(core.reshape(1).astype(jnp.int32), *weights, *(g[None, :] for g in gains))


STEP = 32


def turn_tables():
    lanes = np.arange(128) % (HEAD_DIM // 2)
    frequency = 10000.0 ** -(lanes * 2.0 / HEAD_DIM)
    tables = []
    for unit in (STEP, 1):
        angles = unit * np.arange(STEP)[:, None] * frequency[None, :]
        rest = np.concatenate([np.cos(angles), np.sin(angles)], axis=1)
        for _ in range(3):
            part = rest.astype(jnp.bfloat16)
            tables.append(part)
            rest = rest - part.astype(np.float64)
    return jnp.asarray(np.stack(tables))


def unpack_kernel(core_ref, own, other, tables, x, cos_ref, sin_ref, seg_col, seg_row):
    first = core_ref[0] == 0
    span = x.shape[0] // 2
    eye = lax.broadcasted_iota(jnp.int32, (span, span), 0) == lax.broadcasted_iota(
        jnp.int32, (span, span), 1
    )
    lanes = lax.broadcasted_iota(jnp.int32, (span, STEP), 1).astype(jnp.float32)
    half = HEAD_DIM // 2
    turned = lax.broadcasted_iota(jnp.int32, (span, 128), 1) % HEAD_DIM < half
    for h in range(2):
        rows = slice(h * span, (h + 1) * span)
        mine, theirs = (own, other) if h == 0 else (other, own)
        x[rows, :] = jnp.where(first, mine[0, :span, :], theirs[0, :span, :])
        numbers = [r[0, span : span + 16, : 3 * span].astype(jnp.float32)[:1] for r in (mine, theirs)]
        numbers = jnp.where(first, numbers[0], numbers[1])

        def column(i):
            row = numbers[:, i * span : (i + 1) * span]
            spread = jnp.where(eye, jnp.broadcast_to(row, (span, span)), 0.0)
            return jnp.sum(spread, axis=1, keepdims=True)

        def table(i):
            chosen = jnp.where(column(i) == lanes, 1.0, 0.0).astype(jnp.bfloat16)
            t = sum(dot32(chosen, tables[3 * i + j]) for j in range(3))
            return t[:, :128], t[:, 128:]

        (cos_a, sin_a), (cos_b, sin_b) = table(0), table(1)
        cos_ref[rows, :] = cos_a * cos_b - sin_a * sin_b
        sine = sin_a * cos_b + cos_a * sin_b
        sin_ref[rows, :] = jnp.where(turned, -sine, sine)
        seg_col[rows, :] = jnp.broadcast_to(column(2), (span, 128)).astype(jnp.int32)
        seg_row[:, rows] = numbers[:, 2 * span : 3 * span].astype(jnp.int32)


def unpack_blocks(core, own, other):
    blocks, packed_rows, model = own.shape
    span = 128
    length = blocks * 2 * span
    tables = turn_tables()
    shape = lambda width, kind: jax.ShapeDtypeStruct((length, width), kind)
    of_block = pl.BlockSpec((1, packed_rows, model), lambda i, s: (i, 0, 0))
    rows = lambda width: pl.BlockSpec((2 * span, width), lambda i, s: (i, 0))
    return pl.pallas_call(
        unpack_kernel,
        grid_spec=pltpu.PrefetchScalarGridSpec(
            num_scalar_prefetch=1,
            grid=(blocks,),
            in_specs=[of_block, of_block, pl.BlockSpec(tables.shape, lambda i, s: (0, 0, 0))],
            out_specs=[rows(model), rows(128), rows(128), rows(128)]
            + [pl.BlockSpec((1, 2 * span), lambda i, s: (0, i))],
        ),
        out_shape=[
            shape(model, jnp.bfloat16), shape(128, jnp.float32), shape(128, jnp.float32),
            shape(128, jnp.int32), jax.ShapeDtypeStruct((1, length), jnp.int32),
        ],
        cost_estimate=pl.CostEstimate(flops=1, bytes_accessed=1, transcendentals=0),
        name="unpack",
    )(core.reshape(1).astype(jnp.int32), own, other, tables)


def rounded_sum(*parts):
    total = parts[0]
    for part in parts[1:]:
        total = total + part
    return total


def ff_grads_kernel(bits, c, d_gate, d_up, hid, dy, x_out, x_keep, y_out, y_keep, ff, down):
    rows, cols = x_out.shape[-2:]
    n_wide = d_gate.shape[1] // cols
    n_down = x_out.shape[1] - 2 * n_wide
    away = pl.program_id(0) != bits[1]

    def cut_side(out, lead, side, first):
        for block in range(2):
            here = pl.ds(pl.multiple_of((side * 2 + block) * rows, rows), rows)
            for k in range(n_wide):
                slab = ff[here, k * cols : (k + 1) * cols]
                out[lead, block * n_wide + k] = slab.astype(jnp.bfloat16)
        for j in range(n_down):
            here = pl.ds(pl.multiple_of((side * n_down + j) * rows, rows), rows)
            out[lead, 2 * n_wide + j] = down[here, first : first + cols].astype(jnp.bfloat16)

    down[...] = dot32(hid[...], dy[...], TN)
    ff[...] = dot32(c[...], d_gate[...], TN)
    cut_side(x_out, 0, 1 - bits[0], 0)
    cut_side(x_keep, 0, bits[0], 0)
    ff[...] = dot32(c[...], d_up[...], TN)

    def by_y(out):
        for x in range(2):
            cut_side(out, x, x, cols)

    pl.when(away)(lambda: by_y(y_out))
    pl.when(jnp.logical_not(away))(lambda: by_y(y_keep))


def ff_grads(bits, c, d_gate, d_up, hid, dy, slabs):
    length, model = c.shape
    ff = d_gate.shape[1]
    half = lambda width: pl.BlockSpec((length, width // 2), lambda y, bits: (0, y))
    full = lambda a: pl.BlockSpec(a.shape, lambda y, bits: (0, 0), pipeline_mode=pl.Buffered(1))
    one = pl.BlockSpec((1,) + slabs, lambda y, bits: (y, 0, 0, 0))
    both = pl.BlockSpec((2,) + slabs, lambda y, bits: (0,) * 4)
    return pl.pallas_call(
        ff_grads_kernel,
        grid_spec=pltpu.PrefetchScalarGridSpec(
            num_scalar_prefetch=1,
            grid=(2,),
            in_specs=[half(model), full(d_gate), full(d_up), half(ff), full(dy)],
            out_specs=[one, one, both, both],
            scratch_shapes=[
                pltpu.VMEM((model // 2, ff), jnp.float32), pltpu.VMEM((ff // 2, model), jnp.float32)
            ],
        ),
        out_shape=[jax.ShapeDtypeStruct((2,) + slabs, jnp.bfloat16)] * 4,
        compiler_params=pltpu.CompilerParams(vmem_limit_bytes=VMEM),
        cost_estimate=pl.CostEstimate(flops=1, bytes_accessed=1, transcendentals=0),
        name="ff_grads",
    )(bits, c, d_gate, d_up, hid, dy)


def attn_grads_kernel(
    bits, a, dqk, dv, ob, db, gains, qk_out, qk_keep, vo_out, vo_keep, qk
):
    side = qk.shape[0] // 2
    width = dv.shape[1]
    qk[...] = dot32(a[...], dqk[...], TN)
    for out, x in ((qk_out, 1 - bits[0]), (qk_keep, bits[0])):
        here = pl.ds(pl.multiple_of(x * side, side), side)
        out[0] = qk[here, :].astype(jnp.bfloat16)

    def by_y(out):
        out[:, :width] = dot32(a[...], dv[...], TN).astype(jnp.bfloat16)
        out[:, width : 2 * width] = dot32(ob[...], db[...], TN).astype(jnp.bfloat16)
        out[:, 2 * width :] = gains[...].astype(jnp.bfloat16)

    away = pl.program_id(0) != bits[1]
    pl.when(away)(lambda: by_y(vo_out))
    pl.when(jnp.logical_not(away))(lambda: by_y(vo_keep))


def attn_grads(bits, a, dqk, dv, ob, db, gains):
    length, model = a.shape
    width = dv.shape[1]
    half = lambda: pl.BlockSpec((length, model // 2), lambda y, bits: (0, y))
    full = lambda t: pl.BlockSpec(t.shape, lambda y, bits: (0, 0))
    qk_rows = pl.BlockSpec((1, model // 4, 2 * width), lambda y, bits: (y, 0, 0))
    vo_rows = pl.BlockSpec((model // 2, 2 * width + 128), lambda y, bits: (0, 0))
    return pl.pallas_call(
        attn_grads_kernel,
        grid_spec=pltpu.PrefetchScalarGridSpec(
            num_scalar_prefetch=1,
            grid=(2,),
            in_specs=[
                half(), full(dqk), full(dv), half(),
                pl.BlockSpec((length, width), lambda y, bits: (0, bits[3])),
                pl.BlockSpec((model // 2, 128), lambda y, bits: (y, 0)),
            ],
            out_specs=[qk_rows, qk_rows, vo_rows, vo_rows],
            scratch_shapes=[pltpu.VMEM((model // 2, 2 * width), jnp.float32)],
        ),
        out_shape=[jax.ShapeDtypeStruct((2, model // 4, 2 * width), jnp.bfloat16)] * 2
        + [jax.ShapeDtypeStruct((model // 2, 2 * width + 128), jnp.bfloat16)] * 2,
        compiler_params=pltpu.CompilerParams(vmem_limit_bytes=VMEM),
        cost_estimate=pl.CostEstimate(flops=1, bytes_accessed=1, transcendentals=0),
        name="attn_grads",
    )(bits, a, dqk, dv, ob, db, gains)


def ff_second_kernel(bits, x_keep, x_came, y_keep, y_came, x_out, y_out):
    for p in range(x_out.shape[0]):
        x_out[p] = rounded_sum(x_keep[0, p], x_came[0, p])
        y_out[p] = rounded_sum(y_keep[0, p], y_came[0, p])


def ff_line_kernel(bits, x_keep, x_came, x_last, y_keep, y_came, y_last, kept, sent, slab):
    n_slabs, rows = x_last.shape[:2]
    shard = kept.shape[2]
    n_down = rows // shard
    n_ff = n_slabs - n_down
    for at, keep, came, last in ((0, x_keep, x_came, x_last), (n_slabs, y_keep, y_came, y_last)):
        for p in range(n_slabs):
            slab[...] = rounded_sum(keep[0, p], came[0, p], last[p]).astype(jnp.float32)
            for i in range(n_down):
                piece = slab[i * shard : (i + 1) * shard, :].astype(jnp.bfloat16)
                if p < n_ff:
                    z1, z0, to = i // 2, i % 2, at + p
                else:
                    z1, z0, to = (p - n_ff) // 2, (p - n_ff) % 2, at + n_ff + i

                def put(out, z1=z1, to=to, piece=piece):
                    out[z1, to] = piece

                pl.when(bits[2] == z0)(functools.partial(put, kept))
                pl.when(bits[2] != z0)(functools.partial(put, sent))


def ff_call(kernel, name, bits, inputs, outs, scratch=()):
    def spec(array, at):
        block = tuple(1 if i in at else n for i, n in enumerate(array.shape))
        return pl.BlockSpec(
            block,
            lambda i, bits: tuple(at[d](bits) if d in at else 0 for d in range(array.ndim)),
        )

    return pl.pallas_call(
        kernel,
        grid_spec=pltpu.PrefetchScalarGridSpec(
            num_scalar_prefetch=1,
            grid=(1,),
            in_specs=[spec(*pair) for pair in inputs],
            out_specs=[pl.BlockSpec(o, lambda i, bits, n=len(o): (0,) * n) for o in outs],
            scratch_shapes=scratch,
        ),
        out_shape=[jax.ShapeDtypeStruct(o, jnp.bfloat16) for o in outs],
        compiler_params=pltpu.CompilerParams(vmem_limit_bytes=VMEM),
        cost_estimate=pl.CostEstimate(flops=1, bytes_accessed=1, transcendentals=0),
        name=name,
    )(bits, *[array for array, _ in inputs])


def by_bit(own, other, bit, axis):
    own, other = jnp.expand_dims(own, axis), jnp.expand_dims(other, axis)
    shape = [1] * own.ndim
    shape[axis] = 2
    return jnp.where(lax.broadcasted_iota(jnp.int32, shape, axis) == bit, own, other)


def pick(v, at, axis):
    return lax.dynamic_index_in_dim(v, at, axis, keepdims=False)


def pick_static(v, at, axis):
    return lax.index_in_dim(v, at, axis, keepdims=False)


class Cube:
    def __init__(self, seq_size, ctx_size):
        self.sizes = {"seq": seq_size, "ctx": ctx_size}
        self.steps = {"core": ("seq", 1), "x": ("seq", 2), "y": ("seq", 4), "z0": ("ctx", 1), "z1": ("ctx", 2)}
        self.bits = {
            name: (lax.axis_index(axis) // step) % 2 for name, (axis, step) in self.steps.items()
        }
        self.last = ()

    def step(self, work, *arrays):
        if self.last:
            arrays = lax.optimization_barrier((arrays, self.last))[0]
        result = work(*arrays)
        self.last = tuple(jax.tree.leaves(result))
        return result

    def settle(self):
        names = tuple(self.bits)
        values = self.hold(*self.bits.values())
        self.bits = dict(zip(names, values))

    def hold(self, *arrays):
        return lax.optimization_barrier((arrays, self.last))[0]

    def swap(self, v, name):
        axis, step = self.steps[name]
        return lax.ppermute(v, axis, [(i, i ^ step) for i in range(self.sizes[axis])])

    def mine(self, v, name, axis):
        return pick(v, self.bits[name], axis)

    def away(self, v, name, axis):
        return pick(v, 1 - self.bits[name], axis)

    def joined(self, own, other, name, axis):
        return lax.optimization_barrier(by_bit(own, other, self.bits[name], axis))

    def traded(self, v, came, steps):
        for other, (name, axis, at) in zip(came, steps):
            v = by_bit(self.mine(v, name, axis), other, self.bits[name], at)
        return v

    def summed(self, v, came, steps):
        for other, (name, axis) in zip(came, steps):
            v = low(wide(self.mine(v, name, axis)) + wide(other))
        return v

def low(v):
    return v.astype(jnp.bfloat16)


def wide(v):
    return v.astype(jnp.float32)


def rows_of(v):
    return v.reshape(-1, v.shape[-1])


def r_of(u):
    return lax.rsqrt(jnp.mean(u * u, axis=-1, keepdims=True) + EPS)


def norm_back(u, gain, dn):
    r = r_of(u)
    gd = gain * dn
    return r * gd - u * (r * r * r) * jnp.mean(gd * u, axis=-1, keepdims=True)


def sequence_per_chip(seq_size, ctx_size):
    def on_device(
        tokens, segments, positions,
        w_query, w_key, w_value, w_out, w_gate, w_up, w_down,
        gain_attn, gain_mlp, cotangent,
    ):
        cube = Cube(seq_size, ctx_size)
        step, swap, hold, mine, away = cube.step, cube.swap, cube.hold, cube.mine, cube.away
        joined, traded, summed = cube.joined, cube.traded, cube.summed
        bits = cube.bits
        core = cube.bits["core"]
        seqs, local_len, model = tokens.shape
        seq_len = segments.shape[1]
        span = local_len // 2
        own_rows = w_query.shape[0]
        half_width = w_query.shape[1] // 2
        ff_rows = w_down.shape[0]
        ff_half = w_gate.shape[1] // 2
        n_blocks = seq_size // 2
        ff_block = ff_half // n_blocks
        model_half = model // 2
        pairs = half_width // 128

        attn_own, attn_away, ff_own, ff_away, first, last = step(
            lambda *w: tuple(cut_shards(core, w[:7], w[7:])),
            w_query, w_key, w_value, w_out, w_gate, w_up, w_down, gain_attn, gain_mlp,
        )
        attn_came = swap(attn_away, "core")

        def pack_tokens(tokens, positions, segments):
            own_first = lax.axis_index("ctx") * local_len
            own_segments = lax.dynamic_slice_in_dim(segments, own_first, local_len, axis=1)
            numbers = low(jnp.stack([positions // STEP, positions % STEP, own_segments]))
            numbers = numbers.reshape(3, seqs, 2, span).transpose(1, 2, 0, 3)
            numbers = numbers.reshape(seqs, 2, 1, 3 * span)
            numbers = jnp.pad(numbers, ((0, 0), (0, 0), (0, 15), (0, model - 3 * span)))
            pack = jnp.concatenate([tokens.reshape(seqs, 2, span, model), numbers], axis=2)
            return pack, away(pack, "core", 1)

        to_chip = (("core", 1, 0), ("z0", 1, 1), ("z1", 0, 0))

        def sent_next(steps, n):
            name, axis = steps[n][:2]
            return lambda v, *came: away(traded(v, came, steps), name, axis)

        x_pack, sent = step(pack_tokens, tokens, positions, segments)
        x_came = [swap(sent, "core")]

        attn_piece = step(lambda v, w: joined(v, w, "core", 0), attn_own, attn_came)
        attn_came = swap(attn_piece, "z1")

        x_came.append(swap(step(sent_next(to_chip, 1), x_pack, *x_came), "z0"))

        cube.settle()
        bits = cube.bits

        ff_came = swap(*hold(ff_away), "core")
        ff_piece = step(lambda v, w: joined(v, w, "core", 0), ff_own, ff_came)

        attn_half_line = step(lambda v, w: joined(v, w, "z1", 1), attn_piece, attn_came)
        attn_came = swap(attn_half_line, "z0")

        first_came, last_came = swap(*hold(first), "x"), swap(*hold(last), "y")

        ff_came = swap(*hold(ff_piece), "z1")

        x_came.append(swap(step(sent_next(to_chip, 2), x_pack, *x_came), "z1"))

        down_pair = step(
            lambda a, b, c, d: jnp.concatenate(
                [joined(a, b, "x", 0), joined(c, d, "y", 0)], axis=2
            ),
            first, first_came, last, last_came,
        )

        def attn_to_line(v, came):
            line = joined(v, came, "z0", 2)
            return line[..., : 2 * half_width], line[..., 2 * half_width :]

        qk_line, vo_line = step(attn_to_line, attn_half_line, attn_came)
        qk_came, vo_came = swap(qk_line, "x"), swap(vo_line, "y")

        dy_pack = cotangent.reshape(seqs, 2, span, model)
        dy_came = [swap(step(sent_next(to_chip, 0), dy_pack), "core")]

        ff_half_line = step(lambda v, w: joined(v, w, "z1", 1), ff_piece, ff_came)
        ff_came = swap(ff_half_line, "z0")

        qk_plane = step(lambda v, w: joined(v, w, "x", 0), qk_line, qk_came)
        qk_came = swap(qk_plane, "y")
        vo_plane = step(lambda v, w: joined(v, w, "y", 0), vo_line, vo_came)
        vo_came = swap(vo_plane, "x")

        x_half = step(
            lambda v, *came: traded(v, came, to_chip).reshape(ctx_size, -1, model), x_pack, *x_came
        )
        x_other = swap(x_half, "core")

        down_came = swap(*hold(down_pair), "z1")

        def attn_to_full(qk, qk_came, vo, vo_came):
            qk = rows_of(joined(qk, qk_came, "y", 0))
            vo = rows_of(joined(vo, vo_came, "x", 1))
            gains = wide(vo[:, 2 * half_width : 2 * half_width + 2])
            return (
                qk, vo[:, :half_width], vo[:, half_width : 2 * half_width],
                gains[:, 0][None, :], gains[:, 1],
            )

        qk_full, v_full, out_half, gain_one, gain_two = step(
            attn_to_full, qk_plane, qk_came, vo_plane, vo_came
        )
        out_came = swap(out_half, "core")

        def ff_to_line(v, came):
            line = joined(v, came, "z0", 2)
            return line[..., :ff_half], line[..., ff_half:]

        gate_line, up_line = step(ff_to_line, ff_half_line, ff_came)

        gate_came, up_came = swap(gate_line, "x"), swap(up_line, "y")

        dy_came.append(swap(step(sent_next(to_chip, 1), dy_pack, *dy_came), "z0"))

        def unpack_tokens(x_half, x_other):
            x, cos, sin, seg_col, seg_row = unpack_blocks(core, x_half, x_other)
            return x, x_half[:, :span], seg_col, seg_row, cos, sin

        x, x_half, seg_col, seg_row, cos, sin = step(unpack_tokens, x_half, x_other)

        down_half_line = step(lambda v, w: joined(v, w, "z1", 1), down_pair, down_came)
        down_came = swap(down_half_line, "z0")

        def halves(own, other):
            whole = jnp.zeros((own.shape[0], 2 * own.shape[1]), own.dtype)
            whole = lax.dynamic_update_slice(whole, own, (0, core * own.shape[1]))
            return lax.dynamic_update_slice(whole, other, (0, (1 - core) * own.shape[1]))

        normed, qk, v = step(lambda *t: tuple(project(*t)), x, gain_one, qk_full, v_full, cos, sin)
        segs = (seg_col, seg_row)

        gate_plane = step(lambda v, w: joined(v, w, "x", 0), gate_line, gate_came)
        gate_came = swap(gate_plane, "y")
        up_plane = step(lambda v, w: joined(v, w, "y", 0), up_line, up_came)
        up_came = swap(up_plane, "x")

        dy_came.append(swap(step(sent_next(to_chip, 2), dy_pack, *dy_came), "z1"))


        ob_half, lse = step(lambda *t: tuple(attend((0, pairs), *t)), qk, v, *segs)
        ob_came = swap(ob_half, "core")

        def lay(into, own, bit, axis):
            return lax.dynamic_update_index_in_dim(into, own, bit, axis)

        def lay_own(gate, up):
            ff = jnp.zeros((2,) + gate.shape, gate.dtype)
            return lay(ff, gate, bits["y"], 0), lay(ff, up, bits["x"], 1)

        gate_part, up_part = step(lay_own, gate_plane, up_plane)

        out_full = step(halves, out_half, out_came)

        def down_to_line(v, came):
            line = joined(v, came, "z0", 2)
            return line[..., :model_half], line[..., model_half:]

        first_line, last_line = step(down_to_line, down_half_line, down_came)
        first_came, last_came = swap(first_line, "y"), swap(last_line, "x")

        gate_full, up_full = step(
            lambda a, b, c, d: (
                rows_of(lay(a, b, 1 - bits["y"], 0)), rows_of(lay(c, d, 1 - bits["x"], 1))
            ),
            gate_part, gate_came, up_part, up_came,
        )

        dy_half = step(
            lambda v, *came: traded(v, came, to_chip).reshape(ctx_size, span, model),
            dy_pack, *dy_came,
        )
        dy_other = swap(dy_half, "core")

        ob = step(halves, ob_half, ob_came)

        def own_half(t):
            return mine(t.reshape(ctx_size, 2, span, t.shape[-1]), "core", 1)

        def hidden(x, ob, out_full, gain_two):
            h1 = wide(x) + dot32(ob, out_full)
            return h1, low(h1 * r_of(h1) * gain_two)

        h1, normed_two = step(hidden, x, ob, out_full, gain_two)

        gate = step(dot32, normed_two, gate_full)

        dy = step(
            lambda a, b: joined(a, b, "core", 1).reshape(seq_len, model), dy_half, dy_other
        )

        def up_and_hidden(normed_two, up_full, gate):
            up = dot32(normed_two, up_full)
            s = jax.nn.sigmoid(gate)
            silu = gate * s
            return low(silu), low(up * s * (1.0 + gate * (1.0 - s))), low(silu * up)

        up_factor, gate_factor, hid = step(up_and_hidden, normed_two, up_full, gate)

        down_full = step(
            lambda a, b, c, d: rows_of(
                jnp.concatenate([joined(a, b, "y", 0), joined(c, d, "x", 1)], axis=-1)
            ),
            first_line, first_came, last_line, last_came,
        )

        def back(dy, down_full, gate_factor, up_factor):
            d_hid = dot32(dy, down_full, NT)
            return low(d_hid * wide(gate_factor)), low(d_hid * wide(up_factor))

        by_x = (("x", 1), ("y", 0), ("z0", 2), ("z1", 1), ("core", 0))
        by_y = (("y", 0), ("x", 0), ("z0", 2), ("z1", 1), ("core", 0))

        def to_send(steps, n):
            name, axis = steps[n]
            return lambda v, *came: away(summed(v, came, steps), name, axis)

        d_gate, d_up = step(back, dy, down_full, gate_factor, up_factor)
        n_wide = ff_half // ff_block
        n_down = ff_rows // own_rows
        n_pieces = 2 * n_wide + n_down
        slabs = (n_pieces, ctx_size * own_rows, ff_block)
        bit_array = jnp.stack([bits["x"], bits["y"], bits["z0"], core]).astype(jnp.int32)
        x_mine, x_away = (lambda b: b[0]), (lambda b: 1 - b[0])
        y_mine, y_away = (lambda b: b[1]), (lambda b: 1 - b[1])
        sent_x, x_keep, sent_y, y_keep = step(
            lambda *t: tuple(ff_grads(bit_array, *t, slabs)), normed_two, d_gate, d_up, hid, dy
        )
        x_came, y_came = [swap(sent_x, "x")], [swap(sent_y, "y")]

        def dc_of(d_gate, gate_full, d_up, up_full):
            dc = dot32(d_gate, gate_full, NT) + dot32(d_up, up_full, NT)
            return dc, away(dc.reshape(ctx_size, 2, span, model), "core", 1)

        dc, sent = step(dc_of, d_gate, gate_full, d_up, up_full)
        dc_came = swap(sent, "core")

        def down_of(hid, down_full):
            down = dot32(hid, down_full).reshape(ctx_size, 2, span, model)
            return down, away(down, "core", 1)

        down, sent = step(down_of, hid, down_full)
        down_came = swap(sent, "core")

        def attn_side(dc, came, h1, dy_half, gain_two):
            dc_half = own_half(dc) + came
            dh1 = wide(dy_half) + norm_back(own_half(h1), gain_two, dc_half)
            return dh1, low(dh1), jnp.sum(dc * h1 * r_of(h1), axis=0)

        dh1_half, db_half, gain_two_grad = step(attn_side, dc, dc_came, h1, dy_half, gain_two)
        db_came = swap(db_half, "core")
        home_steps = (("z0", 1, 1), ("z1", 0, 0), ("core", 0, 1))

        def out_of(h1, down, came):
            out = low(own_half(h1) + mine(down, "core", 1) + came).reshape(2, 2, span, model)
            return out, away(out, "z0", 1)

        home, sent = step(out_of, h1, down, down_came)
        home_came = [swap(sent, "z0")]

        def d_attended_of(db_half, db_came, out_full):
            db = joined(db_half, db_came, "core", 1).reshape(seq_len, model)
            out_rows = lax.dynamic_slice_in_dim(out_full, core * half_width, half_width, axis=0)
            return db, low(dot32(db, out_rows, NT))

        db, d_attended = step(d_attended_of, db_half, db_came, out_full)

        backs = (qk, v, d_attended, lse, cos, sin, *segs)
        heads = step(lambda *t: tuple(attend_back((0, pairs - 1), t[:8], t[8:])), *backs)

        home_came.append(swap(step(sent_next(home_steps, 1), home, *home_came), "z1"))

        dqk, dv = step(
            lambda *t: tuple(attend_back((pairs - 1, pairs), t[:8], t[8:])), *backs, *heads
        )

        def plus(v, came):
            return low(wide(v) + wide(came))

        def ff_second(x_keep, x_came, y_keep, y_came):
            return tuple(
                ff_call(
                    ff_second_kernel, "ff_second", bit_array,
                    [(x_keep, {0: y_away}), (x_came, {0: y_away}),
                     (y_keep, {0: x_away}), (y_came, {0: x_away})],
                    [slabs] * 2,
                )
            )

        sent_x, sent_y = step(ff_second, x_keep, *x_came, y_keep, *y_came)
        x_came.append(swap(sent_x, "y"))
        y_came.append(swap(sent_y, "x"))

        home_came.append(swap(step(sent_next(home_steps, 2), home, *home_came), "core"))

        def da_of(qk_full, v_full, dqk, dv, x):
            da = dot32(dqk, qk_full, NT) + dot32(dv, v_full, NT)
            x = wide(x)
            gain = jnp.sum(da * x * r_of(x), axis=0)
            return da, away(da.reshape(ctx_size, 2, span, model), "core", 1), gain

        da, sent, gain_one_grad = step(da_of, qk_full, v_full, dqk, dv, x)
        da_came = swap(sent, "core")

        output = step(
            lambda v, *came: traded(v, came, home_steps).reshape(seqs, local_len, model),
            home, *home_came,
        )

        def input_side(x_half, da, came, gain_one, dh1_half):
            da_half = own_half(da) + came
            du1 = norm_back(wide(x_half), gain_one, da_half)
            du = low(dh1_half + du1).reshape(2, 2, span, model)
            return du, away(du, "z0", 1)

        inward, sent = step(input_side, x_half, da, da_came, gain_one, dh1_half)
        inward_came = [swap(sent, "z0")]

        def attn_grads_of(normed, dqk, dv, ob, db, gain_one, gain_two):
            gains = jnp.pad(jnp.stack([gain_one, gain_two], axis=1), ((0, 0), (0, 126)))
            out = attn_grads(bit_array, normed, dqk, dv, ob, db, gains)
            by_block = lambda v: v.reshape(2, 2, 2, 2, own_rows, v.shape[-1])
            return tuple(by_block(v) for v in out)

        sent_qk, qk_keep, sent_vo, vo_keep = step(
            attn_grads_of, normed, dqk, dv, ob, db, gain_one_grad, gain_two_grad
        )
        qk_came, vo_came = [swap(sent_qk, "x")], [swap(sent_vo, "y")]

        def line_to_send(qk, qk_first, qk_second, vo, vo_first, vo_second):
            qk = summed(plus(qk, qk_first), (qk_second,), by_x[1:])
            vo = summed(plus(vo, vo_first), (vo_second,), by_y[1:])
            line = jnp.concatenate([qk, vo], axis=-1)
            return line, away(line, "z0", 2)

        def ff_line(x_keep, x_came, x_last, y_keep, y_came, y_last):
            return tuple(
                ff_call(
                    ff_line_kernel, "ff_line", bit_array,
                    [(x_keep, {0: y_mine}), (x_came, {0: y_mine}), (x_last, {}),
                     (y_keep, {0: x_mine}), (y_came, {0: x_mine}), (y_last, {})],
                    [(2, 2 * n_pieces, own_rows, ff_block)] * 2,
                    [pltpu.VMEM(slabs[1:], jnp.float32)],
                )
            )

        g_ff, sent = step(ff_line, x_keep, *x_came, y_keep, *y_came)
        ff_came = [swap(sent, "z0")]

        def second_attn(qk, qk_came, vo, vo_came):
            return away(plus(qk, qk_came), "y", 0), away(plus(vo, vo_came), "x", 0)

        sent_qk, sent_vo = step(second_attn, qk_keep, *qk_came, vo_keep, *vo_came)
        qk_came.append(swap(sent_qk, "y"))
        vo_came.append(swap(sent_vo, "x"))

        inward_came.append(swap(step(sent_next(home_steps, 1), inward, *inward_came), "z1"))

        def ff_to_z1(v, came):
            return low(wide(away(v, "z1", 0)) + wide(away(came, "z1", 0)))

        ff_came.append(swap(step(ff_to_z1, g_ff, *ff_came), "z1"))

        g_attn, sent = step(line_to_send, qk_keep, *qk_came, vo_keep, *vo_came)
        attn_came = [swap(sent, "z0")]

        inward_came.append(swap(step(sent_next(home_steps, 2), inward, *inward_came), "core"))

        attn_came.append(swap(step(to_send(by_x[2:], 1), g_attn, *attn_came), "z1"))

        input_grad = step(
            lambda v, *came: wide(traded(v, came, home_steps)).reshape(seqs, local_len, model),
            inward, *inward_came,
        )

        def own_rows_of(v, z0_came, z1_came):
            v = summed(v, (z0_came,), by_x[2:])
            v = wide(mine(v, "z1", 1)) + wide(z1_came)
            return v, away(v, "core", 0)

        def ff_rows_of(v, z0_came, z1_came):
            v = low(wide(mine(v, "z1", 0)) + wide(mine(z0_came, "z1", 0)))
            v = (wide(v) + wide(z1_came)).reshape(2, -1, own_rows, ff_block)
            ff = v[:, : 2 * n_wide].reshape(2, 2, n_wide, own_rows, ff_block)
            down = v[:, 2 * n_wide :].reshape(2, ff_rows, ff_block)
            return ff, away(ff, "core", 1), jnp.concatenate([down[0], down[1]], axis=1)

        g_ff, sent, grad_down = step(ff_rows_of, g_ff, *ff_came)
        ff_came = swap(sent, "core")

        def columns(own, other, first, size):
            own, other = own[:, first : first + size], other[:, first : first + size]
            return [jnp.where(core == 0, own, other), jnp.where(core == 0, other, own)]

        def ff_rows_home(ff, other):
            own = mine(ff, "core", 1)

            def whole_rows(i):
                parts = []
                for block in range(n_blocks):
                    parts += columns(own[i, block], other[i, block], 0, ff_block)
                return jnp.concatenate(parts, axis=1)

            return whole_rows(0), whole_rows(1)

        grad_gate, grad_up = step(ff_rows_home, g_ff, ff_came)

        g_attn, sent = step(own_rows_of, g_attn, *attn_came)
        attn_came = swap(sent, "core")
        def attn_rows_home(own, other):
            def whole_rows(starts, size):
                first, last = zip(*(columns(own, other, at, size) for at in starts))
                return jnp.concatenate(first + last, axis=1)

            query = whole_rows(range(0, 256 * pairs, 256), 128)
            key = whole_rows(range(128, 256 * pairs, 256), 128)
            at = 2 * half_width
            value = whole_rows([at], half_width)
            out = whole_rows([at + half_width], half_width)
            at += 2 * half_width
            gains = (own + other)[:, at : at + 2]
            return query, key, value, out, gains[:, 0], gains[:, 1]

        home_rows = step(lambda v, w: attn_rows_home(mine(v, "core", 0), w), g_attn, attn_came)
        return (output, input_grad) + home_rows[:4] + (grad_gate, grad_up, grad_down) + home_rows[4:]

    return on_device


def solution(mesh):
    in_specs = (
        P("seq", "ctx", None),
        P("seq", None),
        P("seq", "ctx"),
        P(("seq", "ctx"), None),
        P(("seq", "ctx"), None),
        P(("seq", "ctx"), None),
        P(("seq", "ctx"), None),
        P(("seq", "ctx"), None),
        P(("seq", "ctx"), None),
        P(("seq", "ctx"), None),
        P(("seq", "ctx")),
        P(("seq", "ctx")),
        P("seq", "ctx", None),
    )
    out_specs = (
        P("seq", "ctx", None),
        P("seq", "ctx", None),
        P(("seq", "ctx"), None),
        P(("seq", "ctx"), None),
        P(("seq", "ctx"), None),
        P(("seq", "ctx"), None),
        P(("seq", "ctx"), None),
        P(("seq", "ctx"), None),
        P(("seq", "ctx"), None),
        P(("seq", "ctx")),
        P(("seq", "ctx")),
    )
    seq_size, ctx_size = mesh.shape["seq"], mesh.shape["ctx"]
    one_each = sequence_per_chip(seq_size, ctx_size)

    def program(tokens, *others):
        if (seq_size, ctx_size, tokens.shape[0]) == (8, 4, 2):
            return one_each(tokens, *others)
        return on_device(tokens, *others)

    return jax.shard_map(
        program, mesh=mesh, in_specs=in_specs, out_specs=out_specs, check_vma=False
    )
```
